128 devices in a mesh: rep: 4 (over y_lo, core), fsdp: 32 (over y_hi, x, z).
Axes of the slice: x: 4, y: 4 (y_hi: 2, y_lo: 2; y = y_hi * 2 + y_lo), z: 4, core: 2. Of those that a mesh axis runs over, the one named last changes fastest.
Arguments:
- tokens: bfloat16 [2, 128, 128, 1024], P(None, ('rep', 'fsdp')), may hold values from -6 to 6
- segments: int32 [2, 128, 128], P(None, ('rep', 'fsdp')), may hold values from 0 to 31, never falling along the last dimension, each value on 1 to 64 neighbouring positions
- routes: int32 [2, 128, 128, 8], P(None, ('rep', 'fsdp')), may hold values from 0 to 31, all different within a row; in each aligned block of 128 rows (0 to 127, 128 to 255, ..., all dimensions but the last counted through in order) at most 48 rows name the same one
- cotangent: bfloat16 [2, 128, 128, 1024], P(None, ('rep', 'fsdp')), may hold values from -6 to 6
- attn_gain: bfloat16 [1024], P('fsdp'), may hold values from 0.5 to 1.5
- moe_gain: bfloat16 [1024], P('fsdp'), may hold values from 0.5 to 1.5
- w_query: bfloat16 [1024, 1024], P('fsdp'), may hold values from -0.75 to 0.75
- w_key: bfloat16 [1024, 512], P('fsdp'), may hold values from -0.75 to 0.75
- w_value: bfloat16 [1024, 512], P('fsdp'), may hold values from -0.1875 to 0.1875
- w_output: bfloat16 [1024, 1024], P('fsdp'), may hold values from -1.5 to 1.5
- w_router: bfloat16 [1024, 32], P('fsdp'), may hold values from -0.09375 to 0.09375
- w_gate: bfloat16 [32, 1024, 512], P('fsdp'), may hold values from -0.1875 to 0.1875
- w_up: bfloat16 [32, 1024, 512], P('fsdp'), may hold values from -0.1875 to 0.1875
- w_down: bfloat16 [32, 512, 1024], P('fsdp'), may hold values from -6 to 6
Outputs:
- output: bfloat16 [2, 128, 128, 1024], P(None, ('rep', 'fsdp'))
- grad_tokens: float32 [2, 128, 128, 1024], P(None, ('rep', 'fsdp'))
- grad_attn_gain: float32 [1024], P('fsdp')
- grad_moe_gain: float32 [1024], P('fsdp')
- grad_query: float32 [1024, 1024], P('fsdp')
- grad_key: float32 [1024, 512], P('fsdp')
- grad_value: float32 [1024, 512], P('fsdp')
- grad_w_output: float32 [1024, 1024], P('fsdp')
- grad_router: float32 [1024, 32], P('fsdp')
- grad_gate: float32 [32, 1024, 512], P('fsdp')
- grad_up: float32 [32, 1024, 512], P('fsdp')
- grad_down: float32 [32, 512, 1024], P('fsdp')
The draws below stay inside these ranges and needn't reach their ends.
Inputs may be any that keep to these rules, and one draw needn't show every extreme that they name: `segments`: within a sequence segment numbers never fall; every segment has 1 to 64 tokens and some segment has exactly 64. `routes`: A token's 8 experts differ. Within one sequence no expert is named by more than 48 tokens, and in every draw some sequence names some expert exactly 48 times.
All inputs are finite; a program needn't handle non-finite values.
Results may differ from the reference program's by a relative error of at most 0.018.
Values may be sent and summed in bfloat16 or wider, within the bound.
A program may use at most 192 MiB of HBM per device.

```python
import math
import jax
import jax.numpy as jnp
import numpy as np
from jax import lax

D = 1024
HEADS = 16
KV_HEADS = 8
HEAD_DIM = 64
EXPERTS = 32
FE = 512
TOPK = 8
LENGTH = 128
MB = 2
SEQS = 128
CAP = 48
SEGS = 32
SEG_MOST = 64


def block_levels(key, extent, split, smallest, largest):
    def one(dim, blocks):
        draws = jax.random.uniform(jax.random.fold_in(jax.random.fold_in(key, 6), dim), (blocks,), jnp.float32, smallest / len(split), largest / len(split))
        return jnp.repeat(jnp.exp(draws), extent[dim] // blocks).reshape((-1,) + (1,) * (len(extent) - dim - 1))

    gain = one(*split[0])
    for cut in split[1:]:
        gain = gain * one(*cut)
    return gain


def split_up(number_of, total, bound, skew):
    weights = [(1 << 20) // math.isqrt(rank ** skew) + 1 for rank in range(2, number_of + 1)]
    rest, holding = total - bound - (number_of - 1), [1] * (number_of - 1)
    while rest > 0:
        candidates = [i for i in range(number_of - 1) if holding[i] < bound]
        mass, remaining = sum([weights[i] for i in candidates]), rest
        for i in candidates:
            more = min(bound - holding[i], max(1, remaining * weights[i] // mass), rest)
            holding[i] = holding[i] + more
            rest = rest - more
    return np.array([bound] + holding)


def uneven_parts(rng, amount, total, bound, lean):
    if amount == 2:
        one = jax.random.randint(rng, (), max(1, total - bound), min(bound, total - 1) + 1)
        return jnp.stack([one, total - one])
    tallies = jnp.asarray(split_up(amount, total, bound, lean), jnp.int32)
    couples = (amount - 1) // 2
    giver, taker = tallies[1:1 + 2 * couples:2], tallies[2:2 + 2 * couples:2]
    room = jnp.minimum(giver - 1, bound - taker)
    moved = jax.random.randint(jax.random.fold_in(rng, 1), (couples,), 0, 1 << 20) % (room + 1)
    tallies = tallies.at[1:1 + 2 * couples:2].set(giver - moved).at[2:2 + 2 * couples:2].set(taker + moved)
    return tallies[jax.random.permutation(jax.random.fold_in(rng, 2), amount)]


def assign_block(stream_key, own, number, rows, number_of, top, reach, slope):
    order = jax.random.permutation(stream_key, number_of)
    packed, ordinary = shares(number_of, rows * top, reach, slope, True), shares(number_of, rows * top, reach, slope, False)
    places = jnp.arange(number_of)

    def named(sizes, offset_by):
        used = int((sizes > 0).sum())
        fixed = max(1, used // 4)
        passed = fixed + (places - fixed + offset_by * (used - fixed)) % max(1, number_of - fixed)
        return jnp.zeros((number_of,), jnp.int32).at[order[jnp.where(places < fixed, places, passed)]].set(jnp.asarray(sizes, jnp.int32))

    sizes = jnp.where(number % 4 == 0, named(packed, number // 4), named(ordinary, number - number // 4 - 1))
    mixed = jax.random.permutation(jax.random.fold_in(own, 3), number_of)
    source_of, sink = mixed[0:number_of // 2 * 2:2], mixed[1:number_of // 2 * 2:2]
    slack = jnp.minimum(sizes[source_of] - 1, reach - sizes[sink]) // 2
    slack = jnp.where((source_of == order[0]) | (sink == order[0]) | (sizes[sink] == 0), 0, jnp.maximum(slack, 0))
    passed = jax.random.randint(jax.random.fold_in(own, 4), (number_of // 2,), 0, 1 << 20) % (slack + 1)
    sizes = sizes.at[source_of].add(-passed).at[sink].add(passed)
    items = jnp.searchsorted(jnp.cumsum(sizes), jnp.arange(rows * top), side="right").astype(jnp.int32)
    grid = items.reshape(top, rows).T
    grid = grid[jax.random.permutation(jax.random.fold_in(own, 1), rows)]
    offset_by = jax.random.randint(jax.random.fold_in(own, 2), (rows, 1), 0, top)
    return jnp.take_along_axis(grid, (jnp.arange(top)[None, :] + offset_by) % top, axis=1)


def shares(count, total, most, lean, full):
    weights = [(1 << 20) // math.isqrt(standing ** lean) + 1 for standing in range(1, count + 1)]
    largest = most if full else min(most, max(-(-total // count), total * weights[0] // sum(weights)))
    least = 1 if total - largest >= count - 1 else 0
    counts, surplus = [largest] + [least] * (count - 1), total - largest - least * (count - 1)
    while surplus > 0:
        candidates = [i for i in range(1, count) if counts[i] < largest] or [i for i in range(1, count) if counts[i] < most]
        mass, left = sum([weights[i] for i in candidates]), surplus
        for i in candidates:
            addition = min(most - counts[i], max(1, left * weights[i] // mass), surplus)
            counts[i] = counts[i] + addition
            surplus = surplus - addition
    return np.array(counts)


def noise(own_key, extent, deviation, most, cuts=(), kind=jnp.bfloat16):
    loudness = block_levels(own_key, extent, cuts, -0.22, 0.18) if cuts else 1.0
    entries = jax.random.normal(own_key, extent, jnp.float32) * deviation * loudness
    return jnp.minimum(jnp.maximum(entries, -most), most).astype(kind)


def setup_inputs(seed: int = 0) -> dict:
    streams_of = jax.random.split(jax.random.key(seed), 15)
    tokens = noise(streams_of[0], (MB, SEQS, LENGTH, D), 1.0, 6.0, ((1, 128),))
    segments = jax.vmap(lambda own: jnp.searchsorted(jnp.cumsum(uneven_parts(own, SEGS, LENGTH, SEG_MOST, 2)), jnp.arange(LENGTH), side="right"))(jax.random.split(streams_of[1], MB * SEQS)).reshape((MB, SEQS, LENGTH)).astype(jnp.int32)
    routes_keys = jax.random.split(jax.random.fold_in(streams_of[2], 1), MB * SEQS * LENGTH // LENGTH)
    routes_turns = jax.random.permutation(jax.random.fold_in(streams_of[2], 3), MB * SEQS * LENGTH // LENGTH)
    routes = jax.vmap(lambda own, number: assign_block(jax.random.fold_in(streams_of[2], 2), own, number, LENGTH, EXPERTS, TOPK, CAP, 2))(routes_keys, routes_turns).reshape((MB, SEQS, LENGTH, TOPK))
    cotangent = noise(streams_of[3], (MB, SEQS, LENGTH, D), 1.0, 6.0, ((1, 128),))
    attn_gain = jnp.clip(1.0 + 0.1 * jax.random.normal(streams_of[4], (D,), jnp.float32), 0.5, 1.5).astype(jnp.bfloat16)
    moe_gain = jnp.clip(1.0 + 0.1 * jax.random.normal(streams_of[5], (D,), jnp.float32), 0.5, 1.5).astype(jnp.bfloat16)
    w_query = noise(streams_of[6], (D, HEADS * HEAD_DIM), 0.125, 0.75, ((0, 32),))
    w_key = noise(streams_of[7], (D, KV_HEADS * HEAD_DIM), 0.125, 0.75, ((0, 32),))
    w_value = noise(streams_of[8], (D, KV_HEADS * HEAD_DIM), D ** -0.5, 0.1875, ((0, 32),))
    w_output = noise(streams_of[9], (HEADS * HEAD_DIM, D), 0.25, 1.5, ((0, 32),))
    w_router = noise(streams_of[10], (D, EXPERTS), 0.015625, 0.09375, ((0, 32),))
    w_gate = noise(streams_of[11], (EXPERTS, D, FE), D ** -0.5, 0.1875, ((0, 32),))
    w_up = noise(streams_of[12], (EXPERTS, D, FE), D ** -0.5, 0.1875, ((0, 32),))
    w_down = noise(streams_of[13], (EXPERTS, FE, D), 1.0, 6.0, ((0, 32),))
    return {"tokens": tokens, "segments": segments, "routes": routes, "cotangent": cotangent, "attn_gain": attn_gain, "moe_gain": moe_gain, "w_query": w_query, "w_key": w_key, "w_value": w_value, "w_output": w_output, "w_router": w_router, "w_gate": w_gate, "w_up": w_up, "w_down": w_down}


EPS = 1e-06
RESIDUAL = 0.22
ATT_SCALE = 0.015625
ROPE_BASE = 10000.0
NEG = -1000000000.0
PRECISE = lax.Precision.HIGHEST

@jax.custom_vjp
def low(v):
    return lax.optimization_barrier(v.astype(jnp.bfloat16)).astype(jnp.float32)

@jax.custom_vjp
def low_back(v):
    return v

def low_keep(v):
    return (low(v), None)

def low_pass(kept, grad):
    return (grad,)

def back_keep(v):
    return (v, None)

def back_low(kept, grad):
    return (low(grad),)
low.defvjp(low_keep, low_pass)
low_back.defvjp(back_keep, back_low)

def matmul(left_side, right_side):
    return jnp.dot(left_side, right_side, precision=PRECISE, preferred_element_type=jnp.float32)

def phases(segment):
    length = segment.shape[0]
    places = jnp.arange(length, dtype=jnp.int32)
    starts = jnp.concatenate([jnp.ones((1,), dtype=bool), segment[1:] != segment[:-1]])
    opening = lax.cummax(jnp.where(starts, places, 0), axis=0)
    offset = (places - opening).astype(jnp.float32)
    halves = HEAD_DIM // 2
    frequency = jnp.exp(-math.log(ROPE_BASE) * 2.0 * jnp.arange(halves).astype(jnp.float32) / HEAD_DIM)
    angles = offset[:, None] * frequency[None, :]
    angles = jnp.concatenate([angles, angles], axis=1)[:, None, :]
    visible = (places[None, :] <= places[:, None]) & (segment[:, None] == segment[None, :])
    return (jnp.cos(angles), jnp.sin(angles), visible)

def rotate(values, cos_table, sin_table):
    height = values.shape[0]
    per_head = values.reshape(height, -1, HEAD_DIM)
    halves = HEAD_DIM // 2
    turned = jnp.concatenate([-per_head[..., halves:], per_head[..., :halves]], axis=-1)
    return (per_head * cos_table + turned * sin_table).reshape(height, -1)

def slot_index(route_ids):
    flat_routes = route_ids.reshape(-1)
    choose = (flat_routes[:, None] == jnp.arange(EXPERTS, dtype=jnp.int32)[None, :]).astype(jnp.int32)
    before = jnp.cumsum(choose, axis=0) - choose
    slots = lax.optimization_barrier(jnp.sum(before * choose, axis=1))
    return (flat_routes * CAP + slots).astype(jnp.int32)

def forward(values, params, segment, route_ids):
    attn_gain, moe_gain, w_query, w_key, w_value, w_output, w_router, w_gate, w_up, w_down = params
    length = values.shape[0]
    cos_table, sin_table, visible = phases(segment)
    scale_one = lax.rsqrt(lax.optimization_barrier(jnp.mean(values * values, axis=-1, keepdims=True)) + EPS)
    hidden_one = low(values * scale_one * attn_gain)
    query_raw = low_back(matmul(hidden_one, w_query))
    key_raw = low_back(matmul(hidden_one, w_key))
    value_low = low(low_back(matmul(hidden_one, w_value)))
    query_low = low(rotate(query_raw, cos_table, sin_table)).reshape(length, KV_HEADS, HEADS // KV_HEADS, HEAD_DIM)
    key_low = low(rotate(key_raw, cos_table, sin_table)).reshape(length, KV_HEADS, HEAD_DIM)
    scores = jnp.einsum('qkgd,skd->kgqs', query_low, key_low, precision=PRECISE) * ATT_SCALE
    scores = jnp.where(visible[None, None], low_back(scores), NEG)
    probabilities = low(jax.nn.softmax(scores, axis=-1))
    attended = jnp.einsum('kgqs,skd->qkgd', probabilities, value_low.reshape(length, KV_HEADS, HEAD_DIM), precision=PRECISE)
    attended = low(low_back(attended.reshape(length, -1)))
    branch = low_back(matmul(attended, w_output))
    middle = values + RESIDUAL * branch
    scale_two = lax.rsqrt(lax.optimization_barrier(jnp.mean(middle * middle, axis=-1, keepdims=True)) + EPS)
    routed = low(middle * scale_two * moe_gain)
    logits = low_back(matmul(routed, w_router))
    choose = (route_ids[:, :, None] == jnp.arange(EXPERTS, dtype=jnp.int32)[None, None, :]).astype(jnp.float32)
    chosen = lax.optimization_barrier(jnp.sum(choose * logits[:, None, :], axis=-1))
    gate_weights = jax.nn.softmax(chosen, axis=-1)
    places = slot_index(route_ids)
    copies = low_back(jnp.broadcast_to(routed[:, None, :], (length, TOPK, D))).reshape(length * TOPK, D)
    buffer = jnp.zeros((EXPERTS * CAP, D), jnp.float32).at[places].set(copies).reshape(EXPERTS, CAP, D)
    gate_act = low_back(jnp.einsum('ecd,edf->ecf', buffer, w_gate, precision=PRECISE))
    up_act = low_back(jnp.einsum('ecd,edf->ecf', buffer, w_up, precision=PRECISE))
    inner_act = low(jax.nn.silu(gate_act) * up_act)
    expert_out = low(low_back(jnp.einsum('ecf,efd->ecd', inner_act, w_down, precision=PRECISE)))
    picked = expert_out.reshape(EXPERTS * CAP, D)[places].reshape(length, TOPK, D)
    mixture = lax.optimization_barrier(jnp.sum(gate_weights[:, :, None] * picked, axis=1))
    return middle + RESIDUAL * mixture

def reference(tokens, segments, routes, cotangent, attn_gain, moe_gain, w_query, w_key, w_value, w_output, w_router, w_gate, w_up, w_down):
    params = tuple((member.astype(jnp.float32) for member in (attn_gain, moe_gain, w_query, w_key, w_value, w_output, w_router, w_gate, w_up, w_down)))
    total_seqs = MB * SEQS
    flat_tokens = tokens.astype(jnp.float32).reshape(total_seqs, LENGTH, D)
    flat_segments = segments.reshape(total_seqs, LENGTH)
    flat_routes = routes.reshape(total_seqs, LENGTH, TOPK)
    flat_cotangent = cotangent.astype(jnp.float32).reshape(total_seqs, LENGTH, D)

    def advance(totals, members):
        values, segment, route_ids, upstream = members

        def run_layer(inputs, weights):
            return forward(inputs, weights, segment, route_ids)
        result, pullback = jax.vjp(run_layer, values, params)
        input_grad, weight_grads = pullback(upstream)
        totals = tuple((current + update for current, update in zip(totals, weight_grads)))
        return (totals, (result.astype(jnp.bfloat16), input_grad))
    initial = tuple((jnp.zeros_like(member) for member in params))
    totals, (results, input_grads) = lax.scan(advance, initial, (flat_tokens, flat_segments, flat_routes, flat_cotangent))
    return (results.reshape(MB, SEQS, LENGTH, D), input_grads.reshape(MB, SEQS, LENGTH, D), totals[0], totals[1], totals[2], totals[3], totals[4], totals[5], totals[6], totals[7], totals[8], totals[9])
```

```python
import functools
import math

import jax
import jax.numpy as jnp
from jax import lax
from jax.experimental import pallas as pl
from jax.experimental.pallas import tpu as pltpu
from jax.sharding import PartitionSpec as P

D = 1024
HEADS = 16
KV_HEADS = 8
HEAD_DIM = 64
EXPERTS = 32
FE = 512
TOPK = 8
CAP = 48
LENGTH = 128

EPS = 1e-06
RESIDUAL = 0.22
ATT_SCALE = 0.015625
ROPE_BASE = 10000.0
NEG = -1000000000.0

MESH = pl.DeviceIdType.MESH
F32 = jnp.float32
BF16 = jnp.bfloat16
WIDE = 3200
CUT = 1664
HERE = 4


class Place:
    def __init__(self):
        rep = lax.axis_index("rep")
        flat = lax.axis_index("fsdp")
        self.core = lax.rem(rep, 2)
        self.low = lax.div(rep, 2)
        self.high = lax.div(flat, 16)
        self.x = lax.rem(lax.div(flat, 4), 4)
        self.z = lax.rem(flat, 4)

    def at(self, low=None, core=None, high=None, x=None, z=None):
        low = self.low if low is None else low
        core = self.core if core is None else core
        high = self.high if high is None else high
        x = self.x if x is None else x
        z = self.z if z is None else z
        return (low * 2 + core, high * 16 + x * 4 + z)

    def right(self):
        return self.at(x=lax.rem(self.x + 1, 4))

    def left(self):
        return self.at(x=lax.rem(self.x + 3, 4))

    def above(self):
        return self.at(z=lax.rem(self.z + 1, 4))

    def below(self):
        return self.at(z=lax.rem(self.z + 3, 4))

    def cross(self):
        return self.at(low=1 - self.low, high=1 - self.high)

    def twin(self):
        return self.at(low=1 - self.low)

    def sibling(self):
        return self.at(core=1 - self.core)


class Lines:
    def __init__(self, send_sems, recv_sems):
        self.send_sems, self.recv_sems, self.copies = send_sems, recv_sems, []

    def send(self, src, dst, device):
        i = len(self.copies)
        assert i < self.send_sems.shape[0]
        copy = pltpu.make_async_remote_copy(
            src_ref=src,
            dst_ref=dst,
            send_sem=self.send_sems.at[i],
            recv_sem=self.recv_sems.at[i],
            device_id=device,
            device_id_type=MESH,
        )
        copy.start()
        self.copies.append(copy)
        return copy

    def drain(self):
        for copy in self.copies:
            copy.wait_send()


def greet(partners):
    barrier = pltpu.get_barrier_semaphore()
    for partner in partners:
        pl.semaphore_signal(barrier, inc=1, device_id=partner, device_id_type=MESH)
    pl.semaphore_wait(barrier, len(partners))


def drive(*chains):
    live = list(chains)
    while live:
        for chain in list(live):
            try:
                next(chain)
            except StopIteration:
                live.remove(chain)


def ring_gather(lines, source, slot, half, pos, right, left, spread=None):
    ahead, behind, far = lax.rem(pos + 1, 4), lax.rem(pos + 3, 4), lax.rem(pos + 2, 4)
    spread = spread or (lambda p: None)
    a = lines.send(source, slot(pos), right)
    b = lines.send(source, slot(pos), left)
    yield
    a.wait_recv()
    c = lines.send(half(behind, 0), half(behind, 0), right)
    b.wait_recv()
    d = lines.send(half(ahead, 1), half(ahead, 1), left)
    spread(behind)
    spread(ahead)
    yield
    c.wait_recv()
    d.wait_recv()
    spread(far)


def group_gather(lines, me, source, buf):
    rows = buf.shape[1]
    ahead, behind, far = lax.rem(me.x + 1, 4), lax.rem(me.x + 3, 4), lax.rem(me.x + 2, 4)
    right, left, cross = me.right(), me.left(), me.cross()
    base, other = me.high * 4, (1 - me.high) * 4

    def half(k, h):
        return buf.at[k, pl.ds(h * rows // 2, rows // 2)]

    a = lines.send(source, buf.at[base + me.x], right)
    b = lines.send(source, buf.at[base + me.x], left)
    e = lines.send(source, buf.at[base + me.x], cross)
    yield
    a.wait_recv()
    c = lines.send(half(base + behind, 0), half(base + behind, 0), right)
    b.wait_recv()
    d = lines.send(half(base + ahead, 1), half(base + ahead, 1), left)
    e.wait_recv()
    f = lines.send(buf.at[other + me.x], buf.at[other + me.x], right)
    g = lines.send(buf.at[other + me.x], buf.at[other + me.x], left)
    yield
    c.wait_recv()
    d.wait_recv()
    h = lines.send(buf.at[base + far], buf.at[base + far], cross)
    yield
    f.wait_recv()
    g.wait_recv()
    h.wait_recv()


def tiles(rows, step, body):
    @pl.loop(0, rows // step)
    def _(i):
        body(pl.ds(pl.multiple_of(i * step, step), step))


def group_scatter(lines, me, q, out, by, sf, tl, tr, t, hl, hr, nl, nr, fl, fr, fy):
    rows = q.shape[1]
    mid = rows // 2
    step = min(32, mid)
    ahead, behind, far = lax.rem(me.x + 1, 4), lax.rem(me.x + 3, 4), lax.rem(me.x + 2, 4)
    right, left, cross = me.right(), me.left(), me.cross()
    base, other = me.high * 4, (1 - me.high) * 4
    first, second = pl.ds(0, mid), pl.ds(mid, mid)

    def wide(ref, sl):
        return ref[sl].astype(F32)

    e = lines.send(q.at[other + far], by, cross)
    g1 = lines.send(q.at[other + ahead], tl, right)
    g2 = lines.send(q.at[other + behind], tr, left)
    i1 = lines.send(q.at[base + ahead, second], fl.at[second], right)
    i2 = lines.send(q.at[base + behind, first], fr.at[first], left)
    yield
    e.wait_recv()

    def far_sum(sl):
        sf[sl] = (q[base + far, sl].astype(F32) + wide(by, sl)).astype(sf.dtype)

    tiles(rows, step, far_sum)
    j1 = lines.send(sf.at[first], hl, right)
    j2 = lines.send(sf.at[second], hr, left)
    yield
    g1.wait_recv()
    g2.wait_recv()

    def partner_sum(sl):
        t[sl] = (q[other + me.x, sl].astype(F32) + wide(tl, sl) + wide(tr, sl)).astype(t.dtype)

    tiles(rows, step, partner_sum)
    k = lines.send(t, fy, cross)
    yield
    j1.wait_recv()

    def right_sum(sl):
        nl[sl] = (q[base + ahead, sl].astype(F32) + wide(hl, sl)).astype(nl.dtype)

    tiles(mid, step, right_sum)
    l1 = lines.send(nl, fl.at[first], right)
    j2.wait_recv()

    @pl.loop(0, mid // step)
    def _(i):
        here = pl.ds(pl.multiple_of(i * step, step), step)
        there = pl.ds(pl.multiple_of(mid + i * step, step), step)
        nr[here] = (q[base + behind, there].astype(F32) + wide(hr, here)).astype(nr.dtype)

    l2 = lines.send(nr, fr.at[second], left)
    yield
    for copy in (i1, i2, l1, l2, k):
        copy.wait_recv()

    def total(sl):
        out[sl] = q[base + me.x, sl].astype(F32) + wide(fl, sl) + wide(fr, sl) + wide(fy, sl)

    tiles(rows, step, total)


def ring_scatter(lines, arr, pos, right, left, hl, hr, fl, fr, store):
    n = arr.shape[2]
    ahead, behind, far = lax.rem(pos + 1, 4), lax.rem(pos + 3, 4), lax.rem(pos + 2, 4)
    a = lines.send(arr.at[far, 0], hl, right)
    b = lines.send(arr.at[far, 1], hr, left)
    c = lines.send(arr.at[ahead, 1], fl.at[1], right)
    d = lines.send(arr.at[behind, 0], fr.at[0], left)
    yield
    a.wait_recv()

    @pl.loop(0, n)
    def _(j):
        arr[ahead, 0, j] = (arr[ahead, 0, j].astype(F32) + hl[j].astype(F32)).astype(arr.dtype)

    e = lines.send(arr.at[ahead, 0], fl.at[0], right)
    b.wait_recv()

    @pl.loop(0, n)
    def _(j):
        arr[behind, 1, j] = (arr[behind, 1, j].astype(F32) + hr[j].astype(F32)).astype(arr.dtype)

    f = lines.send(arr.at[behind, 1], fr.at[1], left)
    yield
    for copy in (c, d, e, f):
        copy.wait_recv()
    for half in range(2):

        @pl.loop(0, n)
        def _(j, half=half):
            store(
                half,
                j,
                arr[pos, half, j].astype(F32) + fl[half, j].astype(F32) + fr[half, j].astype(F32),
            )


def early_kernel(
    pack, g, slots, wg, wu, wd, dense, gbuf, sbuf, wgb, wub, wdb, send_sems, recv_sems, local_sems
):
    me = Place()
    right, left, above, below = me.right(), me.left(), me.above(), me.below()
    cross, sibling = me.cross(), me.sibling()
    rows = pl.ds(pl.multiple_of(me.core * 16, 16), 16)
    own = me.high * 4 + me.x
    local = [
        pltpu.make_async_copy(pack.at[rows], dense.at[me.high, me.x, me.z, rows], local_sems.at[0]),
        pltpu.make_async_copy(g, gbuf.at[own], local_sems.at[1]),
        pltpu.make_async_copy(slots, sbuf.at[own], local_sems.at[2]),
        pltpu.make_async_copy(wg, wgb.at[me.z], local_sems.at[3]),
        pltpu.make_async_copy(wu, wub.at[me.z], local_sems.at[4]),
        pltpu.make_async_copy(wd, wdb.at[me.z], local_sems.at[5]),
    ]
    for copy in local:
        copy.start()
    greet((right, left, above, below, cross, sibling))
    lines = Lines(send_sems, recv_sems)
    shared = []

    def dense_chain(columns, x_first):
        def on_z(p, k=None):
            if x_first:
                return dense.at[slice(None) if k is None else k, :, p, rows, columns]
            return dense.at[slice(None) if k is None else k, me.x, p, rows, columns]

        def on_x(p, k=None):
            if x_first:
                return dense.at[slice(None) if k is None else k, p, me.z, rows, columns]
            return dense.at[slice(None) if k is None else k, p, :, rows, columns]

        if x_first:
            first = (on_x(me.x), on_x, on_x, me.x, right, left)
            last = (on_z(me.z), on_z, on_z, me.z, above, below)
        else:
            first = (on_z(me.z), on_z, on_z, me.z, above, below)
            last = (on_x(me.x), on_x, on_x, me.x, right, left)
        yield from ring_gather(lines, *first)

        def spread(p):
            shared.append(lines.send(last[1](p), last[1](p), sibling))

        spread(last[3])
        yield from ring_gather(lines, *last, spread=spread)

    def weight_chain(source, buf):
        half_rows = source.shape[0] // 2
        quarter = half_rows // 2
        start = me.core * half_rows

        def slot(p):
            return buf.at[p, pl.ds(pl.multiple_of(start, half_rows), half_rows)]

        def half(p, k):
            return buf.at[p, pl.ds(pl.multiple_of(start + k * quarter, quarter), quarter)]

        def spread(p):
            shared.append(lines.send(slot(p), slot(p), sibling))

        yield from ring_gather(
            lines,
            source.at[pl.ds(pl.multiple_of(start, half_rows), half_rows)],
            slot,
            half,
            me.z,
            above,
            below,
            spread=spread,
        )

    swap = lines.send(pack.at[rows], dense.at[me.high, me.x, me.z, rows], cross)
    local[0].wait()
    swap.wait_recv()
    drive(
        dense_chain(pl.ds(0, CUT), False),
        dense_chain(pl.ds(CUT, WIDE - CUT), True),
        group_gather(lines, me, g, gbuf),
        group_gather(lines, me, slots, sbuf),
        weight_chain(wg, wgb),
        weight_chain(wu, wub),
        weight_chain(wd, wdb),
    )
    for copy in shared:
        copy.wait_recv()
    for copy in local[1:]:
        copy.wait()
    lines.drain()


def anywhere(n):
    return [pl.BlockSpec(memory_space=pl.ANY)] * n


def vmem(n):
    return [pl.BlockSpec(memory_space=pltpu.VMEM)] * n


def sems(n):
    return [pltpu.SemaphoreType.DMA((n,)), pltpu.SemaphoreType.DMA((n,))]


def params(number=None, limit=56):
    if number is None:
        return pltpu.CompilerParams(vmem_limit_bytes=limit << 20)
    return pltpu.CompilerParams(
        collective_id=number, has_side_effects=True, vmem_limit_bytes=limit << 20
    )


def early(pack, g, slots, wg, wu, wd):
    shape = jax.ShapeDtypeStruct
    return pl.pallas_call(
        early_kernel,
        name="early",
        out_shape=(
            shape((2, 4, 4, 32, WIDE), BF16),
            shape((8,) + g.shape, BF16),
            shape((8,) + slots.shape, BF16),
            shape((4,) + wg.shape, BF16),
            shape((4,) + wu.shape, BF16),
            shape((4,) + wd.shape, BF16),
        ),
        in_specs=anywhere(6),
        out_specs=anywhere(6),
        scratch_shapes=sems(72) + [pltpu.SemaphoreType.DMA((6,))],
        compiler_params=params(0),
    )(pack, g, slots, wg, wu, wd)


def route_kernel(h, gates, hbuf, gbuf, send_sems, recv_sems, local_sems):
    me = Place()
    own = me.high * 4 + me.x
    local = [
        pltpu.make_async_copy(h, hbuf.at[own], local_sems.at[0]),
        pltpu.make_async_copy(gates, gbuf.at[own], local_sems.at[1]),
    ]
    for copy in local:
        copy.start()
    greet((me.right(), me.left(), me.cross()))
    lines = Lines(send_sems, recv_sems)
    drive(group_gather(lines, me, h, hbuf), group_gather(lines, me, gates, gbuf))
    for copy in local:
        copy.wait()
    lines.drain()


def route(h, gates):
    shape = jax.ShapeDtypeStruct
    return pl.pallas_call(
        route_kernel,
        name="route",
        out_shape=(shape((8,) + h.shape, h.dtype), shape((8,) + gates.shape, gates.dtype)),
        in_specs=anywhere(2),
        out_specs=anywhere(2),
        scratch_shapes=sems(24) + [pltpu.SemaphoreType.DMA((2,))],
        compiler_params=params(1),
    )(h, gates)


def scatter_scratch(rows, columns, dtype):
    full = pltpu.VMEM((rows, columns), dtype)
    half = pltpu.VMEM((rows // 2, columns), dtype)
    return [full] * 5 + [half] * 4 + [full] * 3


def back_kernel(qy, qh, qg, y, dh, dg, *scratch):
    me = Place()
    send_sems, recv_sems = scratch[:2]
    greet((me.right(), me.left(), me.cross()))
    lines = Lines(send_sems, recv_sems)
    drive(
        group_scatter(lines, me, qg, dg, *scratch[2:14]),
        group_scatter(lines, me, qh, dh, *scratch[14:26]),
        group_scatter(lines, me, qy, y, *scratch[26:38]),
    )
    lines.drain()


def send_back(qy, qh, qg):
    shape = jax.ShapeDtypeStruct
    rows = qy.shape[1]
    return pl.pallas_call(
        back_kernel,
        name="send_back",
        out_shape=(shape((rows, D), F32), shape((rows, D), F32), shape(qg.shape[1:], F32)),
        in_specs=vmem(3),
        out_specs=vmem(3),
        scratch_shapes=sems(36)
        + scatter_scratch(qg.shape[1], qg.shape[2], F32)
        + scatter_scratch(rows, D, BF16)
        + scatter_scratch(rows, D, BF16),
        compiler_params=params(2),
    )(qy, qh, qg)


def expert_sum_kernel(gg, gu, gd, og, ou, od, *scratch):
    me = Place()
    send_sems, recv_sems = scratch[:2]
    above, below, twin, sibling = me.above(), me.below(), me.twin(), me.sibling()
    greet((above, below, twin, sibling))
    lines = Lines(send_sems, recv_sems)

    def chain(grad, out, rc, acc, hl, hr, fl, fr, tot, yb):
        first = lines.send(grad.at[:, 1 - me.core], rc, sibling)
        yield
        first.wait_recv()

        @pl.loop(0, 32)
        def _(i):
            p, k, j = lax.div(i, 8), lax.rem(lax.div(i, 4), 2), lax.rem(i, 4)
            acc[p, k, j] = (
                grad[p, me.core, k, j].astype(F32) + rc[p, k, j].astype(F32)
            ).astype(BF16)

        def store(k, j, value):
            tot[k, j] = value.astype(BF16)

        yield from ring_scatter(lines, acc, me.z, above, below, hl, hr, fl, fr, store)
        second = lines.send(tot, yb, twin)
        yield
        second.wait_recv()
        for k in range(2):

            @pl.loop(0, 4)
            def _(j, k=k):
                out[me.core, k, j] = tot[k, j].astype(F32) + yb[k, j].astype(F32)

        last = lines.send(out.at[me.core], out.at[me.core], sibling)
        yield
        last.wait_recv()

    drive(
        chain(gg, og, *scratch[2:10]),
        chain(gu, ou, *scratch[10:18]),
        chain(gd, od, *scratch[18:26]),
    )
    lines.drain()


def expert_sum(gg, gu, gd):
    def scratch(r, w):
        shapes = [(4, 2, 4, r, w)] * 2 + [(4, r, w)] * 2 + [(2, 4, r, w)] * 4
        return [pltpu.VMEM(s, BF16) for s in shapes]

    shape = jax.ShapeDtypeStruct
    outs = pl.pallas_call(
        expert_sum_kernel,
        name="expert_sum",
        out_shape=(
            shape((2, 2, 4, 64, 512), F32),
            shape((2, 2, 4, 64, 512), F32),
            shape((2, 2, 4, 32, 1024), F32),
        ),
        in_specs=vmem(3),
        out_specs=vmem(3),
        scratch_shapes=sems(30) + scratch(64, 512) + scratch(64, 512) + scratch(32, 1024),
        compiler_params=params(3, 58),
    )(
        gg.reshape(4, 2, 2, 4, 64, 512),
        gu.reshape(4, 2, 2, 4, 64, 512),
        gd.reshape(4, 2, 2, 4, 32, 1024),
    )
    return outs[0].reshape(1, D, FE), outs[1].reshape(1, D, FE), outs[2].reshape(1, FE, D)


def dense_sum_kernel(grads, out, rc, *scratch):
    me = Place()
    send_sems, recv_sems = scratch[:2]
    right, left, above, below = me.right(), me.left(), me.above(), me.below()
    cross, twin, sibling = me.cross(), me.twin(), me.sibling()
    greet((right, left, above, below, cross, twin, sibling))
    lines = Lines(send_sems, recv_sems)
    mine = pl.ds(pl.multiple_of(me.core * 16, 16), 16)
    theirs = pl.ds(pl.multiple_of((1 - me.core) * 16, 16), 16)
    swap = lines.send(grads.at[:, :, :, theirs], rc, sibling)
    swap.wait_recv()

    def chain(columns, x_first, acc, second, hl, hr, fl, fr, hl2, hr2, fl2, fr2, r2, ry, r3, yb):
        @pl.loop(0, 32)
        def _(i):
            k, x, z = lax.div(i, 16), lax.rem(lax.div(i, 4), 4), lax.rem(i, 4)
            value = grads[k, x, z, mine, columns].astype(F32) + rc[k, x, z, :, columns].astype(F32)
            if x_first:
                acc[x, k, z] = value.astype(BF16)
            else:
                acc[z, k, x] = value.astype(BF16)

        yield

        def store(k, j, value):
            second[j, k, 0] = value.astype(BF16)

        def store_last(k, j, value):
            r2[k] = value.astype(BF16)

        on_x, on_z = (me.x, right, left), (me.z, above, below)
        one, two = (on_x, on_z) if x_first else (on_z, on_x)
        yield from ring_scatter(lines, acc, *one, hl, hr, fl, fr, store)
        yield from ring_scatter(lines, second, *two, hl2, hr2, fl2, fr2, store_last)
        a = lines.send(r2.at[1 - me.high], ry, cross)
        yield
        a.wait_recv()
        r3[...] = (r2[me.high].astype(F32) + ry[...].astype(F32)).astype(BF16)
        b = lines.send(r3, yb, twin)
        yield
        b.wait_recv()
        out[mine, columns] = r3[...].astype(F32) + yb[...].astype(F32)
        c = lines.send(out.at[mine, columns], out.at[mine, columns], sibling)
        yield
        c.wait_recv()

    drive(
        chain(pl.ds(0, CUT), True, *scratch[2:16]),
        chain(pl.ds(CUT, WIDE - CUT), False, *scratch[16:30]),
    )
    lines.drain()


def dense_sum(grads):
    def scratch(w):
        shapes = [
            (4, 2, 4, 16, w),
            (4, 2, 1, 16, w),
            (4, 16, w),
            (4, 16, w),
            (2, 4, 16, w),
            (2, 4, 16, w),
            (1, 16, w),
            (1, 16, w),
            (2, 1, 16, w),
            (2, 1, 16, w),
            (2, 16, w),
            (16, w),
            (16, w),
            (16, w),
        ]
        return [pltpu.VMEM(s, BF16) for s in shapes]

    return pl.pallas_call(
        dense_sum_kernel,
        name="dense_sum",
        out_shape=jax.ShapeDtypeStruct((32, WIDE), F32),
        in_specs=vmem(1),
        out_specs=pl.BlockSpec(memory_space=pltpu.VMEM),
        scratch_shapes=[pltpu.VMEM((2, 4, 4, 16, WIDE), BF16)]
        + sems(40)
        + scratch(CUT)
        + scratch(WIDE - CUT),
        compiler_params=params(4),
    )(grads.reshape(2, 4, 4, 32, WIDE))


def dot(a, b, dims=((1,), (0,))):
    return lax.dot_general(a, b, (dims, ((), ())), preferred_element_type=F32)


def experts_kernel(
    h, g, pos, gates, wg, wu, wd, qy, qh, dg, gg, gu, gd, xs, gs, dys, gys, dhs, ms, das, dbs, gcol, dcol
):
    e = pl.program_id(0)
    n_seqs = h.shape[0]
    rows = n_seqs * CAP
    places = lax.broadcasted_iota(jnp.int32, (CAP, LENGTH), 0).astype(F32)

    def slots_of(s, k):
        return pl.ds(pl.multiple_of(s * CAP, CAP), CAP)

    @pl.loop(0, n_seqs)
    def _(s):
        here = slots_of(s, e)
        chosen = places == pos[e, pl.ds(s, 1), :]
        pick = chosen.astype(F32).astype(BF16)
        xs[here] = dot(pick, h[s]).astype(BF16)
        got = dot(pick, g[s])
        weight = jnp.sum(jnp.where(chosen, gates[e, pl.ds(s, 1), :], 0.0), axis=1, keepdims=True)
        gs[here] = got.astype(BF16)
        dys[here] = (weight * (RESIDUAL * got)).astype(BF16)
        gcol[here] = jnp.broadcast_to(weight, (CAP, LENGTH))

    @pl.loop(0, rows // 256)
    def _(r):
        here = pl.ds(pl.multiple_of(r * 256, 256), 256)
        x = xs[here]
        a = dot(x, wg[0])
        b = dot(x, wu[0])
        sig = jax.nn.sigmoid(a)
        swish = a * sig
        m = (swish * b).astype(BF16)
        ms[here] = m
        y = dot(m, wd[0]).astype(BF16).astype(F32)
        inner = RESIDUAL * jnp.sum(gs[here].astype(F32) * y, axis=1, keepdims=True)
        dcol[here] = jnp.broadcast_to(inner, (256, LENGTH))
        gys[e, here] = (gcol[here][:, :1] * y).astype(BF16)
        dm = dot(dys[here], wd[0], ((1,), (1,)))
        da = (dm * b * sig * (1.0 + a * (1.0 - sig))).astype(BF16)
        db = (dm * swish).astype(BF16)
        das[here] = da
        dbs[here] = db
        dh = dot(da, wg[0], ((1,), (1,))) + dot(db, wu[0], ((1,), (1,)))
        dhs[e, here] = dh.astype(BF16)

    @pl.loop(0, n_seqs)
    def _(s):
        chosen = places == pos[e, pl.ds(s, 1), :]
        part = jnp.sum(jnp.where(chosen, dcol[slots_of(s, e)], 0.0), axis=0, keepdims=True)
        dg[e, pl.ds(s, 1), :] = part

    @pl.loop(0, D // 256)
    def _(r):
        here = pl.ds(pl.multiple_of(r * 256, 256), 256)
        x = xs[:, here]
        gg[0, here] = dot(x, das[...], ((0,), (0,))).astype(BF16)
        gu[0, here] = dot(x, dbs[...], ((0,), (0,))).astype(BF16)

    @pl.loop(0, FE // 256)
    def _(r):
        here = pl.ds(pl.multiple_of(r * 256, 256), 256)
        gd[0, here] = dot(ms[:, here], dys[...], ((0,), (0,))).astype(BF16)

    @pl.when(e == HERE - 1)
    def _():
        @pl.loop(0, n_seqs)
        def _(s):
            here = slots_of(s, e)
            pick = jnp.concatenate(
                [(places == pos[k, pl.ds(s, 1), :]).astype(F32).astype(BF16) for k in range(HERE)]
            )
            qy[s] = dot(
                pick, jnp.concatenate([gys[k, here] for k in range(HERE)]), ((0,), (0,))
            ).astype(BF16)
            qh[s] = dot(
                pick, jnp.concatenate([dhs[k, here] for k in range(HERE)]), ((0,), (0,))
            ).astype(BF16)


def experts(h, g, pos, gates, wg, wu, wd):
    n_seqs = h.shape[0]
    rows = n_seqs * CAP
    shape = jax.ShapeDtypeStruct
    whole = pl.BlockSpec(memory_space=pltpu.VMEM)

    def per_expert(a, b):
        return pl.BlockSpec((1, a, b), lambda e: (e, 0, 0))

    return pl.pallas_call(
        experts_kernel,
        name="experts",
        grid=(HERE,),
        out_shape=(
            shape((n_seqs, LENGTH, D), BF16),
            shape((n_seqs, LENGTH, D), BF16),
            shape((HERE, n_seqs, LENGTH), F32),
            shape((HERE, D, FE), BF16),
            shape((HERE, D, FE), BF16),
            shape((HERE, FE, D), BF16),
        ),
        in_specs=[whole] * 4 + [per_expert(D, FE), per_expert(D, FE), per_expert(FE, D)],
        out_specs=(whole, whole, whole, per_expert(D, FE), per_expert(D, FE), per_expert(FE, D)),
        scratch_shapes=[pltpu.VMEM((rows, D), BF16)] * 3
        + [pltpu.VMEM((HERE, rows, D), BF16)] * 2
        + [pltpu.VMEM((rows, FE), BF16)] * 3
        + [pltpu.VMEM((rows, LENGTH), F32)] * 2,
        compiler_params=params(limit=60),
    )(h, g, pos, gates, wg, wu, wd)


def phases(segment):
    length = segment.shape[0]
    places = jnp.arange(length, dtype=jnp.int32)
    same = segment[:, None] == segment[None, :]
    visible = (places[None, :] <= places[:, None]) & same
    offset = jnp.sum(visible.astype(F32), axis=1) - 1.0
    halves = HEAD_DIM // 2
    frequency = jnp.exp(-math.log(ROPE_BASE) * 2.0 * jnp.arange(halves).astype(F32) / HEAD_DIM)
    angles = offset[:, None] * frequency[None, :]
    angles = jnp.concatenate([angles, angles], axis=1)[:, None, :]
    return (jnp.cos(angles), jnp.sin(angles), visible)


def rotate(values, cos_table, sin_table):
    height = values.shape[0]
    per_head = values.reshape(height, -1, HEAD_DIM)
    halves = HEAD_DIM // 2
    turned = jnp.concatenate([-per_head[..., halves:], per_head[..., :halves]], axis=-1)
    return (per_head * cos_table + turned * sin_table).reshape(height, -1)


def slot_table(route_ids):
    length = route_ids.shape[0]
    ids = jnp.arange(EXPERTS, dtype=jnp.int32)
    named = jnp.any(route_ids[None, :, :] == ids[:, None, None], axis=2)
    before = jnp.arange(length)[:, None] < jnp.arange(length)[None, :]
    count = jnp.dot(named.astype(BF16), before.astype(BF16), preferred_element_type=F32)
    return jnp.where(named, count, -1.0)


def normalize(values, gain):
    scale = lax.rsqrt(jnp.mean(values * values, axis=-1, keepdims=True) + EPS)
    normed = values * scale
    return (normed, scale, normed * gain)


def normalize_back(grad_out, normed, scale, gain):
    grad_norm = grad_out * gain
    grad_in = scale * (grad_norm - normed * jnp.mean(grad_norm * normed, axis=-1, keepdims=True))
    return (grad_in, jnp.sum(grad_out * normed, axis=0))


def scores_of(query_low, key_low, visible):
    height = query_low.shape[0]
    query_four = query_low.reshape(height, KV_HEADS, HEADS // KV_HEADS, HEAD_DIM)
    key_three = key_low.reshape(height, KV_HEADS, HEAD_DIM)
    scores = jnp.einsum("qkgd,skd->kgqs", query_four, key_three, preferred_element_type=F32) * ATT_SCALE
    return jnp.where(visible[None, None], scores, NEG)


def attend(query_low, key_low, value_low, visible):
    height = query_low.shape[0]
    scores = scores_of(query_low, key_low, visible)
    highest = jnp.max(scores, axis=-1, keepdims=True)
    log_total = highest + jnp.log(jnp.sum(jnp.exp(scores - highest), axis=-1, keepdims=True))
    attention = jnp.exp(scores - log_total).astype(BF16)
    value_three = value_low.reshape(height, KV_HEADS, HEAD_DIM)
    attended = jnp.einsum("kgqs,skd->qkgd", attention, value_three, preferred_element_type=F32)
    return (attended.reshape(height, -1).astype(BF16), log_total)


def attend_back(query_low, key_low, value_low, visible, log_total, grad_mixed):
    height = query_low.shape[0]
    query_four = query_low.reshape(height, KV_HEADS, HEADS // KV_HEADS, HEAD_DIM)
    key_three = key_low.reshape(height, KV_HEADS, HEAD_DIM)
    value_three = value_low.reshape(height, KV_HEADS, HEAD_DIM)
    attention = jnp.exp(scores_of(query_low, key_low, visible) - log_total)
    attention_low = attention.astype(BF16)
    grad_four = grad_mixed.reshape(height, KV_HEADS, HEADS // KV_HEADS, HEAD_DIM)
    value_grad = jnp.einsum("kgqs,qkgd->skd", attention_low, grad_four, preferred_element_type=F32)
    prob_grad = jnp.einsum("qkgd,skd->kgqs", grad_four, value_three, preferred_element_type=F32)
    inner_prod = jnp.sum(attention * prob_grad, axis=-1, keepdims=True)
    score_grad = (attention * (prob_grad - inner_prod)).astype(BF16)
    query_grad = jnp.einsum("kgqs,skd->qkgd", score_grad, key_three, preferred_element_type=F32) * ATT_SCALE
    key_grad = jnp.einsum("kgqs,qkgd->skd", score_grad, query_four, preferred_element_type=F32) * ATT_SCALE
    return (
        query_grad.reshape(height, -1),
        key_grad.reshape(height, -1),
        value_grad.reshape(height, -1),
    )


def on_device(
    tokens,
    segments,
    routes,
    cotangent,
    attn_gain,
    moe_gain,
    w_query,
    w_key,
    w_value,
    w_output,
    w_router,
    w_gate,
    w_up,
    w_down,
):
    micro = tokens.shape[0]
    rows = micro * LENGTH
    flat = lax.axis_index("fsdp")
    first_expert = (flat // 4) * 4
    segments = segments[:, 0]
    routes = routes[:, 0]
    slots = jax.vmap(slot_table)(routes)
    small = jnp.concatenate(
        [w_router, attn_gain[:, None], moe_gain[:, None], jnp.zeros((32, 94), BF16)], axis=1
    )
    pack = jnp.concatenate([w_query, w_key, w_value, w_output, small], axis=1)
    upstream = cotangent.reshape(rows, D)
    dense, gbuf, sbuf, wgb, wub, wdb = early(
        pack,
        upstream,
        slots.reshape(micro * EXPERTS, LENGTH).astype(BF16),
        w_gate[0],
        w_up[0],
        w_down[0],
    )
    dense = dense.reshape(D, WIDE)
    wq, wk, wv, wo = dense[:, :1024], dense[:, 1024:1536], dense[:, 1536:2048], dense[:, 2048:3072]
    wr = dense[:, 3072:3104]
    gain_one = dense[:, 3104].astype(F32)
    gain_two = dense[:, 3105].astype(F32)

    inputs = tokens.reshape(rows, D).astype(F32)
    cos_table, sin_table, visible = jax.vmap(phases)(segments)

    def split(a):
        return a.reshape((micro, LENGTH) + a.shape[1:])

    def join(a):
        return a.reshape((rows,) + a.shape[2:])

    normed_one, scale_one, hidden_one = normalize(inputs, gain_one)
    hidden_low = hidden_one.astype(BF16)
    query_raw = jnp.dot(hidden_low, wq, preferred_element_type=F32)
    key_raw = jnp.dot(hidden_low, wk, preferred_element_type=F32)
    value_low = jnp.dot(hidden_low, wv, preferred_element_type=F32).astype(BF16)
    query_low = jax.vmap(rotate)(split(query_raw), cos_table, sin_table).astype(BF16)
    key_low = jax.vmap(rotate)(split(key_raw), cos_table, sin_table).astype(BF16)
    mixed, log_total = jax.vmap(attend)(query_low, key_low, split(value_low), visible)
    mixed_low = join(mixed)
    middle = inputs + RESIDUAL * jnp.dot(mixed_low, wo, preferred_element_type=F32)
    normed_two, scale_two, hidden_two = normalize(middle, gain_two)
    routed_low = hidden_two.astype(BF16)
    logits = jnp.dot(routed_low, wr, preferred_element_type=F32)
    by_expert = jnp.swapaxes(split(logits), 1, 2)
    named = slots >= 0
    shifted = jnp.where(named, by_expert, -jnp.inf)
    top = jnp.max(shifted, axis=1, keepdims=True)
    raised = jnp.exp(shifted - top)
    gates = raised / jnp.sum(raised, axis=1, keepdims=True)

    hbuf, gatebuf = route(routed_low, gates.reshape(micro * EXPERTS, LENGTH))

    def mine(buf):
        by_seq = buf.reshape(8 * micro, EXPERTS, LENGTH)
        part = lax.dynamic_slice_in_dim(by_seq, first_expert, HERE, axis=1)
        return jnp.swapaxes(part, 0, 1).astype(F32)

    qy, qh, dg, gg, gu, gd = experts(
        hbuf.reshape(8 * micro, LENGTH, D),
        gbuf.reshape(8 * micro, LENGTH, D),
        mine(sbuf),
        mine(gatebuf),
        wgb,
        wub,
        wdb,
    )
    qg = lax.dynamic_update_slice_in_dim(
        jnp.zeros((8 * micro, EXPERTS, LENGTH), F32), jnp.swapaxes(dg, 0, 1), first_expert, axis=1
    )
    mixture, routed_grad, gate_grad = send_back(
        qy.reshape(8, rows, D), qh.reshape(8, rows, D), qg.reshape(8, micro * EXPERTS, LENGTH)
    )
    grad_gate, grad_up, grad_down = expert_sum(gg, gu, gd)

    result = (middle + RESIDUAL * mixture).astype(BF16)
    gate_grad = gate_grad.reshape(micro, EXPERTS, LENGTH)
    choice = gates * (gate_grad - jnp.sum(gates * gate_grad, axis=1, keepdims=True))
    logit_grad = join(jnp.swapaxes(choice, 1, 2)).astype(BF16)
    router_grad = dot(routed_low, logit_grad, ((0,), (0,)))
    routed_grad = routed_grad + dot(logit_grad, wr, ((1,), (1,)))
    middle_grad, gain_two_grad = normalize_back(routed_grad, normed_two, scale_two, gain_two)
    middle_grad = middle_grad + upstream.astype(F32)
    branch_low = (RESIDUAL * middle_grad).astype(BF16)
    output_grad = dot(mixed_low, branch_low, ((0,), (0,)))
    mixed_grad = dot(branch_low, wo, ((1,), (1,))).astype(BF16)
    query_grad, key_grad, value_grad = jax.vmap(attend_back)(
        query_low, key_low, split(value_low), visible, log_total, split(mixed_grad)
    )
    query_low_grad = join(jax.vmap(rotate)(query_grad, cos_table, -sin_table)).astype(BF16)
    key_low_grad = join(jax.vmap(rotate)(key_grad, cos_table, -sin_table)).astype(BF16)
    value_low_grad = join(value_grad).astype(BF16)
    wq_grad = dot(hidden_low, query_low_grad, ((0,), (0,)))
    wk_grad = dot(hidden_low, key_low_grad, ((0,), (0,)))
    wv_grad = dot(hidden_low, value_low_grad, ((0,), (0,)))
    hidden_grad = (
        dot(query_low_grad, wq, ((1,), (1,)))
        + dot(key_low_grad, wk, ((1,), (1,)))
        + dot(value_low_grad, wv, ((1,), (1,)))
    )
    normed_grad, gain_one_grad = normalize_back(hidden_grad, normed_one, scale_one, gain_one)
    grad_tokens = middle_grad + normed_grad
    grads = jnp.concatenate(
        [
            wq_grad.astype(BF16),
            wk_grad.astype(BF16),
            wv_grad.astype(BF16),
            output_grad.astype(BF16),
            router_grad.astype(BF16),
            gain_one_grad[:, None].astype(BF16),
            gain_two_grad[:, None].astype(BF16),
            jnp.zeros((D, 94), BF16),
        ],
        axis=1,
    )
    summed = dense_sum(grads)
    return (
        result.reshape(micro, 1, LENGTH, D),
        grad_tokens.reshape(micro, 1, LENGTH, D),
        summed[:, 3104],
        summed[:, 3105],
        summed[:, :1024],
        summed[:, 1024:1536],
        summed[:, 1536:2048],
        summed[:, 2048:3072],
        summed[:, 3072:3104],
        grad_gate,
        grad_up,
        grad_down,
    )


def solution(mesh):
    sequences = P(None, ("rep", "fsdp"), None, None)
    placed = (
        sequences,
        P(None, ("rep", "fsdp"), None),
        sequences,
        sequences,
        P("fsdp"),
        P("fsdp"),
        P("fsdp", None),
        P("fsdp", None),
        P("fsdp", None),
        P("fsdp", None),
        P("fsdp", None),
        P("fsdp", None, None),
        P("fsdp", None, None),
        P("fsdp", None, None),
    )
    return jax.shard_map(
        on_device,
        mesh=mesh,
        in_specs=placed,
        out_specs=(sequences, sequences) + placed[4:],
        check_vma=False,
    )
```

```python
import functools
import math

import jax
import jax.numpy as jnp
from jax import lax
from jax.experimental import pallas as pl
from jax.experimental.pallas import tpu as pltpu
from jax.sharding import PartitionSpec as P

D = 1024
HEADS = 16
KV_HEADS = 8
HEAD_DIM = 64
EXPERTS = 32
FE = 512
TOPK = 8
CAP = 48
LENGTH = 128

EPS = 1e-06
RESIDUAL = 0.22
ATT_SCALE = 0.015625
ROPE_BASE = 10000.0
NEG = -1000000000.0

MESH = pl.DeviceIdType.MESH
F32 = jnp.float32
BF16 = jnp.bfloat16
WIDE = 3200
CUT = 1664
HERE = 4


class Place:
    def __init__(self):
        rep = lax.axis_index("rep")
        flat = lax.axis_index("fsdp")
        self.core = lax.rem(rep, 2)
        self.low = lax.div(rep, 2)
        self.high = lax.div(flat, 16)
        self.x = lax.rem(lax.div(flat, 4), 4)
        self.z = lax.rem(flat, 4)

    def at(self, low=None, core=None, high=None, x=None, z=None):
        low = self.low if low is None else low
        core = self.core if core is None else core
        high = self.high if high is None else high
        x = self.x if x is None else x
        z = self.z if z is None else z
        return (low * 2 + core, high * 16 + x * 4 + z)

    def right(self):
        return self.at(x=lax.rem(self.x + 1, 4))

    def left(self):
        return self.at(x=lax.rem(self.x + 3, 4))

    def above(self):
        return self.at(z=lax.rem(self.z + 1, 4))

    def below(self):
        return self.at(z=lax.rem(self.z + 3, 4))

    def cross(self):
        return self.at(low=1 - self.low, high=1 - self.high)

    def twin(self):
        return self.at(low=1 - self.low)

    def sibling(self):
        return self.at(core=1 - self.core)


class Lines:
    def __init__(self, send_sems, recv_sems):
        self.send_sems, self.recv_sems, self.copies = send_sems, recv_sems, []

    def send(self, src, dst, device):
        i = len(self.copies)
        assert i < self.send_sems.shape[0]
        copy = pltpu.make_async_remote_copy(
            src_ref=src,
            dst_ref=dst,
            send_sem=self.send_sems.at[i],
            recv_sem=self.recv_sems.at[i],
            device_id=device,
            device_id_type=MESH,
        )
        copy.start()
        self.copies.append(copy)
        return copy

    def drain(self):
        for copy in self.copies:
            copy.wait_send()


def step(*chains):
    for chain in chains:
        next(chain, None)


def greet(partners):
    barrier = pltpu.get_barrier_semaphore()
    for partner in partners:
        pl.semaphore_signal(barrier, inc=1, device_id=partner, device_id_type=MESH)
    pl.semaphore_wait(barrier, len(partners))


def drive(*chains):
    live = list(chains)
    while live:
        for chain in list(live):
            try:
                next(chain)
            except StopIteration:
                live.remove(chain)


def ring_gather(lines, source, slot, half, pos, right, left, spread=None):
    ahead, behind, far = lax.rem(pos + 1, 4), lax.rem(pos + 3, 4), lax.rem(pos + 2, 4)
    spread = spread or (lambda p: None)
    a = lines.send(source, slot(pos), right)
    b = lines.send(source, slot(pos), left)
    yield
    a.wait_recv()
    c = lines.send(half(behind, 0), half(behind, 0), right)
    b.wait_recv()
    d = lines.send(half(ahead, 1), half(ahead, 1), left)
    spread(behind)
    spread(ahead)
    yield
    c.wait_recv()
    d.wait_recv()
    spread(far)


def group_gather(lines, me, source, buf):
    rows = buf.shape[1]
    ahead, behind, far = lax.rem(me.x + 1, 4), lax.rem(me.x + 3, 4), lax.rem(me.x + 2, 4)
    right, left, cross = me.right(), me.left(), me.cross()
    base, other = me.high * 4, (1 - me.high) * 4

    def half(k, h):
        return buf.at[k, pl.ds(h * rows // 2, rows // 2)]

    a = lines.send(source, buf.at[base + me.x], right)
    b = lines.send(source, buf.at[base + me.x], left)
    e = lines.send(source, buf.at[base + me.x], cross)
    yield
    a.wait_recv()
    c = lines.send(half(base + behind, 0), half(base + behind, 0), right)
    b.wait_recv()
    d = lines.send(half(base + ahead, 1), half(base + ahead, 1), left)
    e.wait_recv()
    f = lines.send(buf.at[other + me.x], buf.at[other + me.x], right)
    g = lines.send(buf.at[other + me.x], buf.at[other + me.x], left)
    yield
    c.wait_recv()
    d.wait_recv()
    h = lines.send(buf.at[base + far], buf.at[base + far], cross)
    yield
    f.wait_recv()
    g.wait_recv()
    h.wait_recv()


def tiles(rows, step, body):
    @pl.loop(0, rows // step)
    def _(i):
        body(pl.ds(pl.multiple_of(i * step, step), step))


def group_scatter(lines, me, q, out, by, sf, tl, tr, t, hl, hr, nl, nr, fl, fr, fy):
    rows = q.shape[1]
    mid = rows // 2
    step = min(32, mid)
    ahead, behind, far = lax.rem(me.x + 1, 4), lax.rem(me.x + 3, 4), lax.rem(me.x + 2, 4)
    right, left, cross = me.right(), me.left(), me.cross()
    base, other = me.high * 4, (1 - me.high) * 4
    first, second = pl.ds(0, mid), pl.ds(mid, mid)

    def wide(ref, sl):
        return ref[sl].astype(F32)

    e = lines.send(q.at[other + far], by, cross)
    g1 = lines.send(q.at[other + ahead], tl, right)
    g2 = lines.send(q.at[other + behind], tr, left)
    i1 = lines.send(q.at[base + ahead, second], fl.at[second], right)
    i2 = lines.send(q.at[base + behind, first], fr.at[first], left)
    yield
    e.wait_recv()

    def far_sum(sl):
        sf[sl] = (q[base + far, sl].astype(F32) + wide(by, sl)).astype(sf.dtype)

    tiles(rows, step, far_sum)
    j1 = lines.send(sf.at[first], hl, right)
    j2 = lines.send(sf.at[second], hr, left)
    yield
    g1.wait_recv()
    g2.wait_recv()

    def partner_sum(sl):
        t[sl] = (q[other + me.x, sl].astype(F32) + wide(tl, sl) + wide(tr, sl)).astype(t.dtype)

    tiles(rows, step, partner_sum)
    k = lines.send(t, fy, cross)
    yield
    j1.wait_recv()

    def right_sum(sl):
        nl[sl] = (q[base + ahead, sl].astype(F32) + wide(hl, sl)).astype(nl.dtype)

    tiles(mid, step, right_sum)
    l1 = lines.send(nl, fl.at[first], right)
    j2.wait_recv()

    @pl.loop(0, mid // step)
    def _(i):
        here = pl.ds(pl.multiple_of(i * step, step), step)
        there = pl.ds(pl.multiple_of(mid + i * step, step), step)
        nr[here] = (q[base + behind, there].astype(F32) + wide(hr, here)).astype(nr.dtype)

    l2 = lines.send(nr, fr.at[second], left)
    yield
    for copy in (i1, i2, l1, l2, k):
        copy.wait_recv()

    def total(sl):
        out[sl] = q[base + me.x, sl].astype(F32) + wide(fl, sl) + wide(fr, sl) + wide(fy, sl)

    tiles(rows, step, total)


def ring_scatter(lines, arr, pos, right, left, hl, hr, fl, fr, store):
    n = arr.shape[2]
    ahead, behind, far = lax.rem(pos + 1, 4), lax.rem(pos + 3, 4), lax.rem(pos + 2, 4)
    a = lines.send(arr.at[far, 0], hl, right)
    b = lines.send(arr.at[far, 1], hr, left)
    c = lines.send(arr.at[ahead, 1], fl.at[1], right)
    d = lines.send(arr.at[behind, 0], fr.at[0], left)
    yield
    a.wait_recv()

    @pl.loop(0, n)
    def _(j):
        arr[ahead, 0, j] = arr[ahead, 0, j] + hl[j]

    e = lines.send(arr.at[ahead, 0], fl.at[0], right)
    b.wait_recv()

    @pl.loop(0, n)
    def _(j):
        arr[behind, 1, j] = arr[behind, 1, j] + hr[j]

    f = lines.send(arr.at[behind, 1], fr.at[1], left)
    yield
    for copy in (c, d, e, f):
        copy.wait_recv()
    for half in range(2):

        @pl.loop(0, n)
        def _(j, half=half):
            store(
                half,
                j,
                arr[pos, half, j].astype(F32) + fl[half, j].astype(F32) + fr[half, j].astype(F32),
            )


def dot(a, b, dims=((1,), (0,))):
    return lax.dot_general(a, b, (dims, ((), ())), preferred_element_type=F32)


def lanes():
    return lax.broadcasted_iota(jnp.int32, (1, 128), 1)


def swap_halves(u):
    return jnp.where(
        lax.rem(lanes(), 64) < 32, pltpu.roll(u, 96, axis=1), pltpu.roll(u, 32, axis=1)
    )


def doubled(tile, odd):
    wide = tile.astype(F32)
    turned = pltpu.roll(wide, 64, axis=1)
    low = lanes() < 64
    return jnp.where(low, turned if odd else wide, wide if odd else turned).astype(BF16)


def stacked(pair):
    wide = pair.astype(F32)
    low = lanes() < 64
    return jnp.concatenate([jnp.where(low, wide, 0.0), jnp.where(low, 0.0, wide)]).astype(BF16)


def side_by_side(both):
    return jnp.where(lanes() < 64, both[:128], both[128:])


def folded(even, odd):
    even = even + pltpu.roll(even, 64, axis=1)
    odd = odd + pltpu.roll(odd, 64, axis=1)
    return jnp.where(lanes() < 64, even, odd)


def norm_scale(values):
    return lax.rsqrt(jnp.mean(values * values, axis=1, keepdims=True) + EPS)


def gain_rows(small):
    row = lax.broadcasted_iota(jnp.int32, (8, 128), 0)
    lane = lax.broadcasted_iota(jnp.int32, (8, 128), 1)
    pick = (lane == row + EXPERTS).astype(F32).astype(BF16)
    rows = dot(pick, small, ((1,), (1,)))
    return rows[0:1], rows[1:2]


def column_sums(values, column):
    rows = values.shape[0]
    pick = (lax.broadcasted_iota(jnp.int32, (rows, 128), 1) == column).astype(F32).astype(BF16)
    upper = values.astype(BF16)
    lower = (values - upper.astype(F32)).astype(BF16)
    return dot(upper, pick, ((0,), (0,))) + dot(lower, pick, ((0,), (0,)))


def anywhere(n):
    return [pl.BlockSpec(memory_space=pl.ANY)] * n


def vmem(n):
    return [pl.BlockSpec(memory_space=pltpu.VMEM)] * n


def sems(n):
    return [pltpu.SemaphoreType.DMA((n,)), pltpu.SemaphoreType.DMA((n,))]


def params(number=None, limit=56):
    if number is None:
        return pltpu.CompilerParams(vmem_limit_bytes=limit << 20)
    return pltpu.CompilerParams(
        collective_id=number, has_side_effects=True, vmem_limit_bytes=limit << 20
    )


def front_kernel(
    tokens, cos, sin, keep, slots, pack, g, wg, wu, wd,
    dense, gbuf, sbuf, wgb, wub, wdb, hbuf, gatebuf, q, k, v, p, o, y1, gates,
    dn, h, send_sems, recv_sems, local_sems,
):
    me = Place()
    right, left, above, below = me.right(), me.left(), me.above(), me.below()
    cross, sibling = me.cross(), me.sibling()
    rows = pl.ds(pl.multiple_of(me.core * 16, 16), 16)
    own = me.high * 4 + me.x
    local = [
        pltpu.make_async_copy(pack.at[rows], dn.at[me.high, me.x, me.z, rows], local_sems.at[0]),
        pltpu.make_async_copy(g, gbuf.at[own], local_sems.at[1]),
        pltpu.make_async_copy(slots, sbuf.at[own], local_sems.at[2]),
        pltpu.make_async_copy(wg, wgb.at[me.z], local_sems.at[3]),
        pltpu.make_async_copy(wu, wub.at[me.z], local_sems.at[4]),
        pltpu.make_async_copy(wd, wdb.at[me.z], local_sems.at[5]),
    ]
    for copy in local:
        copy.start()
    greet((right, left, above, below, cross, sibling))
    lines = Lines(send_sems, recv_sems)
    shared = []

    def dense_chain(columns, x_first):
        def on_z(p, k=None):
            if x_first:
                return dn.at[slice(None) if k is None else k, :, p, rows, columns]
            return dn.at[slice(None) if k is None else k, me.x, p, rows, columns]

        def on_x(p, k=None):
            if x_first:
                return dn.at[slice(None) if k is None else k, p, me.z, rows, columns]
            return dn.at[slice(None) if k is None else k, p, :, rows, columns]

        if x_first:
            first = (on_x(me.x), on_x, on_x, me.x, right, left)
            last = (on_z(me.z), on_z, on_z, me.z, above, below)
        else:
            first = (on_z(me.z), on_z, on_z, me.z, above, below)
            last = (on_x(me.x), on_x, on_x, me.x, right, left)
        yield from ring_gather(lines, *first)

        def spread(p):
            shared.append(lines.send(last[1](p), last[1](p), sibling))

        spread(last[3])
        yield from ring_gather(lines, *last, spread=spread)

    def weight_chain(source, buf):
        half_rows = source.shape[0] // 2
        quarter = half_rows // 2
        start = me.core * half_rows

        def slot(p):
            return buf.at[p, pl.ds(pl.multiple_of(start, half_rows), half_rows)]

        def half(p, k):
            return buf.at[p, pl.ds(pl.multiple_of(start + k * quarter, quarter), quarter)]

        def spread(p):
            shared.append(lines.send(slot(p), slot(p), sibling))

        yield from ring_gather(
            lines,
            source.at[pl.ds(pl.multiple_of(start, half_rows), half_rows)],
            slot,
            half,
            me.z,
            above,
            below,
            spread=spread,
        )

    swap = lines.send(pack.at[rows], dn.at[me.high, me.x, me.z, rows], cross)
    local[0].wait()
    swap.wait_recv()
    gs = group_gather(lines, me, g, gbuf)
    ss = group_gather(lines, me, slots, sbuf)
    w1, w2, w3 = weight_chain(wg, wgb), weight_chain(wu, wub), weight_chain(wd, wdb)
    drive(dense_chain(pl.ds(0, CUT), False), dense_chain(pl.ds(CUT, WIDE - CUT), True))
    for copy in shared:
        copy.wait_recv()
    del shared[:]
    step(gs, ss, w1)
    keeping = pltpu.make_async_copy(dn, dense, local_sems.at[6])
    keeping.start()

    def weight(start, size):
        return dn[:, :, :, :, start : start + size].reshape(D, size)

    small = weight(3072, 128)
    gain_one, gain_two = gain_rows(small)
    x = tokens[...].astype(F32)
    h[...] = (x * norm_scale(x) * gain_one).astype(BF16)
    for piece in range(4):
        raw = dot(h[...], weight(piece * 256, 256))
        for t in range(2):
            u = raw[:, t * 128 : t * 128 + 128]
            q[:, piece * 256 + t * 128 : piece * 256 + t * 128 + 128] = (
                u * cos[...] + swap_halves(u) * sin[...]
            ).astype(BF16)
    for piece in range(2):
        raw = dot(h[...], weight(1024 + piece * 256, 256))
        for t in range(2):
            u = raw[:, t * 128 : t * 128 + 128]
            k[:, piece * 256 + t * 128 : piece * 256 + t * 128 + 128] = (
                u * cos[...] + swap_halves(u) * sin[...]
            ).astype(BF16)
    v[...] = dot(h[...], weight(1536, 512)).astype(BF16)
    step(w2)

    def attend(i):
        s, m = lax.div(i, 4), lax.rem(i, 4)
        here = pl.ds(pl.multiple_of(s * 128, 128), 128)
        column = pl.ds(pl.multiple_of(m * 128, 128), 128)
        seen = keep[s]
        seen = jnp.concatenate([seen, seen]) > 0.0
        k_tile, v_tile = k[here, column], v[here, column]
        for odd in range(2):
            q_column = pl.ds(pl.multiple_of(m * 256 + odd * 128, 128), 128)
            scores = dot(stacked(q[here, q_column]), doubled(k_tile, odd), ((1,), (1,))) * ATT_SCALE
            scores = jnp.where(seen, scores, NEG)
            raised = jnp.exp(scores - jnp.max(scores, axis=1, keepdims=True))
            probs = raised / jnp.sum(raised, axis=1, keepdims=True)
            p[i, odd] = probs
            both = dot(probs.astype(BF16), doubled(v_tile, odd))
            o[here, q_column] = side_by_side(both).astype(BF16)

    for part in range(4):

        @pl.loop(part * 2, part * 2 + 2)
        def _(i):
            attend(i)

        if part == 1:
            step(w1)
        if part == 2:
            step(gs, ss)
        if part == 3:
            step(w3)

    middle = tokens[...].astype(F32) + RESIDUAL * dot(o[...], weight(2048, 1024))
    y1[...] = middle
    h[...] = (middle * norm_scale(middle) * gain_two).astype(BF16)
    logits = dot(small, h[...], ((0,), (1,)))[:EXPERTS]
    named = slots[...] >= 0.0
    top = jnp.max(jnp.where(named, logits, -jnp.inf), axis=0, keepdims=True)
    raised = jnp.where(named, jnp.exp(jnp.where(named, logits - top, 0.0)), 0.0)
    gates[...] = raised / jnp.sum(raised, axis=0, keepdims=True)

    late = [
        pltpu.make_async_copy(h, hbuf.at[own], local_sems.at[7]),
        pltpu.make_async_copy(gates, gatebuf.at[own], local_sems.at[8]),
    ]
    for copy in late:
        copy.start()
    drive(
        group_gather(lines, me, h, hbuf),
        group_gather(lines, me, gates, gatebuf),
        gs,
        ss,
        w1,
        w2,
        w3,
    )
    for copy in shared:
        copy.wait_recv()
    for copy in local[1:] + [keeping] + late:
        copy.wait()
    lines.drain()


def front(tokens, cos, sin, keep, slots, pack, g, wg, wu, wd):
    shape = jax.ShapeDtypeStruct
    rows = tokens.shape[0]
    return pl.pallas_call(
        front_kernel,
        name="front",
        out_shape=(
            shape((2, 4, 4, 32, WIDE), BF16),
            shape((8,) + g.shape, BF16),
            shape((8,) + slots.shape, F32),
            shape((4,) + wg.shape, BF16),
            shape((4,) + wu.shape, BF16),
            shape((4,) + wd.shape, BF16),
            shape((8, rows, D), BF16),
            shape((8, EXPERTS, rows), F32),
            shape((rows, 1024), BF16),
            shape((rows, 512), BF16),
            shape((rows, 512), BF16),
            shape((8, 2, 256, 128), F32),
            shape((rows, 1024), BF16),
            shape((rows, D), F32),
            shape((EXPERTS, rows), F32),
        ),
        in_specs=vmem(6) + anywhere(4),
        out_specs=anywhere(8) + vmem(7),
        scratch_shapes=[pltpu.VMEM((2, 4, 4, 32, WIDE), BF16), pltpu.VMEM((rows, D), BF16)]
        + sems(88)
        + [pltpu.SemaphoreType.DMA((9,))],
        compiler_params=params(0),
    )(tokens, cos, sin, keep, slots, pack, g, wg, wu, wd)


def scatter_scratch(rows, columns, dtype):
    full = pltpu.VMEM((rows, columns), dtype)
    half = pltpu.VMEM((rows // 2, columns), dtype)
    return [full] * 5 + [half] * 4 + [full] * 3


def back_kernel(qh, qg, dh, dg, *scratch):
    me = Place()
    send_sems, recv_sems = scratch[:2]
    greet((me.right(), me.left(), me.cross()))
    lines = Lines(send_sems, recv_sems)
    drive(
        group_scatter(lines, me, qg, dg, *scratch[2:14]),
        group_scatter(lines, me, qh, dh, *scratch[14:26]),
    )
    lines.drain()


def send_back(qh, qg):
    shape = jax.ShapeDtypeStruct
    rows = qh.shape[1]
    return pl.pallas_call(
        back_kernel,
        name="send_back",
        out_shape=(shape((rows, D), F32), shape(qg.shape[1:], F32)),
        in_specs=vmem(2),
        out_specs=vmem(2),
        scratch_shapes=sems(36)
        + scatter_scratch(qg.shape[1], qg.shape[2], F32)
        + scatter_scratch(rows, D, BF16),
        compiler_params=params(1),
    )(qh, qg)


def retreat_kernel(
    tokens, cos, sin, gates, dense, g, y1, q, k, v, p, o, dh, dg, qy, gg, gu, gd,
    grads, grad_tokens, result, tg, tu, td,
    h, do, dq, dk, dv, small_grad, mixture, *scratch,
):
    me = Place()
    send_sems, recv_sems, local_sems = scratch[:3]
    above, below, sibling = me.above(), me.below(), me.sibling()
    local = []
    for i, (grad, acc) in enumerate(((gg, scratch[4]), (gu, scratch[10]), (gd, scratch[16]))):
        local.append(pltpu.make_async_copy(grad.at[:, me.core], acc, local_sems.at[i]))
        local[-1].start()
    greet((me.right(), me.left(), me.cross(), above, below, sibling))
    lines = Lines(send_sems, recv_sems)

    def chain(grad, tot, mine, rc, acc, hl, hr, fl, fr):
        first = lines.send(grad.at[:, 1 - me.core], rc, sibling)
        yield
        mine.wait()
        first.wait_recv()

        @pl.loop(0, 32)
        def _(i):
            a, b, j = lax.div(i, 8), lax.rem(lax.div(i, 4), 2), lax.rem(i, 4)
            acc[a, b, j] = acc[a, b, j] + rc[a, b, j]

        def store(b, j, value):
            tot[b, j] = value.astype(BF16)

        yield from ring_scatter(lines, acc, me.z, above, below, hl, hr, fl, fr, store)

    e1 = chain(gg, tg, local[0], *scratch[3:9])
    e2 = chain(gu, tu, local[1], *scratch[9:15])
    e3 = chain(gd, td, local[2], *scratch[15:21])
    ys = group_scatter(lines, me, qy, mixture, *scratch[21:33])
    step(e1, e2, e3, ys)

    small = dense[:, 3072:3200]
    gain_one, gain_two = gain_rows(small)
    x = tokens[...].astype(F32)
    h[...] = (x * norm_scale(x) * gain_one).astype(BF16)
    middle = y1[...]
    scale = norm_scale(middle)
    normed = middle * scale
    routed = (normed * gain_two).astype(BF16)
    inner = jnp.sum(gates[...] * dg[...], axis=0, keepdims=True)
    choice = gates[...] * (dg[...] - inner)
    by_token = jnp.transpose(
        jnp.concatenate([choice, jnp.zeros((128 - EXPERTS, choice.shape[1]), F32)])
    ).astype(BF16)
    dh2 = dh[...] + dot(by_token, small, ((1,), (1,)))
    small_grad[...] = dot(routed, by_token, ((0,), (0,))) + column_sums(dh2 * normed, EXPERTS + 1)
    dn = dh2 * gain_two
    dy = g[...].astype(F32) + scale * (dn - normed * jnp.mean(dn * normed, axis=1, keepdims=True))
    grad_tokens[...] = dy
    dz = (RESIDUAL * dy).astype(BF16)
    step(e1)
    for t in range(4):
        here = slice(t * 256, t * 256 + 256)
        grads[here, 2048:3072] = dot(o[:, here], dz, ((0,), (0,))).astype(BF16)
    do[...] = dot(dz, dense[:, 2048:3072], ((1,), (1,))).astype(BF16)
    step(e2)

    def attend_back(i):
        s, m = lax.div(i, 4), lax.rem(i, 4)
        here = pl.ds(pl.multiple_of(s * 128, 128), 128)
        column = pl.ds(pl.multiple_of(m * 128, 128), 128)
        cos_s, sin_s = cos[here], sin[here]
        k_tile, v_tile = k[here, column], v[here, column]
        dk_both, dv_both = [], []
        for odd in range(2):
            q_column = pl.ds(pl.multiple_of(m * 256 + odd * 128, 128), 128)
            q_two, do_two = stacked(q[here, q_column]), stacked(do[here, q_column])
            probs = p[i, odd]
            dp = dot(do_two, doubled(v_tile, odd), ((1,), (1,)))
            inner = jnp.sum(probs * dp, axis=1, keepdims=True)
            ds = (probs * (dp - inner)).astype(BF16)
            dv_both.append(dot(probs.astype(BF16), do_two, ((0,), (0,))))
            dk_both.append(dot(ds, q_two, ((0,), (0,))) * ATT_SCALE)
            u = side_by_side(dot(ds, doubled(k_tile, odd))) * ATT_SCALE
            dq[here, q_column] = (u * cos_s - swap_halves(u) * sin_s).astype(BF16)
        u = folded(*dk_both)
        dk[here, column] = (u * cos_s - swap_halves(u) * sin_s).astype(BF16)
        dv[here, column] = folded(*dv_both).astype(BF16)

    for part in range(4):

        @pl.loop(part * 2, part * 2 + 2)
        def _(i):
            attend_back(i)

        step((e3, ys, e1, e2)[part])

    for t in range(4):
        here = slice(t * 256, t * 256 + 256)
        grads[here, 0:1024] = dot(h[:, here], dq[...], ((0,), (0,))).astype(BF16)
        grads[here, 1024:1536] = dot(h[:, here], dk[...], ((0,), (0,))).astype(BF16)
        grads[here, 1536:2048] = dot(h[:, here], dv[...], ((0,), (0,))).astype(BF16)
    dh1 = (
        dot(dq[...], dense[:, 0:1024], ((1,), (1,)))
        + dot(dk[...], dense[:, 1024:1536], ((1,), (1,)))
        + dot(dv[...], dense[:, 1536:2048], ((1,), (1,)))
    )
    step(e3, ys)
    x = tokens[...].astype(F32)
    scale = norm_scale(x)
    normed = x * scale
    grads[:, 3072:3200] = (small_grad[...] + column_sums(dh1 * normed, EXPERTS)).astype(BF16)
    dn = dh1 * gain_one
    grad_tokens[...] += scale * (dn - normed * jnp.mean(dn * normed, axis=1, keepdims=True))
    drive(ys, e1, e2, e3)
    result[...] = (y1[...] + RESIDUAL * mixture[...]).astype(BF16)
    lines.drain()


def halves(r, w):
    return (4, 2, 2, 4, r, w)


def retreat(tokens, cos, sin, gates, dense, g, y1, q, k, v, p, o, dh, dg, qy, gg, gu, gd):
    def scratch(r, w):
        shapes = [(4, 2, 4, r, w)] * 2 + [(4, r, w)] * 2 + [(2, 4, r, w)] * 2
        return [pltpu.VMEM(s, BF16) for s in shapes]

    shape = jax.ShapeDtypeStruct
    rows = tokens.shape[0]
    return pl.pallas_call(
        retreat_kernel,
        name="retreat",
        out_shape=(
            shape((D, WIDE), BF16),
            shape((rows, D), F32),
            shape((rows, D), BF16),
            shape((2, 4, 64, 512), BF16),
            shape((2, 4, 64, 512), BF16),
            shape((2, 4, 32, 1024), BF16),
        ),
        in_specs=vmem(15) + anywhere(3),
        out_specs=vmem(6),
        scratch_shapes=[
            pltpu.VMEM((rows, D), BF16),
            pltpu.VMEM((rows, 1024), BF16),
            pltpu.VMEM((rows, 1024), BF16),
            pltpu.VMEM((rows, 512), BF16),
            pltpu.VMEM((rows, 512), BF16),
            pltpu.VMEM((D, 128), F32),
            pltpu.VMEM((rows, D), F32),
        ]
        + sems(40)
        + [pltpu.SemaphoreType.DMA((3,))]
        + scratch(64, 512)
        + scratch(64, 512)
        + scratch(32, 1024)
        + scatter_scratch(rows, D, BF16),
        compiler_params=params(2, 60),
    )(
        tokens, cos, sin, gates, dense, g, y1, q, k, v, p, o, dh, dg, qy,
        gg.reshape(halves(64, 512)), gu.reshape(halves(64, 512)), gd.reshape(halves(32, 1024)),
    )


def settle_kernel(grads, tg, tu, td, out, og, ou, od, rc, *scratch):
    me = Place()
    send_sems, recv_sems = scratch[:2]
    right, left, above, below = me.right(), me.left(), me.above(), me.below()
    cross, twin, sibling = me.cross(), me.twin(), me.sibling()
    greet((right, left, above, below, cross, twin, sibling))
    lines = Lines(send_sems, recv_sems)
    mine = pl.ds(pl.multiple_of(me.core * 16, 16), 16)
    theirs = pl.ds(pl.multiple_of((1 - me.core) * 16, 16), 16)
    swap = lines.send(grads.at[:, :, :, theirs], rc, sibling)

    def chain(columns, x_first, acc, second, hl, hr, fl, fr, hl2, hr2, fl2, fr2, r2, ry, r3, yb):
        @pl.loop(0, 32)
        def _(i):
            k, x, z = lax.div(i, 16), lax.rem(lax.div(i, 4), 4), lax.rem(i, 4)
            value = grads[k, x, z, mine, columns].astype(F32) + rc[k, x, z, :, columns].astype(F32)
            if x_first:
                acc[x, k, z] = value.astype(BF16)
            else:
                acc[z, k, x] = value.astype(BF16)

        yield

        def store(k, j, value):
            second[j, k, 0] = value.astype(BF16)

        def store_last(k, j, value):
            r2[k] = value.astype(BF16)

        on_x, on_z = (me.x, right, left), (me.z, above, below)
        one, two = (on_x, on_z) if x_first else (on_z, on_x)
        yield from ring_scatter(lines, acc, *one, hl, hr, fl, fr, store)
        yield from ring_scatter(lines, second, *two, hl2, hr2, fl2, fr2, store_last)
        a = lines.send(r2.at[1 - me.high], ry, cross)
        yield
        a.wait_recv()
        r3[...] = (r2[me.high].astype(F32) + ry[...].astype(F32)).astype(BF16)
        b = lines.send(r3, yb, twin)
        yield
        b.wait_recv()
        out[mine, columns] = r3[...].astype(F32) + yb[...].astype(F32)
        c = lines.send(out.at[mine, columns], out.at[mine, columns], sibling)
        yield
        c.wait_recv()

    def swapped(tot, whole, other):
        a = lines.send(tot, other, twin)
        yield
        a.wait_recv()
        for k in range(2):

            @pl.loop(0, 4)
            def _(j, k=k):
                whole[me.core, k, j] = tot[k, j].astype(F32) + other[k, j].astype(F32)

        b = lines.send(whole.at[me.core], whole.at[me.core], sibling)
        yield
        b.wait_recv()

    others = [swapped(t, w, s) for t, w, s in zip((tg, tu, td), (og, ou, od), scratch[30:33])]
    step(*others)
    swap.wait_recv()
    drive(
        chain(pl.ds(0, CUT), True, *scratch[2:16]),
        chain(pl.ds(CUT, WIDE - CUT), False, *scratch[16:30]),
    )
    drive(*others)
    lines.drain()


def settle(grads, tg, tu, td):
    def scratch(w):
        shapes = [
            (4, 2, 4, 16, w),
            (4, 2, 1, 16, w),
            (4, 16, w),
            (4, 16, w),
            (2, 4, 16, w),
            (2, 4, 16, w),
            (1, 16, w),
            (1, 16, w),
            (2, 1, 16, w),
            (2, 1, 16, w),
            (2, 16, w),
            (16, w),
            (16, w),
            (16, w),
        ]
        return [pltpu.VMEM(s, BF16) for s in shapes]

    shape = jax.ShapeDtypeStruct
    return pl.pallas_call(
        settle_kernel,
        name="settle",
        out_shape=(
            shape((32, WIDE), F32),
            shape((2, 2, 4, 64, 512), F32),
            shape((2, 2, 4, 64, 512), F32),
            shape((2, 2, 4, 32, 1024), F32),
        ),
        in_specs=vmem(4),
        out_specs=vmem(4),
        scratch_shapes=[pltpu.VMEM((2, 4, 4, 16, WIDE), BF16)]
        + sems(48)
        + scratch(CUT)
        + scratch(WIDE - CUT)
        + [pltpu.VMEM(t.shape, BF16) for t in (tg, tu, td)],
        compiler_params=params(3),
    )(grads.reshape(2, 4, 4, 32, WIDE), tg, tu, td)


def experts_kernel(
    h, g, pos, gates, wg, wu, wd, qy, qh, dg, gg, gu, gd, xs, gs, dys, gys, dhs, ms, das, dbs, gcol, dcol
):
    e = pl.program_id(0)
    n_seqs = h.shape[0]
    rows = n_seqs * CAP
    places = lax.broadcasted_iota(jnp.int32, (CAP, LENGTH), 0).astype(F32)

    def slots_of(s, k):
        return pl.ds(pl.multiple_of(s * CAP, CAP), CAP)

    @pl.loop(0, n_seqs)
    def _(s):
        here = slots_of(s, e)
        chosen = places == pos[e, pl.ds(s, 1), :]
        pick = chosen.astype(F32).astype(BF16)
        xs[here] = dot(pick, h[s]).astype(BF16)
        got = dot(pick, g[s])
        weight = jnp.sum(jnp.where(chosen, gates[e, pl.ds(s, 1), :], 0.0), axis=1, keepdims=True)
        gs[here] = got.astype(BF16)
        dys[here] = (weight * (RESIDUAL * got)).astype(BF16)
        gcol[here] = jnp.broadcast_to(weight, (CAP, LENGTH))

    @pl.loop(0, rows // 256)
    def _(r):
        here = pl.ds(pl.multiple_of(r * 256, 256), 256)
        x = xs[here]
        a = dot(x, wg[0])
        b = dot(x, wu[0])
        sig = jax.nn.sigmoid(a)
        swish = a * sig
        m = (swish * b).astype(BF16)
        ms[here] = m
        y = dot(m, wd[0]).astype(BF16).astype(F32)
        inner = RESIDUAL * jnp.sum(gs[here].astype(F32) * y, axis=1, keepdims=True)
        dcol[here] = jnp.broadcast_to(inner, (256, LENGTH))
        gys[e, here] = (gcol[here][:, :1] * y).astype(BF16)
        dm = dot(dys[here], wd[0], ((1,), (1,)))
        da = (dm * b * sig * (1.0 + a * (1.0 - sig))).astype(BF16)
        db = (dm * swish).astype(BF16)
        das[here] = da
        dbs[here] = db
        dh = dot(da, wg[0], ((1,), (1,))) + dot(db, wu[0], ((1,), (1,)))
        dhs[e, here] = dh.astype(BF16)

    @pl.loop(0, n_seqs)
    def _(s):
        chosen = places == pos[e, pl.ds(s, 1), :]
        part = jnp.sum(jnp.where(chosen, dcol[slots_of(s, e)], 0.0), axis=0, keepdims=True)
        dg[e, pl.ds(s, 1), :] = part

    @pl.loop(0, D // 256)
    def _(r):
        here = pl.ds(pl.multiple_of(r * 256, 256), 256)
        x = xs[:, here]
        gg[0, here] = dot(x, das[...], ((0,), (0,))).astype(BF16)
        gu[0, here] = dot(x, dbs[...], ((0,), (0,))).astype(BF16)

    @pl.loop(0, FE // 256)
    def _(r):
        here = pl.ds(pl.multiple_of(r * 256, 256), 256)
        gd[0, here] = dot(ms[:, here], dys[...], ((0,), (0,))).astype(BF16)

    @pl.when(e == HERE - 1)
    def _():
        @pl.loop(0, n_seqs)
        def _(s):
            here = slots_of(s, e)
            pick = jnp.concatenate(
                [(places == pos[k, pl.ds(s, 1), :]).astype(F32).astype(BF16) for k in range(HERE)]
            )
            qy[s] = dot(
                pick, jnp.concatenate([gys[k, here] for k in range(HERE)]), ((0,), (0,))
            ).astype(BF16)
            qh[s] = dot(
                pick, jnp.concatenate([dhs[k, here] for k in range(HERE)]), ((0,), (0,))
            ).astype(BF16)


def experts(h, g, pos, gates, wg, wu, wd):
    n_seqs = h.shape[0]
    rows = n_seqs * CAP
    shape = jax.ShapeDtypeStruct
    whole = pl.BlockSpec(memory_space=pltpu.VMEM)

    def per_expert(a, b):
        return pl.BlockSpec((1, a, b), lambda e: (e, 0, 0))

    return pl.pallas_call(
        experts_kernel,
        name="experts",
        grid=(HERE,),
        out_shape=(
            shape((n_seqs, LENGTH, D), BF16),
            shape((n_seqs, LENGTH, D), BF16),
            shape((HERE, n_seqs, LENGTH), F32),
            shape((HERE, D, FE), BF16),
            shape((HERE, D, FE), BF16),
            shape((HERE, FE, D), BF16),
        ),
        in_specs=[whole] * 4 + [per_expert(D, FE), per_expert(D, FE), per_expert(FE, D)],
        out_specs=(whole, whole, whole, per_expert(D, FE), per_expert(D, FE), per_expert(FE, D)),
        scratch_shapes=[pltpu.VMEM((rows, D), BF16)] * 3
        + [pltpu.VMEM((HERE, rows, D), BF16)] * 2
        + [pltpu.VMEM((rows, FE), BF16)] * 3
        + [pltpu.VMEM((rows, LENGTH), F32)] * 2,
        compiler_params=params(limit=60),
    )(h, g, pos, gates, wg, wu, wd)


def phases(segment):
    length = segment.shape[0]
    places = jnp.arange(length, dtype=jnp.int32)
    same = segment[:, None] == segment[None, :]
    visible = (places[None, :] <= places[:, None]) & same
    offset = jnp.sum(visible.astype(F32), axis=1) - 1.0
    halves = HEAD_DIM // 2
    frequency = jnp.exp(-math.log(ROPE_BASE) * 2.0 * jnp.arange(halves).astype(F32) / HEAD_DIM)
    angles = offset[:, None] * frequency[None, :]
    cos, sin = jnp.cos(angles), jnp.sin(angles)
    return (
        jnp.concatenate([cos] * 4, axis=1),
        jnp.concatenate([-sin, sin] * 2, axis=1),
        visible.astype(F32),
    )


def slot_table(route_ids):
    length = route_ids.shape[0]
    ids = jnp.arange(EXPERTS, dtype=jnp.int32)
    named = jnp.any(route_ids[None, :, :] == ids[:, None, None], axis=2)
    before = jnp.arange(length)[:, None] < jnp.arange(length)[None, :]
    count = jnp.dot(named.astype(BF16), before.astype(BF16), preferred_element_type=F32)
    return jnp.where(named, count, -1.0)


def on_device(
    tokens,
    segments,
    routes,
    cotangent,
    attn_gain,
    moe_gain,
    w_query,
    w_key,
    w_value,
    w_output,
    w_router,
    w_gate,
    w_up,
    w_down,
):
    micro = tokens.shape[0]
    rows = micro * LENGTH
    first_expert = (lax.axis_index("fsdp") // 4) * 4
    cos, sin, keep = jax.vmap(phases)(segments[:, 0])
    cos, sin = cos.reshape(rows, 128), sin.reshape(rows, 128)
    slots = jnp.swapaxes(jax.vmap(slot_table)(routes[:, 0]), 0, 1).reshape(EXPERTS, rows)
    small = jnp.concatenate(
        [w_router, attn_gain[:, None], moe_gain[:, None], jnp.zeros((32, 94), BF16)], axis=1
    )
    pack = jnp.concatenate([w_query, w_key, w_value, w_output, small], axis=1)
    inputs = tokens.reshape(rows, D)
    upstream = cotangent.reshape(rows, D)
    dense, gbuf, sbuf, wgb, wub, wdb, hbuf, gatebuf, q, k, v, p, o, y1, gates = front(
        inputs, cos, sin, keep, slots, pack, upstream, w_gate[0], w_up[0], w_down[0]
    )

    def mine(buf):
        part = lax.dynamic_slice_in_dim(buf, first_expert, HERE, axis=1)
        return jnp.swapaxes(part, 0, 1).reshape(HERE, 8 * micro, LENGTH)

    qy, qh, dg, gg, gu, gd = experts(
        hbuf.reshape(8 * micro, LENGTH, D),
        gbuf.reshape(8 * micro, LENGTH, D),
        mine(sbuf),
        mine(gatebuf),
        wgb,
        wub,
        wdb,
    )
    qg = lax.dynamic_update_slice_in_dim(
        jnp.zeros((8, EXPERTS, rows), F32),
        jnp.swapaxes(dg.reshape(HERE, 8, rows), 0, 1),
        first_expert,
        axis=1,
    )
    dh, gate_grad = send_back(qh.reshape(8, rows, D), qg)
    grads, grad_tokens, result, tg, tu, td = retreat(
        inputs, cos, sin, gates, dense.reshape(D, WIDE), upstream, y1, q, k, v, p, o, dh, gate_grad,
        qy.reshape(8, rows, D), gg, gu, gd,
    )
    summed, grad_gate, grad_up, grad_down = settle(grads, tg, tu, td)
    return (
        result.reshape(micro, 1, LENGTH, D),
        grad_tokens.reshape(micro, 1, LENGTH, D),
        summed[:, 3104],
        summed[:, 3105],
        summed[:, :1024],
        summed[:, 1024:1536],
        summed[:, 1536:2048],
        summed[:, 2048:3072],
        summed[:, 3072:3104],
        grad_gate.reshape(1, D, FE),
        grad_up.reshape(1, D, FE),
        grad_down.reshape(1, FE, D),
    )


def solution(mesh):
    sequences = P(None, ("rep", "fsdp"), None, None)
    placed = (
        sequences,
        P(None, ("rep", "fsdp"), None),
        sequences,
        sequences,
        P("fsdp"),
        P("fsdp"),
        P("fsdp", None),
        P("fsdp", None),
        P("fsdp", None),
        P("fsdp", None),
        P("fsdp", None),
        P("fsdp", None, None),
        P("fsdp", None, None),
        P("fsdp", None, None),
    )
    return jax.shard_map(
        on_device,
        mesh=mesh,
        in_specs=placed,
        out_specs=(sequences, sequences) + placed[4:],
        check_vma=False,
    )
```

```python
import functools
import math

import jax
import jax.numpy as jnp
from jax import lax
from jax.experimental import pallas as pl
from jax.experimental.pallas import tpu as pltpu
from jax.sharding import PartitionSpec as P

D = 1024
HEADS = 16
KV_HEADS = 8
HEAD_DIM = 64
EXPERTS = 32
FE = 512
TOPK = 8
CAP = 48
LENGTH = 128

EPS = 1e-06
RESIDUAL = 0.22
ATT_SCALE = 0.015625
ROPE_BASE = 10000.0
NEG = -1000000000.0

MESH = pl.DeviceIdType.MESH
F32 = jnp.float32
BF16 = jnp.bfloat16
WIDE = 3200
CUT = 1664
HERE = 4


class Place:
    def __init__(self):
        rep = lax.axis_index("rep")
        flat = lax.axis_index("fsdp")
        self.core = lax.rem(rep, 2)
        self.low = lax.div(rep, 2)
        self.high = lax.div(flat, 16)
        self.x = lax.rem(lax.div(flat, 4), 4)
        self.z = lax.rem(flat, 4)

    def at(self, low=None, core=None, high=None, x=None, z=None):
        low = self.low if low is None else low
        core = self.core if core is None else core
        high = self.high if high is None else high
        x = self.x if x is None else x
        z = self.z if z is None else z
        return (low * 2 + core, high * 16 + x * 4 + z)

    def right(self):
        return self.at(x=lax.rem(self.x + 1, 4))

    def left(self):
        return self.at(x=lax.rem(self.x + 3, 4))

    def above(self):
        return self.at(z=lax.rem(self.z + 1, 4))

    def below(self):
        return self.at(z=lax.rem(self.z + 3, 4))

    def cross(self):
        return self.at(low=1 - self.low, high=1 - self.high)

    def twin(self):
        return self.at(low=1 - self.low)

    def sibling(self):
        return self.at(core=1 - self.core)


class Lines:
    def __init__(self, send_sems, recv_sems):
        self.send_sems, self.recv_sems, self.copies = send_sems, recv_sems, []

    def send(self, src, dst, device):
        i = len(self.copies)
        assert i < self.send_sems.shape[0]
        copy = pltpu.make_async_remote_copy(
            src_ref=src,
            dst_ref=dst,
            send_sem=self.send_sems.at[i],
            recv_sem=self.recv_sems.at[i],
            device_id=device,
            device_id_type=MESH,
        )
        copy.start()
        self.copies.append(copy)
        return copy

    def drain(self):
        for copy in self.copies:
            copy.wait_send()


def step(*chains):
    for chain in chains:
        next(chain, None)


def greet(partners):
    barrier = pltpu.get_barrier_semaphore()
    for partner in partners:
        pl.semaphore_signal(barrier, inc=1, device_id=partner, device_id_type=MESH)
    pl.semaphore_wait(barrier, len(partners))


def drive(*chains):
    live = list(chains)
    while live:
        for chain in list(live):
            try:
                next(chain)
            except StopIteration:
                live.remove(chain)


def ring_gather(lines, source, slot, half, pos, right, left, spread=None):
    ahead, behind, far = lax.rem(pos + 1, 4), lax.rem(pos + 3, 4), lax.rem(pos + 2, 4)
    spread = spread or (lambda p: None)
    a = lines.send(source, slot(pos), right)
    b = lines.send(source, slot(pos), left)
    yield
    a.wait_recv()
    c = lines.send(half(behind, 0), half(behind, 0), right)
    b.wait_recv()
    d = lines.send(half(ahead, 1), half(ahead, 1), left)
    spread(behind)
    spread(ahead)
    yield
    c.wait_recv()
    d.wait_recv()
    spread(far)


def group_gather(lines, me, source, buf, start=0, rows=None):
    rows = rows or buf.shape[1]
    ahead, behind, far = lax.rem(me.x + 1, 4), lax.rem(me.x + 3, 4), lax.rem(me.x + 2, 4)
    right, left, cross = me.right(), me.left(), me.cross()
    base, other = me.high * 4, (1 - me.high) * 4

    def slot(k):
        return buf.at[k, pl.ds(start, rows)]

    def half(k, h):
        return buf.at[k, pl.ds(start + h * rows // 2, rows // 2)]

    e = lines.send(source, slot(base + me.x), cross)
    a = lines.send(source, slot(base + me.x), right)
    b = lines.send(source, slot(base + me.x), left)
    yield
    a.wait_recv()
    c = lines.send(half(base + behind, 0), half(base + behind, 0), right)
    b.wait_recv()
    d = lines.send(half(base + ahead, 1), half(base + ahead, 1), left)
    e.wait_recv()
    f = lines.send(slot(other + me.x), slot(other + me.x), right)
    g = lines.send(slot(other + me.x), slot(other + me.x), left)
    yield
    c.wait_recv()
    d.wait_recv()
    h = lines.send(slot(base + far), slot(base + far), cross)
    yield
    f.wait_recv()
    g.wait_recv()
    h.wait_recv()


def tiles(rows, step, body):
    @pl.loop(0, rows // step)
    def _(i):
        body(pl.ds(pl.multiple_of(i * step, step), step))


def group_scatter(lines, me, q, out, start, rows, by, sf, tl, tr, t, hl, hr, nl, nr, fl, fr, fy):
    mid = rows // 2
    step_rows = min(32, mid)
    ahead, behind, far = lax.rem(me.x + 1, 4), lax.rem(me.x + 3, 4), lax.rem(me.x + 2, 4)
    right, left, cross = me.right(), me.left(), me.cross()
    base, other = me.high * 4, (1 - me.high) * 4
    first, second = pl.ds(0, mid), pl.ds(mid, mid)

    def whole(k):
        return q.at[k, pl.ds(start, rows)]

    def part(k, h):
        return q.at[k, pl.ds(start + h * mid, mid)]

    def each(count, offset, body):
        @pl.loop(0, count // step_rows)
        def _(i):
            here = pl.multiple_of(i * step_rows, step_rows)
            there = pl.multiple_of(start + offset + i * step_rows, step_rows)
            body(pl.ds(here, step_rows), pl.ds(there, step_rows))

    e = lines.send(whole(other + far), by, cross)
    g1 = lines.send(whole(other + ahead), tl, right)
    g2 = lines.send(whole(other + behind), tr, left)
    i1 = lines.send(part(base + ahead, 1), fl.at[second], right)
    i2 = lines.send(part(base + behind, 0), fr.at[first], left)
    yield
    e.wait_recv()

    def far_sum(here, there):
        sf[here] = q[base + far, there] + by[here]

    each(rows, 0, far_sum)
    j1 = lines.send(sf.at[first], hl, right)
    j2 = lines.send(sf.at[second], hr, left)
    yield
    g1.wait_recv()
    g2.wait_recv()

    def partner_sum(here, there):
        total = q[other + me.x, there].astype(F32) + tl[here].astype(F32) + tr[here].astype(F32)
        t[here] = total.astype(t.dtype)

    each(rows, 0, partner_sum)
    k = lines.send(t, fy, cross)
    yield
    j1.wait_recv()

    def right_sum(here, there):
        nl[here] = q[base + ahead, there] + hl[here]

    each(mid, 0, right_sum)
    l1 = lines.send(nl, fl.at[first], right)
    j2.wait_recv()

    def left_sum(here, there):
        nr[here] = q[base + behind, there] + hr[here]

    each(mid, mid, left_sum)
    l2 = lines.send(nr, fr.at[second], left)
    yield
    for copy in (i1, i2, l1, l2, k):
        copy.wait_recv()

    def total(here, there):
        out[there] = (
            q[base + me.x, there].astype(F32)
            + fl[here].astype(F32)
            + fr[here].astype(F32)
            + fy[here].astype(F32)
        )

    each(rows, 0, total)


def ring_scatter(lines, arr, pos, right, left, hl, hr, fl, fr, store):
    n = arr.shape[2]
    ahead, behind, far = lax.rem(pos + 1, 4), lax.rem(pos + 3, 4), lax.rem(pos + 2, 4)
    a = lines.send(arr.at[far, 0], hl, right)
    b = lines.send(arr.at[far, 1], hr, left)
    c = lines.send(arr.at[ahead, 1], fl.at[1], right)
    d = lines.send(arr.at[behind, 0], fr.at[0], left)
    yield
    a.wait_recv()

    @pl.loop(0, n)
    def _(j):
        arr[ahead, 0, j] = arr[ahead, 0, j] + hl[j]

    e = lines.send(arr.at[ahead, 0], fl.at[0], right)
    b.wait_recv()

    @pl.loop(0, n)
    def _(j):
        arr[behind, 1, j] = arr[behind, 1, j] + hr[j]

    f = lines.send(arr.at[behind, 1], fr.at[1], left)
    yield
    for copy in (c, d, e, f):
        copy.wait_recv()
    for half in range(2):

        @pl.loop(0, n)
        def _(j, half=half):
            store(
                half,
                j,
                arr[pos, half, j].astype(F32) + fl[half, j].astype(F32) + fr[half, j].astype(F32),
            )


def dot(a, b, dims=((1,), (0,))):
    return lax.dot_general(a, b, (dims, ((), ())), preferred_element_type=F32)


def lanes():
    return lax.broadcasted_iota(jnp.int32, (1, 128), 1)


def swap_halves(u):
    return jnp.where(
        lax.rem(lanes(), 64) < 32, pltpu.roll(u, 96, axis=1), pltpu.roll(u, 32, axis=1)
    )


def doubled(tile, odd):
    wide = tile.astype(F32)
    turned = pltpu.roll(wide, 64, axis=1)
    low = lanes() < 64
    return jnp.where(low, turned if odd else wide, wide if odd else turned).astype(BF16)


def stacked(pair):
    wide = pair.astype(F32)
    low = lanes() < 64
    return jnp.concatenate([jnp.where(low, wide, 0.0), jnp.where(low, 0.0, wide)]).astype(BF16)


def side_by_side(both):
    return jnp.where(lanes() < 64, both[:128], both[128:])


def folded(even, odd):
    even = even + pltpu.roll(even, 64, axis=1)
    odd = odd + pltpu.roll(odd, 64, axis=1)
    return jnp.where(lanes() < 64, even, odd)


def side(table):
    return jnp.concatenate([table[:EXPERTS], table[EXPERTS:]], axis=1)


def phases(segment):
    across = jnp.broadcast_to(segment.astype(F32), (LENGTH, LENGTH))
    down = jnp.transpose(across)
    t = lax.broadcasted_iota(jnp.int32, (LENGTH, LENGTH), 0)
    u = lax.broadcasted_iota(jnp.int32, (LENGTH, LENGTH), 1)
    keep = jnp.where((u <= t) & (across == down), 1.0, 0.0)
    offset = jnp.sum(keep, axis=1, keepdims=True) - 1.0
    step_of = lax.rem(lanes(), 32).astype(F32)
    frequency = jnp.exp(-math.log(ROPE_BASE) * 2.0 * step_of / HEAD_DIM)
    angles = offset * frequency
    sign = jnp.where(lax.rem(lanes(), 64) < 32, -1.0, 1.0)
    return jnp.cos(angles), sign * jnp.sin(angles), keep


def slot_table(route_ids):
    wide = jnp.concatenate([route_ids.astype(F32), jnp.zeros((LENGTH, 128 - TOPK), F32)], axis=1)
    by_choice = jnp.transpose(wide)
    ids = lax.broadcasted_iota(jnp.int32, (EXPERTS, LENGTH), 0).astype(F32)
    named = jnp.zeros((EXPERTS, LENGTH), F32)
    for j in range(TOPK):
        named = jnp.where(by_choice[j : j + 1] == ids, 1.0, named)
    t = lax.broadcasted_iota(jnp.int32, (LENGTH, LENGTH), 0)
    u = lax.broadcasted_iota(jnp.int32, (LENGTH, LENGTH), 1)
    before = jnp.where(t < u, 1.0, 0.0).astype(BF16)
    return jnp.where(named > 0.0, dot(named.astype(BF16), before), -1.0)


def small_shard(router, gains):
    wide = jnp.concatenate([router.astype(F32), jnp.zeros((32, 128 - EXPERTS), F32)], axis=1)
    row = lax.broadcasted_iota(jnp.int32, (32, 32), 0)
    lane = lax.broadcasted_iota(jnp.int32, (32, 32), 1)
    for i in range(2):
        across = jnp.broadcast_to(gains[i : i + 1].astype(F32), (32, 32))
        column = jnp.sum(jnp.where(row == lane, across, 0.0), axis=1, keepdims=True)
        wide = jnp.where(lanes() == EXPERTS + i, column, wide)
    return wide.astype(BF16)


def norm_scale(values):
    return lax.rsqrt(jnp.mean(values * values, axis=1, keepdims=True) + EPS)


def gain_rows(small):
    row = lax.broadcasted_iota(jnp.int32, (8, 128), 0)
    lane = lax.broadcasted_iota(jnp.int32, (8, 128), 1)
    pick = (lane == row + EXPERTS).astype(F32).astype(BF16)
    rows = dot(pick, small, ((1,), (1,)))
    return rows[0:1], rows[1:2]


def column_sums(values, column):
    rows = values.shape[0]
    pick = (lax.broadcasted_iota(jnp.int32, (rows, 128), 1) == column).astype(F32).astype(BF16)
    upper = values.astype(BF16)
    lower = (values - upper.astype(F32)).astype(BF16)
    return dot(upper, pick, ((0,), (0,))) + dot(lower, pick, ((0,), (0,)))


def anywhere(n):
    return [pl.BlockSpec(memory_space=pl.ANY)] * n


def vmem(n):
    return [pl.BlockSpec(memory_space=pltpu.VMEM)] * n


def sems(n):
    return [pltpu.SemaphoreType.DMA((n,)), pltpu.SemaphoreType.DMA((n,))]


def params(number=None, limit=56):
    if number is None:
        return pltpu.CompilerParams(vmem_limit_bytes=limit << 20)
    return pltpu.CompilerParams(
        collective_id=number, has_side_effects=True, vmem_limit_bytes=limit << 20
    )


def front_kernel(
    tokens, segments, routes, wq_own, wk_own, wv_own, wo_own, wr_own, gains, g, wg, wu, wd,
    dense, gbuf, sbuf, wgb, wub, wdb, hbuf, gatebuf, q, k, v, p, o, y1, gates, cos, sin,
    dn, h, keep, slots, send_sems, recv_sems, local_sems,
):
    me = Place()
    right, left, above, below = me.right(), me.left(), me.above(), me.below()
    cross, sibling = me.cross(), me.sibling()
    rows = pl.ds(pl.multiple_of(me.core * 16, 16), 16)
    own = me.high * 4 + me.x
    local = [
        pltpu.make_async_copy(g, gbuf.at[own], local_sems.at[1]),
        pltpu.make_async_copy(wg, wgb.at[me.z], local_sems.at[3]),
        pltpu.make_async_copy(wu, wub.at[me.z], local_sems.at[4]),
        pltpu.make_async_copy(wd, wdb.at[me.z], local_sems.at[5]),
    ]
    for copy in local:
        copy.start()
    shard = dn.at[me.high, me.x, me.z]
    shard[:, 0:1024] = wq_own[...]
    shard[:, 1024:1536] = wk_own[...]
    shard[:, 1536:2048] = wv_own[...]
    shard[:, 2048:3072] = wo_own[...]
    shard[:, 3072:3200] = small_shard(wr_own[...], gains[...])
    greet((right, left, above, below, cross, sibling))
    lines = Lines(send_sems, recv_sems)
    shared = []

    def dense_chain(columns, x_first):
        on_x, on_z = (me.x, right, left), (me.z, above, below)
        (pos, up, down), (pos2, up2, down2) = (on_x, on_z) if x_first else (on_z, on_x)
        ahead, behind, far = lax.rem(pos + 1, 4), lax.rem(pos + 3, 4), lax.rem(pos + 2, 4)

        def piece(one, two, k=None):
            x, z = (one, two) if x_first else (two, one)
            return dn.at[slice(None) if k is None else k, x, z, rows, columns]

        def unit(one):
            def spread(two):
                shared.append(lines.send(piece(one, two), piece(one, two), sibling))

            def slot(two):
                return piece(one, two)

            def half(two, k):
                return piece(one, two, k)

            chain = ring_gather(lines, slot(pos2), slot, half, pos2, up2, down2, spread=spread)
            next(chain)
            spread(pos2)
            return chain

        mine = piece(pos, pos2)
        a = lines.send(mine, mine, up)
        b = lines.send(mine, mine, down)
        units = [unit(pos)]
        yield
        a.wait_recv()
        c = lines.send(piece(behind, pos2, 0), piece(behind, pos2, 0), up)
        units.append(unit(behind))
        b.wait_recv()
        d = lines.send(piece(ahead, pos2, 1), piece(ahead, pos2, 1), down)
        units.append(unit(ahead))
        yield
        step(units[0])
        yield
        c.wait_recv()
        d.wait_recv()
        units.append(unit(far))
        yield
        step(units[1], units[2])
        yield
        step(units[0], units[3])
        yield
        step(*units[1:])
        step(*units)

    def weight_chain(source, buf):
        half_rows = source.shape[0] // 2
        quarter = half_rows // 2
        start = me.core * half_rows

        def slot(p):
            return buf.at[p, pl.ds(pl.multiple_of(start, half_rows), half_rows)]

        def half(p, k):
            return buf.at[p, pl.ds(pl.multiple_of(start + k * quarter, quarter), quarter)]

        def spread(p):
            shared.append(lines.send(slot(p), slot(p), sibling))

        yield from ring_gather(
            lines,
            source.at[pl.ds(pl.multiple_of(start, half_rows), half_rows)],
            slot,
            half,
            me.z,
            above,
            below,
            spread=spread,
        )

    swap = lines.send(shard.at[rows], shard.at[rows], cross)
    for part in range(2):
        here = slice(part * LENGTH, (part + 1) * LENGTH)
        cos[here], sin[here], keep[part] = phases(segments[part : part + 1, :])
        slots[part * EXPERTS : (part + 1) * EXPERTS] = slot_table(routes[here, :])
    local.append(pltpu.make_async_copy(slots, sbuf.at[own], local_sems.at[2]))
    local[-1].start()
    swap.wait_recv()
    gs = group_gather(lines, me, g, gbuf)
    ss = group_gather(lines, me, slots, sbuf)
    w1, w2, w3 = weight_chain(wg, wgb), weight_chain(wu, wub), weight_chain(wd, wdb)
    dense_a, dense_b = dense_chain(pl.ds(0, CUT), False), dense_chain(pl.ds(CUT, WIDE - CUT), True)
    for _ in range(4):
        step(dense_a, dense_b)
    step(gs, ss, w1)
    drive(dense_a, dense_b)
    for copy in shared:
        copy.wait_recv()
    del shared[:]
    step(gs, ss)
    keeping = pltpu.make_async_copy(dn, dense, local_sems.at[6])
    keeping.start()

    def weight(start, size):
        return dn[:, :, :, :, start : start + size].reshape(D, size)

    small = weight(3072, 128)
    gain_one, gain_two = gain_rows(small)
    x = tokens[...].astype(F32)
    h[...] = (x * norm_scale(x) * gain_one).astype(BF16)
    for piece in range(4):
        raw = dot(h[...], weight(piece * 256, 256))
        for t in range(2):
            u = raw[:, t * 128 : t * 128 + 128]
            q[:, piece * 256 + t * 128 : piece * 256 + t * 128 + 128] = (
                u * cos[...] + swap_halves(u) * sin[...]
            ).astype(BF16)
    for piece in range(2):
        raw = dot(h[...], weight(1024 + piece * 256, 256))
        for t in range(2):
            u = raw[:, t * 128 : t * 128 + 128]
            k[:, piece * 256 + t * 128 : piece * 256 + t * 128 + 128] = (
                u * cos[...] + swap_halves(u) * sin[...]
            ).astype(BF16)
    v[...] = dot(h[...], weight(1536, 512)).astype(BF16)
    step(w1, w2)

    def attend(i):
        s, m = lax.div(i, 4), lax.rem(i, 4)
        here = pl.ds(pl.multiple_of(s * 128, 128), 128)
        column = pl.ds(pl.multiple_of(m * 128, 128), 128)
        seen = keep[s]
        seen = jnp.concatenate([seen, seen]) > 0.0
        k_tile, v_tile = k[here, column], v[here, column]
        for odd in range(2):
            q_column = pl.ds(pl.multiple_of(m * 256 + odd * 128, 128), 128)
            scores = dot(stacked(q[here, q_column]), doubled(k_tile, odd), ((1,), (1,))) * ATT_SCALE
            scores = jnp.where(seen, scores, NEG)
            raised = jnp.exp(scores - jnp.max(scores, axis=1, keepdims=True))
            probs = raised / jnp.sum(raised, axis=1, keepdims=True)
            p[i, odd] = probs
            both = dot(probs.astype(BF16), doubled(v_tile, odd))
            o[here, q_column] = side_by_side(both).astype(BF16)

    late = []
    routed = []
    for part in range(2):

        @pl.loop(part * 4, part * 4 + 4)
        def _(i):
            attend(i)

        here = slice(part * LENGTH, (part + 1) * LENGTH)
        middle = tokens[here].astype(F32) + RESIDUAL * dot(o[here], weight(2048, 1024))
        y1[here] = middle
        h[here] = (middle * norm_scale(middle) * gain_two).astype(BF16)
        routed.append(group_gather(lines, me, h.at[here], hbuf, part * LENGTH, LENGTH))
        step(routed[part])
        late.append(pltpu.make_async_copy(h.at[here], hbuf.at[own, here], local_sems.at[7 + part]))
        late[part].start()
        logits = dot(small, h[here], ((0,), (1,)))[:EXPERTS]
        table = slice(part * EXPERTS, (part + 1) * EXPERTS)
        named = slots[table] >= 0.0
        top = jnp.max(jnp.where(named, logits, -jnp.inf), axis=0, keepdims=True)
        raised = jnp.where(named, jnp.exp(jnp.where(named, logits - top, 0.0)), 0.0)
        gates[table] = raised / jnp.sum(raised, axis=0, keepdims=True)

    weighed = group_gather(lines, me, gates, gatebuf)
    late.append(pltpu.make_async_copy(gates, gatebuf.at[own], local_sems.at[9]))
    late[2].start()
    step(weighed, w3, gs, ss)
    step(routed[0], w2)
    step(routed[1], weighed, w1, w3)
    step(routed[0], w2)
    step(routed[1], weighed)
    drive(routed[0], routed[1], weighed, gs, ss, w1, w2, w3)
    for copy in shared:
        copy.wait_recv()
    for copy in local + [keeping] + late:
        copy.wait()
    lines.drain()


def front(tokens, segments, routes, wq, wk, wv, wo, wr, gains, g, wg, wu, wd):
    shape = jax.ShapeDtypeStruct
    rows = tokens.shape[0]
    slots = shape((2 * EXPERTS, LENGTH), F32)
    return pl.pallas_call(
        front_kernel,
        name="front",
        out_shape=(
            shape((2, 4, 4, 32, WIDE), BF16),
            shape((8,) + g.shape, BF16),
            shape((8,) + slots.shape, F32),
            shape((4,) + wg.shape, BF16),
            shape((4,) + wu.shape, BF16),
            shape((4,) + wd.shape, BF16),
            shape((8, rows, D), BF16),
            shape((8,) + slots.shape, F32),
            shape((rows, 1024), BF16),
            shape((rows, 512), BF16),
            shape((rows, 512), BF16),
            shape((8, 2, 256, 128), F32),
            shape((rows, 1024), BF16),
            shape((rows, D), F32),
            shape(slots.shape, F32),
            shape((rows, 128), F32),
            shape((rows, 128), F32),
        ),
        in_specs=vmem(13),
        out_specs=anywhere(8) + vmem(9),
        scratch_shapes=[
            pltpu.VMEM((2, 4, 4, 32, WIDE), BF16),
            pltpu.VMEM((rows, D), BF16),
            pltpu.VMEM((2, LENGTH, LENGTH), F32),
            pltpu.VMEM(slots.shape, F32),
        ]
        + sems(140)
        + [pltpu.SemaphoreType.DMA((10,))],
        compiler_params=params(0),
    )(tokens, segments, routes, wq, wk, wv, wo, wr, gains, g, wg, wu, wd)


def scatter_scratch(rows, columns, dtype):
    full = pltpu.VMEM((rows, columns), dtype)
    half = pltpu.VMEM((rows // 2, columns), dtype)
    return [full] * 5 + [half] * 4 + [full] * 3


def retreat_kernel(
    tokens, cos, sin, gates, dense, g, y1, q, k, v, p, o, dh, dg, qy, gg, gu, gd,
    grads, grad_tokens, result, tg, tu, td,
    h, do, dq, dk, dv, small_grad, mixture, *scratch,
):
    me = Place()
    send_sems, recv_sems, local_sems = scratch[:3]
    above, below, sibling = me.above(), me.below(), me.sibling()
    local = []
    for i, (grad, acc) in enumerate(((gg, scratch[4]), (gu, scratch[10]), (gd, scratch[16]))):
        local.append(pltpu.make_async_copy(grad.at[:, me.core], acc, local_sems.at[i]))
        local[-1].start()
    greet((me.right(), me.left(), me.cross(), above, below, sibling))
    lines = Lines(send_sems, recv_sems)

    def chain(grad, tot, mine, rc, acc, hl, hr, fl, fr):
        first = lines.send(grad.at[:, 1 - me.core], rc, sibling)
        yield
        mine.wait()
        first.wait_recv()

        @pl.loop(0, 32)
        def _(i):
            a, b, j = lax.div(i, 8), lax.rem(lax.div(i, 4), 2), lax.rem(i, 4)
            acc[a, b, j] = acc[a, b, j] + rc[a, b, j]

        def store(b, j, value):
            tot[b, j] = value.astype(BF16)

        yield from ring_scatter(lines, acc, me.z, above, below, hl, hr, fl, fr, store)

    e1 = chain(gg, tg, local[0], *scratch[3:9])
    e2 = chain(gu, tu, local[1], *scratch[9:15])
    e3 = chain(gd, td, local[2], *scratch[15:21])
    ys = group_scatter(lines, me, qy, mixture, 0, 2 * LENGTH, *scratch[21:33])
    step(e1, e2, e3, ys)

    small = dense[:, 3072:3200]
    gain_one, gain_two = gain_rows(small)
    x = tokens[...].astype(F32)
    h[...] = (x * norm_scale(x) * gain_one).astype(BF16)
    middle = y1[...]
    scale = norm_scale(middle)
    normed = middle * scale
    routed = (normed * gain_two).astype(BF16)
    weights, grad = side(gates), side(dg)
    choice = weights * (grad - jnp.sum(weights * grad, axis=0, keepdims=True))
    by_token = jnp.transpose(
        jnp.concatenate([choice, jnp.zeros((128 - EXPERTS, choice.shape[1]), F32)])
    ).astype(BF16)
    dh2 = dh[...] + dot(by_token, small, ((1,), (1,)))
    small_grad[...] = dot(routed, by_token, ((0,), (0,))) + column_sums(dh2 * normed, EXPERTS + 1)
    dn = dh2 * gain_two
    dy = g[...].astype(F32) + scale * (dn - normed * jnp.mean(dn * normed, axis=1, keepdims=True))
    grad_tokens[...] = dy
    dz = (RESIDUAL * dy).astype(BF16)
    step(e1)
    for t in range(4):
        here = slice(t * 256, t * 256 + 256)
        grads[here, 2048:3072] = dot(o[:, here], dz, ((0,), (0,))).astype(BF16)
    do[...] = dot(dz, dense[:, 2048:3072], ((1,), (1,))).astype(BF16)
    step(e2)

    def attend_back(i):
        s, m = lax.div(i, 4), lax.rem(i, 4)
        here = pl.ds(pl.multiple_of(s * 128, 128), 128)
        column = pl.ds(pl.multiple_of(m * 128, 128), 128)
        cos_s, sin_s = cos[here], sin[here]
        k_tile, v_tile = k[here, column], v[here, column]
        dk_both, dv_both = [], []
        for odd in range(2):
            q_column = pl.ds(pl.multiple_of(m * 256 + odd * 128, 128), 128)
            q_two, do_two = stacked(q[here, q_column]), stacked(do[here, q_column])
            probs = p[i, odd]
            dp = dot(do_two, doubled(v_tile, odd), ((1,), (1,)))
            inner = jnp.sum(probs * dp, axis=1, keepdims=True)
            ds = (probs * (dp - inner)).astype(BF16)
            dv_both.append(dot(probs.astype(BF16), do_two, ((0,), (0,))))
            dk_both.append(dot(ds, q_two, ((0,), (0,))) * ATT_SCALE)
            u = side_by_side(dot(ds, doubled(k_tile, odd))) * ATT_SCALE
            dq[here, q_column] = (u * cos_s - swap_halves(u) * sin_s).astype(BF16)
        u = folded(*dk_both)
        dk[here, column] = (u * cos_s - swap_halves(u) * sin_s).astype(BF16)
        dv[here, column] = folded(*dv_both).astype(BF16)

    for part in range(4):

        @pl.loop(part * 2, part * 2 + 2)
        def _(i):
            attend_back(i)

        step((e3, ys, e1, e2)[part])

    for t in range(4):
        here = slice(t * 256, t * 256 + 256)
        grads[here, 0:1024] = dot(h[:, here], dq[...], ((0,), (0,))).astype(BF16)
        grads[here, 1024:1536] = dot(h[:, here], dk[...], ((0,), (0,))).astype(BF16)
        grads[here, 1536:2048] = dot(h[:, here], dv[...], ((0,), (0,))).astype(BF16)
    dh1 = (
        dot(dq[...], dense[:, 0:1024], ((1,), (1,)))
        + dot(dk[...], dense[:, 1024:1536], ((1,), (1,)))
        + dot(dv[...], dense[:, 1536:2048], ((1,), (1,)))
    )
    step(e3, ys)
    x = tokens[...].astype(F32)
    scale = norm_scale(x)
    normed = x * scale
    grads[:, 3072:3200] = (small_grad[...] + column_sums(dh1 * normed, EXPERTS)).astype(BF16)
    dn = dh1 * gain_one
    grad_tokens[...] += scale * (dn - normed * jnp.mean(dn * normed, axis=1, keepdims=True))
    drive(ys, e1, e2, e3)
    result[...] = (y1[...] + RESIDUAL * mixture[...]).astype(BF16)
    lines.drain()


def halves(r, w):
    return (4, 2, 2, 4, r, w)


def retreat(tokens, cos, sin, gates, dense, g, y1, q, k, v, p, o, dh, dg, qy, gg, gu, gd):
    def scratch(r, w):
        shapes = [(4, 2, 4, r, w)] * 2 + [(4, r, w)] * 2 + [(2, 4, r, w)] * 2
        return [pltpu.VMEM(s, BF16) for s in shapes]

    shape = jax.ShapeDtypeStruct
    rows = tokens.shape[0]
    return pl.pallas_call(
        retreat_kernel,
        name="retreat",
        out_shape=(
            shape((D, WIDE), BF16),
            shape((rows, D), F32),
            shape((rows, D), BF16),
            shape((2, 4, 64, 512), BF16),
            shape((2, 4, 64, 512), BF16),
            shape((2, 4, 32, 1024), BF16),
        ),
        in_specs=vmem(15) + anywhere(3),
        out_specs=vmem(6),
        scratch_shapes=[
            pltpu.VMEM((rows, D), BF16),
            pltpu.VMEM((rows, 1024), BF16),
            pltpu.VMEM((rows, 1024), BF16),
            pltpu.VMEM((rows, 512), BF16),
            pltpu.VMEM((rows, 512), BF16),
            pltpu.VMEM((D, 128), F32),
            pltpu.VMEM((rows, D), F32),
        ]
        + sems(40)
        + [pltpu.SemaphoreType.DMA((3,))]
        + scratch(64, 512)
        + scratch(64, 512)
        + scratch(32, 1024)
        + scatter_scratch(rows, D, BF16),
        compiler_params=params(2, 60),
    )(
        tokens, cos, sin, gates, dense, g, y1, q, k, v, p, o, dh, dg, qy,
        gg.reshape(halves(64, 512)), gu.reshape(halves(64, 512)), gd.reshape(halves(32, 1024)),
    )


def settle_kernel(grads, tg, tu, td, oq, ok, ov, oo, osmall, og, ou, od, rc, out, *scratch):
    me = Place()
    send_sems, recv_sems = scratch[:2]
    right, left, above, below = me.right(), me.left(), me.above(), me.below()
    cross, twin, sibling = me.cross(), me.twin(), me.sibling()
    greet((right, left, above, below, cross, twin, sibling))
    lines = Lines(send_sems, recv_sems)
    mine = pl.ds(pl.multiple_of(me.core * 16, 16), 16)
    theirs = pl.ds(pl.multiple_of((1 - me.core) * 16, 16), 16)

    def swap(columns):
        return lines.send(grads.at[:, :, :, theirs, columns], rc.at[:, :, :, :, columns], sibling)

    swaps = [swap(pl.ds(0, CUT)), swap(pl.ds(CUT, WIDE - CUT))]

    def chain(swap, columns, x_first, acc, second, hl, hr, fl, fr, hl2, hr2, fl2, fr2, r2, ry, r3, yb):
        swap.wait_recv()

        @pl.loop(0, 32)
        def _(i):
            k, x, z = lax.div(i, 16), lax.rem(lax.div(i, 4), 4), lax.rem(i, 4)
            value = grads[k, x, z, mine, columns] + rc[k, x, z, :, columns]
            if x_first:
                acc[x, k, z] = value
            else:
                acc[z, k, x] = value

        yield

        def store(k, j, value):
            second[j, k, 0] = value.astype(BF16)

        def store_last(k, j, value):
            r2[k] = value.astype(BF16)

        on_x, on_z = (me.x, right, left), (me.z, above, below)
        one, two = (on_x, on_z) if x_first else (on_z, on_x)
        yield from ring_scatter(lines, acc, *one, hl, hr, fl, fr, store)
        yield from ring_scatter(lines, second, *two, hl2, hr2, fl2, fr2, store_last)
        a = lines.send(r2.at[1 - me.high], ry, cross)
        yield
        a.wait_recv()
        r3[...] = (r2[me.high].astype(F32) + ry[...].astype(F32)).astype(BF16)
        b = lines.send(r3, yb, twin)
        yield
        b.wait_recv()
        out[mine, columns] = r3[...].astype(F32) + yb[...].astype(F32)
        c = lines.send(out.at[mine, columns], out.at[mine, columns], sibling)
        yield
        c.wait_recv()

    def swapped(tot, whole, other):
        a = lines.send(tot, other, twin)
        yield
        a.wait_recv()
        for k in range(2):

            @pl.loop(0, 4)
            def _(j, k=k):
                whole[me.core, k, j] = tot[k, j].astype(F32) + other[k, j].astype(F32)

        b = lines.send(whole.at[me.core], whole.at[me.core], sibling)
        yield
        b.wait_recv()

    others = [swapped(t, w, s) for t, w, s in zip((tg, tu, td), (og, ou, od), scratch[30:33])]
    step(*others)
    one = chain(swaps[0], pl.ds(0, CUT), True, *scratch[2:16])
    two = chain(swaps[1], pl.ds(CUT, WIDE - CUT), False, *scratch[16:30])
    step(one)
    step(one, two)
    drive(one, two)
    drive(*others)
    start = 0
    for part in (oq, ok, ov, oo, osmall):
        part[...] = out[:, start : start + part.shape[1]]
        start += part.shape[1]
    lines.drain()


def settle(grads, tg, tu, td):
    def scratch(w):
        shapes = [
            (4, 2, 4, 16, w),
            (4, 2, 1, 16, w),
            (4, 16, w),
            (4, 16, w),
            (2, 4, 16, w),
            (2, 4, 16, w),
            (1, 16, w),
            (1, 16, w),
            (2, 1, 16, w),
            (2, 1, 16, w),
            (2, 16, w),
            (16, w),
            (16, w),
            (16, w),
        ]
        return [pltpu.VMEM(s, BF16) for s in shapes]

    shape = jax.ShapeDtypeStruct
    return pl.pallas_call(
        settle_kernel,
        name="settle",
        out_shape=(
            shape((32, 1024), F32),
            shape((32, 512), F32),
            shape((32, 512), F32),
            shape((32, 1024), F32),
            shape((32, 128), F32),
            shape((2, 2, 4, 64, 512), F32),
            shape((2, 2, 4, 64, 512), F32),
            shape((2, 2, 4, 32, 1024), F32),
        ),
        in_specs=vmem(4),
        out_specs=vmem(8),
        scratch_shapes=[pltpu.VMEM((2, 4, 4, 16, WIDE), BF16), pltpu.VMEM((32, WIDE), F32)]
        + sems(48)
        + scratch(CUT)
        + scratch(WIDE - CUT)
        + [pltpu.VMEM(t.shape, BF16) for t in (tg, tu, td)],
        compiler_params=params(3),
    )(grads.reshape(2, 4, 4, 32, WIDE), tg, tu, td)


def finish_kernel(*refs):
    n = len(refs) // 3
    sources, targets, stages, arrived = refs[:n], refs[n : 2 * n], refs[2 * n : 3 * n], refs[3 * n]
    fetches, writes = [], []
    for i in range(n):
        fetches.append(pltpu.make_async_copy(sources[i], stages[i], arrived.at[i]))
        writes.append(pltpu.make_async_copy(stages[i], targets[i], arrived.at[n + i]))
        fetches[i].start()
    for i in range(n):
        fetches[i].wait()
        writes[i].start()
    for write in writes:
        write.wait()


def finish(*arrays):
    n = len(arrays)
    return pl.pallas_call(
        finish_kernel,
        name="finish",
        out_shape=tuple(jax.ShapeDtypeStruct(a.shape, a.dtype) for a in arrays),
        in_specs=anywhere(n),
        out_specs=tuple(anywhere(n)),
        scratch_shapes=[pltpu.VMEM(a.shape, a.dtype) for a in arrays]
        + [pltpu.SemaphoreType.DMA((2 * n,))],
        compiler_params=params(limit=60),
    )(*arrays)


def experts_kernel(
    h_all, g_all, pos, gates, wg, wu, wd,
    qy, dh, dg, gg, gu, gd,
    hg, xs, gs, dys, dhs, ms, das, dbs, gcol, dcol, qg, gg_part, gu_part, local_sems, send_sems, recv_sems, *scratch,
):
    e = pl.program_id(0)
    me = Place()
    partners = (me.right(), me.left(), me.cross())
    first = me.high * 16 + me.x * 4
    n_seqs = 16
    rows = n_seqs * CAP
    places = lax.broadcasted_iota(jnp.int32, (CAP, LENGTH), 0).astype(F32)

    def row_of(table, member, part, k):
        return table[member, pl.ds(part * EXPERTS + first + k, 1), :]

    def slots_of(member, part):
        return pl.ds(pl.multiple_of((member * 2 + part) * CAP, CAP), CAP)

    def picks(member, part):
        chosen = [places == row_of(pos, member, part, k) for k in range(HERE)]
        return chosen, jnp.concatenate([c.astype(F32).astype(BF16) for c in chosen])

    @pl.when(e == 0)
    def _():
        loads = [
            pltpu.make_async_copy(h_all, hg.at[0], local_sems.at[0]),
            pltpu.make_async_copy(g_all, hg.at[1], local_sems.at[1]),
        ]
        for load in loads:
            load.start()
        greet(partners)
        qg[...] = jnp.zeros_like(qg)
        for load in loads:
            load.wait()

        @pl.loop(0, 8)
        def _(member):
            for part in range(2):
                chosen, pick = picks(member, part)
                here = slots_of(member, part)
                tokens = slice(part * LENGTH, (part + 1) * LENGTH)
                got = dot(pick, hg[0, member, tokens]).astype(BF16)
                for k in range(HERE):
                    xs[k, here] = got[k * CAP : (k + 1) * CAP]
                got = dot(pick, hg[1, member, tokens]).astype(BF16)
                for k in range(HERE):
                    gs[k, here] = got[k * CAP : (k + 1) * CAP]
                    weight = jnp.sum(
                        jnp.where(chosen[k], row_of(gates, member, part, k), 0.0),
                        axis=1,
                        keepdims=True,
                    )
                    gcol[k, here] = jnp.broadcast_to(weight, (CAP, LENGTH))

    @pl.loop(0, rows // 256)
    def _(r):
        here = pl.ds(pl.multiple_of(r * 256, 256), 256)
        x = xs[e, here]
        g_slot = gs[e, here].astype(F32)
        weight = gcol[e, here][:, :1]
        dy = (weight * (RESIDUAL * g_slot)).astype(BF16)
        dys[here] = dy
        a = dot(x, wg[0])
        b = dot(x, wu[0])
        sig = jax.nn.sigmoid(a)
        swish = a * sig
        m = (swish * b).astype(BF16)
        ms[here] = m
        y = dot(m, wd[0]).astype(BF16).astype(F32)
        inner = RESIDUAL * jnp.sum(g_slot * y, axis=1, keepdims=True)
        dcol[here] = jnp.broadcast_to(inner, (256, LENGTH))
        gs[e, here] = (weight * y).astype(BF16)
        dm = dot(dy, wd[0], ((1,), (1,)))
        da = (dm * b * sig * (1.0 + a * (1.0 - sig))).astype(BF16)
        db = (dm * swish).astype(BF16)
        das[e, here] = da
        dbs[e, here] = db
        dh_slot = dot(da, wg[0], ((1,), (1,))) + dot(db, wu[0], ((1,), (1,)))
        dhs[e, here] = dh_slot.astype(BF16)

    @pl.loop(0, 8)
    def _(member):
        for part in range(2):
            chosen = places == row_of(pos, member, part, e)
            total = jnp.sum(
                jnp.where(chosen, dcol[slots_of(member, part)], 0.0), axis=0, keepdims=True
            )
            qg[member, pl.ds(part * EXPERTS + first + e, 1), :] = total

    @pl.loop(0, FE // 256)
    def _(r):
        here = pl.ds(pl.multiple_of(r * 256, 256), 256)
        gd[0, here] = dot(ms[:, here], dys[...], ((0,), (0,))).astype(BF16)

    @pl.when(e == HERE - 1)
    def _():
        def combine(source, where, part):
            @pl.loop(0, 8)
            def _(member):
                _, pick = picks(member, part)
                here = slots_of(member, part)
                stack = jnp.concatenate([source[k, here] for k in range(HERE)])
                hg[where, member, part * LENGTH : (part + 1) * LENGTH] = dot(
                    pick, stack, ((0,), (0,))
                ).astype(BF16)

        lines = Lines(send_sems, recv_sems)
        sums = [
            group_scatter(lines, me, hg.at[0], dh, 0, LENGTH, *scratch[12:24]),
            group_scatter(lines, me, hg.at[0], dh, LENGTH, LENGTH, *scratch[24:36]),
            group_scatter(lines, me, qg, dg, 0, 2 * EXPERTS, *scratch[0:12]),
        ]
        for part in range(2):
            combine(dhs, 0, part)
            step(sums[part])
        step(sums[2])
        for part in range(2):
            combine(gs, 1, part)
        keep = pltpu.make_async_copy(hg.at[1], qy, local_sems.at[0])
        keep.start()
        for k in range(HERE):
            slot = k % 2
            copies = (
                pltpu.make_async_copy(gg_part.at[slot], gg.at[k], local_sems.at[1 + slot]),
                pltpu.make_async_copy(gu_part.at[slot], gu.at[k], local_sems.at[3 + slot]),
            )
            if k >= 2:
                for copy in copies:
                    copy.wait()

            @pl.loop(0, D // 256)
            def _(r, k=k, slot=slot):
                here = pl.ds(pl.multiple_of(r * 256, 256), 256)
                x = xs[k, :, here]
                gg_part[slot, here] = dot(x, das[k], ((0,), (0,))).astype(BF16)
                gu_part[slot, here] = dot(x, dbs[k], ((0,), (0,))).astype(BF16)

            for copy in copies:
                copy.start()
            step(*((), sums, sums[:1], sums[1:])[k])
        drive(*sums)
        for slot in range(2):
            pltpu.make_async_copy(gg_part.at[slot], gg.at[2 + slot], local_sems.at[1 + slot]).wait()
            pltpu.make_async_copy(gu_part.at[slot], gu.at[2 + slot], local_sems.at[3 + slot]).wait()
        keep.wait()
        lines.drain()


def experts(h, g, pos, gates, wg, wu, wd):
    rows = 16 * CAP
    shape = jax.ShapeDtypeStruct
    whole = pl.BlockSpec(memory_space=pltpu.VMEM)

    def per_expert(a, b):
        return pl.BlockSpec((1, a, b), lambda e: (e, 0, 0))

    return pl.pallas_call(
        experts_kernel,
        name="experts",
        grid=(HERE,),
        out_shape=(
            shape(h.shape, BF16),
            shape(h.shape[1:], F32),
            shape(gates.shape[1:], F32),
            shape((HERE, D, FE), BF16),
            shape((HERE, D, FE), BF16),
            shape((HERE, FE, D), BF16),
        ),
        in_specs=anywhere(2)
        + [whole] * 2
        + [per_expert(D, FE), per_expert(D, FE), per_expert(FE, D)],
        out_specs=anywhere(1) + [whole] * 2 + anywhere(2) + [per_expert(FE, D)],
        scratch_shapes=[
            pltpu.VMEM((2,) + h.shape, BF16),
            pltpu.VMEM((HERE, rows, D), BF16),
            pltpu.VMEM((HERE, rows, D), BF16),
            pltpu.VMEM((rows, D), BF16),
            pltpu.VMEM((HERE, rows, D), BF16),
            pltpu.VMEM((rows, FE), BF16),
            pltpu.VMEM((HERE, rows, FE), BF16),
            pltpu.VMEM((HERE, rows, FE), BF16),
            pltpu.VMEM((HERE, rows, LENGTH), F32),
            pltpu.VMEM((rows, LENGTH), F32),
            pltpu.VMEM(gates.shape, F32),
            pltpu.VMEM((2, D, FE), BF16),
            pltpu.VMEM((2, D, FE), BF16),
            pltpu.SemaphoreType.DMA((5,)),
        ]
        + sems(36)
        + scatter_scratch(gates.shape[1], gates.shape[2], F32)
        + scatter_scratch(LENGTH, D, BF16)
        + scatter_scratch(LENGTH, D, BF16),
        compiler_params=params(1, 60),
    )(h, g, pos, gates, wg, wu, wd)


def on_device(
    tokens,
    segments,
    routes,
    cotangent,
    attn_gain,
    moe_gain,
    w_query,
    w_key,
    w_value,
    w_output,
    w_router,
    w_gate,
    w_up,
    w_down,
):
    micro = tokens.shape[0]
    rows = micro * LENGTH
    inputs = tokens.reshape(rows, D)
    upstream = cotangent.reshape(rows, D)
    dense, gbuf, sbuf, wgb, wub, wdb, hbuf, gatebuf, q, k, v, p, o, y1, gates, cos, sin = front(
        inputs,
        segments[:, 0],
        routes.reshape(rows, TOPK),
        w_query,
        w_key,
        w_value,
        w_output,
        w_router,
        jnp.stack([attn_gain, moe_gain]).astype(F32),
        upstream,
        w_gate[0],
        w_up[0],
        w_down[0],
    )

    qy, dh, gate_grad, gg, gu, gd = experts(hbuf, gbuf, sbuf, gatebuf, wgb, wub, wdb)
    grads, grad_tokens, result, tg, tu, td = retreat(
        inputs, cos, sin, gates, dense.reshape(D, WIDE), upstream, y1, q, k, v, p, o, dh, gate_grad,
        qy, gg, gu, gd,
    )
    gq, gk, gv, go, gsmall, grad_gate, grad_up, grad_down, grad_tokens, result = finish(
        *settle(grads, tg, tu, td), grad_tokens, result
    )
    return (
        result.reshape(micro, 1, LENGTH, D),
        grad_tokens.reshape(micro, 1, LENGTH, D),
        gsmall[:, 32],
        gsmall[:, 33],
        gq,
        gk,
        gv,
        go,
        gsmall[:, :32],
        grad_gate.reshape(1, D, FE),
        grad_up.reshape(1, D, FE),
        grad_down.reshape(1, FE, D),
    )


def solution(mesh):
    sequences = P(None, ("rep", "fsdp"), None, None)
    placed = (
        sequences,
        P(None, ("rep", "fsdp"), None),
        sequences,
        sequences,
        P("fsdp"),
        P("fsdp"),
        P("fsdp", None),
        P("fsdp", None),
        P("fsdp", None),
        P("fsdp", None),
        P("fsdp", None),
        P("fsdp", None, None),
        P("fsdp", None, None),
        P("fsdp", None, None),
    )
    return jax.shard_map(
        on_device,
        mesh=mesh,
        in_specs=placed,
        out_specs=(sequences, sequences) + placed[4:],
        check_vma=False,
    )
```

```python
import functools
import math

import jax
import jax.numpy as jnp
from jax import lax
from jax.experimental import pallas as pl
from jax.experimental.pallas import tpu as pltpu
from jax.sharding import PartitionSpec as P

D = 1024
HEADS = 16
KV_HEADS = 8
HEAD_DIM = 64
EXPERTS = 32
FE = 512
TOPK = 8
CAP = 48
LENGTH = 128

EPS = 1e-06
RESIDUAL = 0.22
ATT_SCALE = 0.015625
ROPE_BASE = 10000.0
NEG = -1000000000.0

MESH = pl.DeviceIdType.MESH
F32 = jnp.float32
BF16 = jnp.bfloat16
WIDE = 3200
CUT = 1664
HERE = 4


class Place:
    def __init__(self):
        rep = lax.axis_index("rep")
        flat = lax.axis_index("fsdp")
        self.core = lax.rem(rep, 2)
        self.low = lax.div(rep, 2)
        self.high = lax.div(flat, 16)
        self.x = lax.rem(lax.div(flat, 4), 4)
        self.z = lax.rem(flat, 4)

    def at(self, low=None, core=None, high=None, x=None, z=None):
        low = self.low if low is None else low
        core = self.core if core is None else core
        high = self.high if high is None else high
        x = self.x if x is None else x
        z = self.z if z is None else z
        return (low * 2 + core, high * 16 + x * 4 + z)

    def right(self):
        return self.at(x=lax.rem(self.x + 1, 4))

    def left(self):
        return self.at(x=lax.rem(self.x + 3, 4))

    def above(self):
        return self.at(z=lax.rem(self.z + 1, 4))

    def below(self):
        return self.at(z=lax.rem(self.z + 3, 4))

    def cross(self):
        return self.at(low=1 - self.low, high=1 - self.high)

    def twin(self):
        return self.at(low=1 - self.low)

    def sibling(self):
        return self.at(core=1 - self.core)


class Lines:
    def __init__(self, send_sems, recv_sems):
        self.send_sems, self.recv_sems, self.copies, self.left = send_sems, recv_sems, [], 0

    def send(self, src, dst, device):
        i = len(self.copies)
        assert i < self.send_sems.shape[0]
        copy = pltpu.make_async_remote_copy(
            src_ref=src,
            dst_ref=dst,
            send_sem=self.send_sems.at[i],
            recv_sem=self.recv_sems.at[i],
            device_id=device,
            device_id_type=MESH,
        )
        copy.start()
        self.copies.append(copy)
        return copy

    def drain(self):
        for copy in self.copies[self.left :]:
            copy.wait_send()
        self.left = len(self.copies)


def step(*chains):
    for chain in chains:
        next(chain, None)


def greet(partners):
    barrier = pltpu.get_barrier_semaphore()
    for partner in partners:
        pl.semaphore_signal(barrier, inc=1, device_id=partner, device_id_type=MESH)
    pl.semaphore_wait(barrier, len(partners))


def drive(*chains):
    live = list(chains)
    while live:
        for chain in list(live):
            try:
                next(chain)
            except StopIteration:
                live.remove(chain)


def ring_gather(lines, source, slot, half, pos, right, left, spread=None):
    ahead, behind, far = lax.rem(pos + 1, 4), lax.rem(pos + 3, 4), lax.rem(pos + 2, 4)
    spread = spread or (lambda p: None)
    a = lines.send(source, slot(pos), right)
    b = lines.send(source, slot(pos), left)
    yield
    a.wait_recv()
    c = lines.send(half(behind, 0), half(behind, 0), right)
    b.wait_recv()
    d = lines.send(half(ahead, 1), half(ahead, 1), left)
    spread(behind)
    spread(ahead)
    yield
    c.wait_recv()
    d.wait_recv()
    spread(far)


def group_gather(lines, me, source, buf, start=0, rows=None, last=True):
    rows = rows or buf.shape[1]
    ahead, behind, far = lax.rem(me.x + 1, 4), lax.rem(me.x + 3, 4), lax.rem(me.x + 2, 4)
    right, left, cross = me.right(), me.left(), me.cross()
    base, other = me.high * 4, (1 - me.high) * 4

    def slot(k):
        return buf.at[k, pl.ds(start, rows)]

    def half(k, h):
        return buf.at[k, pl.ds(start + h * rows // 2, rows // 2)]

    e = lines.send(source, slot(base + me.x), cross)
    a = lines.send(source, slot(base + me.x), right)
    b = lines.send(source, slot(base + me.x), left)
    yield
    a.wait_recv()
    c = lines.send(half(base + behind, 0), half(base + behind, 0), right)
    b.wait_recv()
    d = lines.send(half(base + ahead, 1), half(base + ahead, 1), left)
    e.wait_recv()
    f = lines.send(slot(other + me.x), slot(other + me.x), right)
    g = lines.send(slot(other + me.x), slot(other + me.x), left)
    yield
    c.wait_recv()
    d.wait_recv()
    if last:
        h = lines.send(slot(base + far), slot(base + far), cross)
        yield
        h.wait_recv()
    f.wait_recv()
    g.wait_recv()


def weight_chain(lines, me, shared, source, buf):
    half_rows = source.shape[0] // 2
    quarter = half_rows // 2
    start = me.core * half_rows
    mine = pl.ds(pl.multiple_of(start, half_rows), half_rows)

    def slot(p):
        return buf.at[p, mine]

    def half(p, k):
        return buf.at[p, pl.ds(pl.multiple_of(start + k * quarter, quarter), quarter)]

    def spread(p):
        shared.append(lines.send(slot(p), slot(p), me.sibling()))

    yield from ring_gather(
        lines, source.at[mine], slot, half, me.z, me.above(), me.below(), spread=spread
    )


def group_scatter(lines, me, q, out, start, rows, by, tl, tr, hl, hr, fl, fr, fy):
    mid = rows // 2
    step_rows = min(32, mid)
    ahead, behind, far = lax.rem(me.x + 1, 4), lax.rem(me.x + 3, 4), lax.rem(me.x + 2, 4)
    right, left, cross = me.right(), me.left(), me.cross()
    base, other = me.high * 4, (1 - me.high) * 4
    first, second = pl.ds(0, mid), pl.ds(mid, mid)

    def whole(k):
        return q.at[k, pl.ds(start, rows)]

    def part(k, h):
        return q.at[k, pl.ds(start + h * mid, mid)]

    def each(count, offset, body):
        @pl.loop(0, count // step_rows)
        def _(i):
            here = pl.multiple_of(i * step_rows, step_rows)
            there = pl.multiple_of(start + offset + i * step_rows, step_rows)
            body(pl.ds(here, step_rows), pl.ds(there, step_rows))

    e = lines.send(whole(other + far), by, cross)
    g1 = lines.send(whole(other + ahead), tl, right)
    g2 = lines.send(whole(other + behind), tr, left)
    i1 = lines.send(part(base + ahead, 1), fl.at[second], right)
    i2 = lines.send(part(base + behind, 0), fr.at[first], left)
    yield
    e.wait_recv()

    def far_sum(here, there):
        by[here] = q[base + far, there] + by[here]

    each(rows, 0, far_sum)
    j1 = lines.send(by.at[first], hl, right)
    j2 = lines.send(by.at[second], hr, left)
    yield
    g1.wait_recv()
    g2.wait_recv()

    def partner_sum(here, there):
        total = q[other + me.x, there].astype(F32) + tl[here].astype(F32) + tr[here].astype(F32)
        tl[here] = total.astype(tl.dtype)

    each(rows, 0, partner_sum)
    k = lines.send(tl, fy, cross)
    yield
    j1.wait_recv()

    def right_sum(here, there):
        hl[here] = q[base + ahead, there] + hl[here]

    each(mid, 0, right_sum)
    l1 = lines.send(hl, fl.at[first], right)
    j2.wait_recv()

    def left_sum(here, there):
        hr[here] = q[base + behind, there] + hr[here]

    each(mid, mid, left_sum)
    l2 = lines.send(hr, fr.at[second], left)
    yield
    for copy in (i1, i2, l1, l2, k):
        copy.wait_recv()

    def total(here, there):
        out[there] = (
            q[base + me.x, there].astype(F32)
            + fl[here].astype(F32)
            + fr[here].astype(F32)
            + fy[here].astype(F32)
        )

    each(rows, 0, total)


def ring_scatter(lines, arr, pos, right, left, hl, hr, fl, fr, store):
    n = arr.shape[2]
    ahead, behind, far = lax.rem(pos + 1, 4), lax.rem(pos + 3, 4), lax.rem(pos + 2, 4)
    a = lines.send(arr.at[far, 0], hl, right)
    b = lines.send(arr.at[far, 1], hr, left)
    c = lines.send(arr.at[ahead, 1], fl.at[1], right)
    d = lines.send(arr.at[behind, 0], fr.at[0], left)
    yield
    a.wait_recv()

    @pl.loop(0, n)
    def _(j):
        arr[ahead, 0, j] = arr[ahead, 0, j] + hl[j]

    e = lines.send(arr.at[ahead, 0], fl.at[0], right)
    b.wait_recv()

    @pl.loop(0, n)
    def _(j):
        arr[behind, 1, j] = arr[behind, 1, j] + hr[j]

    f = lines.send(arr.at[behind, 1], fr.at[1], left)
    yield
    for copy in (c, d, e, f):
        copy.wait_recv()
    for half in range(2):

        @pl.loop(0, n)
        def _(j, half=half):
            store(
                half,
                j,
                arr[pos, half, j].astype(F32) + fl[half, j].astype(F32) + fr[half, j].astype(F32),
            )


def dot(a, b, dims=((1,), (0,))):
    return lax.dot_general(a, b, (dims, ((), ())), preferred_element_type=F32)


def lanes():
    return lax.broadcasted_iota(jnp.int32, (1, 128), 1)


def swap_halves(u):
    return jnp.where(
        lax.rem(lanes(), 64) < 32, pltpu.roll(u, 96, axis=1), pltpu.roll(u, 32, axis=1)
    )


def doubled(tile, odd):
    wide = tile.astype(F32)
    turned = pltpu.roll(wide, 64, axis=1)
    low = lanes() < 64
    return jnp.where(low, turned if odd else wide, wide if odd else turned).astype(BF16)


def stacked(pair):
    wide = pair.astype(F32)
    low = lanes() < 64
    return jnp.concatenate([jnp.where(low, wide, 0.0), jnp.where(low, 0.0, wide)]).astype(BF16)


def side_by_side(both):
    return jnp.where(lanes() < 64, both[:128], both[128:])


def folded(even, odd):
    even = even + pltpu.roll(even, 64, axis=1)
    odd = odd + pltpu.roll(odd, 64, axis=1)
    return jnp.where(lanes() < 64, even, odd)


def side(table):
    return jnp.concatenate([table[:EXPERTS], table[EXPERTS:]], axis=1)


def phases(segment):
    across = jnp.broadcast_to(segment.astype(F32), (LENGTH, LENGTH))
    down = jnp.transpose(across)
    t = lax.broadcasted_iota(jnp.int32, (LENGTH, LENGTH), 0)
    u = lax.broadcasted_iota(jnp.int32, (LENGTH, LENGTH), 1)
    keep = jnp.where((u <= t) & (across == down), 1.0, 0.0)
    offset = jnp.sum(keep, axis=1, keepdims=True) - 1.0
    step_of = lax.rem(lanes(), 32).astype(F32)
    frequency = jnp.exp(-math.log(ROPE_BASE) * 2.0 * step_of / HEAD_DIM)
    angles = offset * frequency
    sign = jnp.where(lax.rem(lanes(), 64) < 32, -1.0, 1.0)
    return jnp.cos(angles), sign * jnp.sin(angles), keep


def slot_table(route_ids):
    wide = jnp.concatenate([route_ids.astype(F32), jnp.zeros((LENGTH, 128 - TOPK), F32)], axis=1)
    by_choice = jnp.transpose(wide)
    ids = lax.broadcasted_iota(jnp.int32, (EXPERTS, LENGTH), 0).astype(F32)
    named = jnp.zeros((EXPERTS, LENGTH), F32)
    for j in range(TOPK):
        named = jnp.where(by_choice[j : j + 1] == ids, 1.0, named)
    t = lax.broadcasted_iota(jnp.int32, (LENGTH, LENGTH), 0)
    u = lax.broadcasted_iota(jnp.int32, (LENGTH, LENGTH), 1)
    before = jnp.where(t < u, 1.0, 0.0).astype(BF16)
    return jnp.where(named > 0.0, dot(named.astype(BF16), before), -1.0)


def small_shard(router, gains):
    wide = jnp.concatenate([router.astype(F32), jnp.zeros((32, 128 - EXPERTS), F32)], axis=1)
    row = lax.broadcasted_iota(jnp.int32, (32, 32), 0)
    lane = lax.broadcasted_iota(jnp.int32, (32, 32), 1)
    for i in range(2):
        across = jnp.broadcast_to(gains[i : i + 1].astype(F32), (32, 32))
        column = jnp.sum(jnp.where(row == lane, across, 0.0), axis=1, keepdims=True)
        wide = jnp.where(lanes() == EXPERTS + i, column, wide)
    return wide.astype(BF16)


def norm_scale(values):
    return lax.rsqrt(jnp.mean(values * values, axis=1, keepdims=True) + EPS)


def gain_rows(small):
    row = lax.broadcasted_iota(jnp.int32, (8, 128), 0)
    lane = lax.broadcasted_iota(jnp.int32, (8, 128), 1)
    pick = (lane == row + EXPERTS).astype(F32).astype(BF16)
    rows = dot(pick, small, ((1,), (1,)))
    return rows[0:1], rows[1:2]


def column_sums(values, column):
    rows = values.shape[0]
    pick = (lax.broadcasted_iota(jnp.int32, (rows, 128), 1) == column).astype(F32).astype(BF16)
    upper = values.astype(BF16)
    lower = (values - upper.astype(F32)).astype(BF16)
    return dot(upper, pick, ((0,), (0,))) + dot(lower, pick, ((0,), (0,)))


def anywhere(n):
    return [pl.BlockSpec(memory_space=pl.ANY)] * n


def vmem(n):
    return [pl.BlockSpec(memory_space=pltpu.VMEM)] * n


def sems(n):
    return [pltpu.SemaphoreType.DMA((n,)), pltpu.SemaphoreType.DMA((n,))]


def params(number=None, limit=56):
    if number is None:
        return pltpu.CompilerParams(vmem_limit_bytes=limit << 20)
    return pltpu.CompilerParams(
        collective_id=number, has_side_effects=True, vmem_limit_bytes=limit << 20
    )


def front_kernel(
    tokens, segments, routes, wq_own, wk_own, wv_own, wo_own, wr_own, gains, g, wg, wu,
    dense, gbuf, sbuf, wgb, wub, h2, q, k, v, p, o, y1, gates, cos, sin,
    dn, h, keep, slots, send_sems, recv_sems, local_sems,
):
    me = Place()
    right, left, above, below = me.right(), me.left(), me.above(), me.below()
    cross, sibling = me.cross(), me.sibling()
    rows = pl.ds(pl.multiple_of(me.core * 16, 16), 16)
    own = me.high * 4 + me.x
    local = [
        pltpu.make_async_copy(g, gbuf.at[own], local_sems.at[1]),
        pltpu.make_async_copy(wg, wgb.at[me.z], local_sems.at[3]),
        pltpu.make_async_copy(wu, wub.at[me.z], local_sems.at[4]),
    ]
    for copy in local:
        copy.start()
    shard = dn.at[me.high, me.x, me.z]
    shard[:, 0:1024] = wq_own[...]
    shard[:, 1024:1536] = wk_own[...]
    shard[:, 1536:2048] = wv_own[...]
    shard[:, 2048:3072] = wo_own[...]
    shard[:, 3072:3200] = small_shard(wr_own[...], gains[...])
    greet((right, left, above, below, cross, sibling))
    lines = Lines(send_sems, recv_sems)
    shared = []

    def dense_chain(columns, x_first):
        on_x, on_z = (me.x, right, left), (me.z, above, below)
        (pos, up, down), (pos2, up2, down2) = (on_x, on_z) if x_first else (on_z, on_x)
        ahead, behind, far = lax.rem(pos + 1, 4), lax.rem(pos + 3, 4), lax.rem(pos + 2, 4)

        def piece(one, two, k=None):
            x, z = (one, two) if x_first else (two, one)
            return dn.at[slice(None) if k is None else k, x, z, rows, columns]

        def unit(one):
            def spread(two):
                shared.append(lines.send(piece(one, two), piece(one, two), sibling))

            def slot(two):
                return piece(one, two)

            def half(two, k):
                return piece(one, two, k)

            chain = ring_gather(lines, slot(pos2), slot, half, pos2, up2, down2, spread=spread)
            next(chain)
            spread(pos2)
            return chain

        mine = piece(pos, pos2)
        a = lines.send(mine, mine, up)
        b = lines.send(mine, mine, down)
        units = [unit(pos)]
        yield
        a.wait_recv()
        c = lines.send(piece(behind, pos2, 0), piece(behind, pos2, 0), up)
        units.append(unit(behind))
        b.wait_recv()
        d = lines.send(piece(ahead, pos2, 1), piece(ahead, pos2, 1), down)
        units.append(unit(ahead))
        yield
        step(units[0])
        yield
        c.wait_recv()
        d.wait_recv()
        units.append(unit(far))
        yield
        step(units[1], units[2])
        yield
        step(units[0], units[3])
        yield
        step(*units[1:])
        step(*units)

    swap = lines.send(shard.at[rows], shard.at[rows], cross)
    for part in range(2):
        here = slice(part * LENGTH, (part + 1) * LENGTH)
        cos[here], sin[here], keep[part] = phases(segments[part : part + 1, :])
        slots[part * EXPERTS : (part + 1) * EXPERTS] = slot_table(routes[here, :])
    local.append(pltpu.make_async_copy(slots, sbuf.at[own], local_sems.at[2]))
    local[-1].start()
    swap.wait_recv()
    gs = group_gather(lines, me, g, gbuf, last=False)
    ss = group_gather(lines, me, slots, sbuf)
    w1 = weight_chain(lines, me, shared, wg, wgb)
    w2 = weight_chain(lines, me, shared, wu, wub)
    dense_a, dense_b = dense_chain(pl.ds(0, CUT), False), dense_chain(pl.ds(CUT, WIDE - CUT), True)
    step(dense_a, dense_b)
    step(gs, ss, w1)
    drive(dense_a, dense_b)
    for copy in shared:
        copy.wait_recv()
    del shared[:]
    step(gs, ss, w2)
    keeping = pltpu.make_async_copy(dn, dense, local_sems.at[6])
    keeping.start()

    def weight(start, size):
        return dn[:, :, :, :, start : start + size].reshape(D, size)

    small = weight(3072, 128)
    gain_one, gain_two = gain_rows(small)
    x = tokens[...].astype(F32)
    h[...] = (x * norm_scale(x) * gain_one).astype(BF16)
    for piece in range(4):
        raw = dot(h[...], weight(piece * 256, 256))
        for t in range(2):
            u = raw[:, t * 128 : t * 128 + 128]
            q[:, piece * 256 + t * 128 : piece * 256 + t * 128 + 128] = (
                u * cos[...] + swap_halves(u) * sin[...]
            ).astype(BF16)
    for piece in range(2):
        raw = dot(h[...], weight(1024 + piece * 256, 256))
        for t in range(2):
            u = raw[:, t * 128 : t * 128 + 128]
            k[:, piece * 256 + t * 128 : piece * 256 + t * 128 + 128] = (
                u * cos[...] + swap_halves(u) * sin[...]
            ).astype(BF16)
    v[...] = dot(h[...], weight(1536, 512)).astype(BF16)
    step(w1)

    def attend(i):
        s, m = lax.div(i, 4), lax.rem(i, 4)
        here = pl.ds(pl.multiple_of(s * 128, 128), 128)
        column = pl.ds(pl.multiple_of(m * 128, 128), 128)
        seen = keep[s]
        seen = jnp.concatenate([seen, seen]) > 0.0
        k_tile, v_tile = k[here, column], v[here, column]
        for odd in range(2):
            q_column = pl.ds(pl.multiple_of(m * 256 + odd * 128, 128), 128)
            scores = dot(stacked(q[here, q_column]), doubled(k_tile, odd), ((1,), (1,))) * ATT_SCALE
            scores = jnp.where(seen, scores, NEG)
            raised = jnp.exp(scores - jnp.max(scores, axis=1, keepdims=True))
            probs = raised / jnp.sum(raised, axis=1, keepdims=True)
            p[i, odd] = probs
            both = dot(probs.astype(BF16), doubled(v_tile, odd))
            o[here, q_column] = side_by_side(both).astype(BF16)

    for part in range(2):

        @pl.loop(part * 4, part * 4 + 4)
        def _(i):
            attend(i)

        if part == 0:
            step(w2, ss)

    middle = tokens[...].astype(F32) + RESIDUAL * dot(o[...], weight(2048, 1024))
    y1[...] = middle
    h2[...] = (middle * norm_scale(middle) * gain_two).astype(BF16)
    logits = dot(small, h2[...], ((0,), (1,)))[:EXPERTS]
    named = side(slots) >= 0.0
    top = jnp.max(jnp.where(named, logits, -jnp.inf), axis=0, keepdims=True)
    raised = jnp.where(named, jnp.exp(jnp.where(named, logits - top, 0.0)), 0.0)
    raised = raised / jnp.sum(raised, axis=0, keepdims=True)
    gates[:EXPERTS] = raised[:, :LENGTH]
    gates[EXPERTS:] = raised[:, LENGTH:]
    drive(ss, w1, w2, gs)
    for copy in shared:
        copy.wait_recv()
    for copy in local + [keeping]:
        copy.wait()
    lines.drain()


def front(tokens, segments, routes, wq, wk, wv, wo, wr, gains, g, wg, wu):
    shape = jax.ShapeDtypeStruct
    rows = tokens.shape[0]
    slots = shape((2 * EXPERTS, LENGTH), F32)
    return pl.pallas_call(
        front_kernel,
        name="front",
        out_shape=(
            shape((2, 4, 4, 32, WIDE), BF16),
            shape((8,) + g.shape, BF16),
            shape((8,) + slots.shape, F32),
            shape((4,) + wg.shape, BF16),
            shape((4,) + wu.shape, BF16),
            shape((rows, D), BF16),
            shape((rows, 1024), BF16),
            shape((rows, 512), BF16),
            shape((rows, 512), BF16),
            shape((8, 2, 256, 128), F32),
            shape((rows, 1024), BF16),
            shape((rows, D), F32),
            shape(slots.shape, F32),
            shape((rows, 128), F32),
            shape((rows, 128), F32),
        ),
        in_specs=vmem(12),
        out_specs=anywhere(5) + vmem(10),
        scratch_shapes=[
            pltpu.VMEM((2, 4, 4, 32, WIDE), BF16),
            pltpu.VMEM((rows, D), BF16),
            pltpu.VMEM((2, LENGTH, LENGTH), F32),
            pltpu.VMEM(slots.shape, F32),
        ]
        + sems(140)
        + [pltpu.SemaphoreType.DMA((7,))],
        compiler_params=params(0),
    )(tokens, segments, routes, wq, wk, wv, wo, wr, gains, g, wg, wu)


def scatter_scratch(rows, columns, dtype):
    full = pltpu.VMEM((rows, columns), dtype)
    half = pltpu.VMEM((rows // 2, columns), dtype)
    return [full] * 3 + [half] * 2 + [full] * 3


def retreat_kernel(
    tokens, cos, sin, gates, dense, g, y1, q, k, v, p, o, dh, dg, qy, gg, gu, gd,
    grads, got, grad_tokens, result, tg, tu, td,
    h, do, dq, dk, dv, small_grad, mixture, *scratch,
):
    me = Place()
    send_sems, recv_sems, local_sems = scratch[:3]
    above, below = me.above(), me.below()
    local = []
    for i, (grad, acc) in enumerate(((gg, scratch[4]), (gu, scratch[10]), (gd, scratch[16]))):
        local.append(pltpu.make_async_copy(grad.at[0], acc, local_sems.at[i]))
        local[-1].start()
    for i, (grad, rc) in enumerate(((gg, scratch[3]), (gu, scratch[9]), (gd, scratch[15]))):
        local.append(pltpu.make_async_copy(grad.at[1], rc, local_sems.at[3 + i]))
        local[-1].start()
    greet((me.right(), me.left(), me.cross(), above, below, me.sibling()))
    lines = Lines(send_sems, recv_sems)

    theirs = pl.ds(pl.multiple_of((1 - me.core) * 16, 16), 16)
    handed = []

    def keep_rows(t, columns, value):
        shards = value.astype(BF16).reshape(2, 4, 32, value.shape[1])
        grads[t // 2, (t % 2) * 2 : (t % 2) * 2 + 2, :, :, columns] = shards

    def hand(columns):
        handed.append(
            lines.send(
                grads.at[:, :, :, theirs, columns], got.at[:, :, :, :, columns], me.sibling()
            )
        )

    def chain(tot, mine, theirs_in, rc, acc, hl, hr, fl, fr):
        mine.wait()
        theirs_in.wait()

        @pl.loop(0, 32)
        def _(i):
            a, b, j = lax.div(i, 8), lax.rem(lax.div(i, 4), 2), lax.rem(i, 4)
            acc[a, b, j] = acc[a, b, j] + rc[a, b, j]

        def store(b, j, value):
            tot[b, j] = value.astype(BF16)

        yield from ring_scatter(lines, acc, me.z, above, below, hl, hr, fl, fr, store)

    e1 = chain(tg, local[0], local[3], *scratch[3:9])
    e2 = chain(tu, local[1], local[4], *scratch[9:15])
    e3 = chain(td, local[2], local[5], *scratch[15:21])
    ys = group_scatter(lines, me, qy, mixture, 0, 2 * LENGTH, *scratch[21:29])
    step(e1, ys)

    small = dense[:, 3072:3200]
    gain_one, gain_two = gain_rows(small)
    x = tokens[...].astype(F32)
    h[...] = (x * norm_scale(x) * gain_one).astype(BF16)
    middle = y1[...]
    scale = norm_scale(middle)
    normed = middle * scale
    routed = (normed * gain_two).astype(BF16)
    weights, grad = side(gates), side(dg)
    choice = weights * (grad - jnp.sum(weights * grad, axis=0, keepdims=True))
    by_token = jnp.transpose(
        jnp.concatenate([choice, jnp.zeros((128 - EXPERTS, choice.shape[1]), F32)])
    ).astype(BF16)
    dh2 = dh[...] + dot(by_token, small, ((1,), (1,)))
    small_grad[...] = dot(routed, by_token, ((0,), (0,))) + column_sums(dh2 * normed, EXPERTS + 1)
    dn = dh2 * gain_two
    dy = g[...].astype(F32) + scale * (dn - normed * jnp.mean(dn * normed, axis=1, keepdims=True))
    grad_tokens[...] = dy
    dz = (RESIDUAL * dy).astype(BF16)
    step(e2)
    for t in range(4):
        here = slice(t * 256, t * 256 + 256)
        keep_rows(t, pl.ds(2048, 1024), dot(o[:, here], dz, ((0,), (0,))))
    hand(pl.ds(2048, 1024))
    do[...] = dot(dz, dense[:, 2048:3072], ((1,), (1,))).astype(BF16)
    step(e1, ys)

    def attend_back(i):
        s, m = lax.div(i, 4), lax.rem(i, 4)
        here = pl.ds(pl.multiple_of(s * 128, 128), 128)
        column = pl.ds(pl.multiple_of(m * 128, 128), 128)
        cos_s, sin_s = cos[here], sin[here]
        k_tile, v_tile = k[here, column], v[here, column]
        dk_both, dv_both = [], []
        for odd in range(2):
            q_column = pl.ds(pl.multiple_of(m * 256 + odd * 128, 128), 128)
            q_two, do_two = stacked(q[here, q_column]), stacked(do[here, q_column])
            probs = p[i, odd]
            dp = dot(do_two, doubled(v_tile, odd), ((1,), (1,)))
            inner = jnp.sum(probs * dp, axis=1, keepdims=True)
            ds = (probs * (dp - inner)).astype(BF16)
            dv_both.append(dot(probs.astype(BF16), do_two, ((0,), (0,))))
            dk_both.append(dot(ds, q_two, ((0,), (0,))) * ATT_SCALE)
            u = side_by_side(dot(ds, doubled(k_tile, odd))) * ATT_SCALE
            dq[here, q_column] = (u * cos_s - swap_halves(u) * sin_s).astype(BF16)
        u = folded(*dk_both)
        dk[here, column] = (u * cos_s - swap_halves(u) * sin_s).astype(BF16)
        dv[here, column] = folded(*dv_both).astype(BF16)

    for part in range(4):

        @pl.loop(part * 2, part * 2 + 2)
        def _(i):
            attend_back(i)

        step(*((e3,), (ys, e2), (e1,), (ys, e3))[part])

    for t in range(4):
        here = slice(t * 256, t * 256 + 256)
        keep_rows(t, pl.ds(0, 1024), dot(h[:, here], dq[...], ((0,), (0,))))
        keep_rows(t, pl.ds(1024, 512), dot(h[:, here], dk[...], ((0,), (0,))))
        keep_rows(t, pl.ds(1536, 512), dot(h[:, here], dv[...], ((0,), (0,))))
    hand(pl.ds(0, 2048))
    dh1 = (
        dot(dq[...], dense[:, 0:1024], ((1,), (1,)))
        + dot(dk[...], dense[:, 1024:1536], ((1,), (1,)))
        + dot(dv[...], dense[:, 1536:2048], ((1,), (1,)))
    )
    step(e2, ys)
    x = tokens[...].astype(F32)
    scale = norm_scale(x)
    normed = x * scale
    small_sum = small_grad[...] + column_sums(dh1 * normed, EXPERTS)
    for t in range(4):
        keep_rows(t, pl.ds(3072, 128), small_sum[t * 256 : t * 256 + 256])
    hand(pl.ds(3072, 128))
    dn = dh1 * gain_one
    grad_tokens[...] += scale * (dn - normed * jnp.mean(dn * normed, axis=1, keepdims=True))
    drive(ys, e1, e2, e3)
    result[...] = (y1[...] + RESIDUAL * mixture[...]).astype(BF16)
    for copy in handed:
        copy.wait_recv()
    lines.drain()


def halves(r, w):
    return (2, 4, 2, 4, r, w)


def retreat(tokens, cos, sin, gates, dense, g, y1, q, k, v, p, o, dh, dg, qy, gg, gu, gd):
    def scratch(r, w):
        shapes = [(4, 2, 4, r, w)] * 2 + [(4, r, w)] * 2 + [(2, 4, r, w)] * 2
        return [pltpu.VMEM(s, BF16) for s in shapes]

    shape = jax.ShapeDtypeStruct
    rows = tokens.shape[0]
    return pl.pallas_call(
        retreat_kernel,
        name="retreat",
        out_shape=(
            shape((2, 4, 4, 32, WIDE), BF16),
            shape((2, 4, 4, 16, WIDE), BF16),
            shape((rows, D), F32),
            shape((rows, D), BF16),
            shape((2, 4, 64, 512), BF16),
            shape((2, 4, 64, 512), BF16),
            shape((2, 4, 32, 1024), BF16),
        ),
        in_specs=vmem(15) + anywhere(3),
        out_specs=vmem(1) + anywhere(1) + vmem(5),
        scratch_shapes=[
            pltpu.VMEM((rows, D), BF16),
            pltpu.VMEM((rows, 1024), BF16),
            pltpu.VMEM((rows, 1024), BF16),
            pltpu.VMEM((rows, 512), BF16),
            pltpu.VMEM((rows, 512), BF16),
            pltpu.VMEM((D, 128), F32),
            pltpu.VMEM((rows, D), F32),
        ]
        + sems(40)
        + [pltpu.SemaphoreType.DMA((6,))]
        + scratch(64, 512)
        + scratch(64, 512)
        + scratch(32, 1024)
        + scatter_scratch(rows, D, BF16),
        compiler_params=params(2, 60),
    )(
        tokens, cos, sin, gates, dense, g, y1, q, k, v, p, o, dh, dg, qy,
        gg.reshape(halves(64, 512)), gu.reshape(halves(64, 512)), gd.reshape(halves(32, 1024)),
    )


def settle_kernel(grads, rc, tg, tu, td, oq, ok, ov, oo, osmall, og, ou, od, out, *scratch):
    me = Place()
    send_sems, recv_sems = scratch[:2]
    right, left, above, below = me.right(), me.left(), me.above(), me.below()
    cross, twin, sibling = me.cross(), me.twin(), me.sibling()
    greet((right, left, above, below, cross, twin, sibling))
    lines = Lines(send_sems, recv_sems)
    mine = pl.ds(pl.multiple_of(me.core * 16, 16), 16)
    theirs = pl.ds(pl.multiple_of((1 - me.core) * 16, 16), 16)

    def chain(columns, x_first, acc, second, hl, hr, fl, fr, hl2, hr2, fl2, fr2, r2, ry, r3, yb):
        @pl.loop(0, 32)
        def _(i):
            k, x, z = lax.div(i, 16), lax.rem(lax.div(i, 4), 4), lax.rem(i, 4)
            value = grads[k, x, z, mine, columns] + rc[k, x, z, :, columns]
            if x_first:
                acc[x, k, z] = value
            else:
                acc[z, k, x] = value

        yield

        def store(k, j, value):
            second[j, k, 0] = value.astype(BF16)

        def store_last(k, j, value):
            r2[k] = value.astype(BF16)

        on_x, on_z = (me.x, right, left), (me.z, above, below)
        one, two = (on_x, on_z) if x_first else (on_z, on_x)
        yield from ring_scatter(lines, acc, *one, hl, hr, fl, fr, store)
        yield from ring_scatter(lines, second, *two, hl2, hr2, fl2, fr2, store_last)
        a = lines.send(r2.at[1 - me.high], ry, cross)
        yield
        a.wait_recv()
        r3[...] = (r2[me.high].astype(F32) + ry[...].astype(F32)).astype(BF16)
        b = lines.send(r3, yb, twin)
        yield
        b.wait_recv()
        out[mine, columns] = r3[...].astype(F32) + yb[...].astype(F32)
        c = lines.send(out.at[mine, columns], out.at[mine, columns], sibling)
        yield
        c.wait_recv()

    def swapped(tot, whole, other):
        a = lines.send(tot, other, twin)
        yield
        a.wait_recv()
        for k in range(2):

            @pl.loop(0, 4)
            def _(j, k=k):
                whole[me.core, k, j] = tot[k, j].astype(F32) + other[k, j].astype(F32)

        b = lines.send(whole.at[me.core], whole.at[me.core], sibling)
        yield
        b.wait_recv()

    others = [swapped(t, w, s) for t, w, s in zip((tg, tu, td), (og, ou, od), scratch[30:33])]
    step(*others)
    one = chain(pl.ds(0, CUT), True, *scratch[2:16])
    two = chain(pl.ds(CUT, WIDE - CUT), False, *scratch[16:30])
    step(one)
    step(one)
    step(two)
    step(two)
    drive(one, two)
    drive(*others)
    start = 0
    for part in (oq, ok, ov, oo, osmall):
        part[...] = out[:, start : start + part.shape[1]]
        start += part.shape[1]
    lines.drain()


def settle(grads, got, tg, tu, td):
    def scratch(w):
        shapes = [
            (4, 2, 4, 16, w),
            (4, 2, 1, 16, w),
            (4, 16, w),
            (4, 16, w),
            (2, 4, 16, w),
            (2, 4, 16, w),
            (1, 16, w),
            (1, 16, w),
            (2, 1, 16, w),
            (2, 1, 16, w),
            (2, 16, w),
            (16, w),
            (16, w),
            (16, w),
        ]
        return [pltpu.VMEM(s, BF16) for s in shapes]

    shape = jax.ShapeDtypeStruct
    return pl.pallas_call(
        settle_kernel,
        name="settle",
        out_shape=(
            shape((32, 1024), F32),
            shape((32, 512), F32),
            shape((32, 512), F32),
            shape((32, 1024), F32),
            shape((32, 128), F32),
            shape((2, 2, 4, 64, 512), F32),
            shape((2, 2, 4, 64, 512), F32),
            shape((2, 2, 4, 32, 1024), F32),
        ),
        in_specs=vmem(5),
        out_specs=vmem(8),
        scratch_shapes=[pltpu.VMEM((32, WIDE), F32)]
        + sems(48)
        + scratch(CUT)
        + scratch(WIDE - CUT)
        + [pltpu.VMEM(t.shape, BF16) for t in (tg, tu, td)],
        compiler_params=params(3),
    )(grads, got, tg, tu, td)


def finish_kernel(*refs):
    n = len(refs) // 3
    sources, targets, stages, arrived = refs[:n], refs[n : 2 * n], refs[2 * n : 3 * n], refs[3 * n]
    fetches, writes = [], []
    for i in range(n):
        fetches.append(pltpu.make_async_copy(sources[i], stages[i], arrived.at[i]))
        writes.append(pltpu.make_async_copy(stages[i], targets[i], arrived.at[n + i]))
        fetches[i].start()
    for i in range(n):
        fetches[i].wait()
        writes[i].start()
    for write in writes:
        write.wait()


def finish(*arrays):
    n = len(arrays)
    return pl.pallas_call(
        finish_kernel,
        name="finish",
        out_shape=tuple(jax.ShapeDtypeStruct(a.shape, a.dtype) for a in arrays),
        in_specs=anywhere(n),
        out_specs=tuple(anywhere(n)),
        scratch_shapes=[pltpu.VMEM(a.shape, a.dtype) for a in arrays]
        + [pltpu.SemaphoreType.DMA((2 * n,))],
        compiler_params=params(limit=60),
    )(*arrays)


HALF = 8 * CAP
TILE = 384


def experts_kernel(
    h2, own_gates, g_all, pos, wg_all, wu_all, wd,
    qy, dh, dg, gg, gu, gd,
    hb, gb, gates, wdb, wg, wu, xs, gs, ms, das, dbs, gys, dhs, gcol, dcol, qg, gg_part, gu_part, gd_part,
    local_sems, send_sems, recv_sems, hand_send, hand_recv, *scratch,
):
    me = Place()
    own = me.high * 4 + me.x
    first = me.high * 16 + me.x * 4
    rows = 2 * HALF
    places = lax.broadcasted_iota(jnp.int32, (CAP, LENGTH), 0).astype(F32)

    def fetch(e):
        slot = lax.rem(e, 2)
        return (
            pltpu.make_async_copy(wg_all.at[e], wg.at[slot], local_sems.at[slot]),
            pltpu.make_async_copy(wu_all.at[e], wu.at[slot], local_sems.at[2 + slot]),
        )

    base, other = me.high * 4, (1 - me.high) * 4
    ahead, behind, far = lax.rem(me.x + 1, 4), lax.rem(me.x + 3, 4), lax.rem(me.x + 2, 4)
    local = [
        pltpu.make_async_copy(h2, hb.at[own], local_sems.at[4]),
        pltpu.make_async_copy(own_gates, gates.at[own], local_sems.at[5]),
        pltpu.make_async_copy(wd, wdb.at[me.z], local_sems.at[6]),
        pltpu.make_async_copy(g_all.at[pl.ds(base, 4)], gb.at[pl.ds(base, 4)], local_sems.at[7]),
    ] + [
        pltpu.make_async_copy(g_all.at[other + p], gb.at[other + p], local_sems.at[8 + i])
        for i, p in enumerate((me.x, ahead, behind))
    ]
    for copy in (*local, *fetch(0), *fetch(1)):
        copy.start()
    greet((me.right(), me.left(), me.cross(), me.above(), me.below(), me.sibling()))
    lines = Lines(send_sems, recv_sems)
    shared = []
    weighed = group_gather(lines, me, own_gates, gates)
    h0 = group_gather(lines, me, h2.at[pl.ds(0, LENGTH)], hb, 0, LENGTH)
    h1 = group_gather(lines, me, h2.at[pl.ds(LENGTH, LENGTH)], hb, LENGTH, LENGTH)
    w3 = weight_chain(lines, me, shared, wd, wdb)
    step(weighed, h0, w3)
    last_g = lines.send(g_all.at[base + far], gb.at[base + far], me.cross())
    qg[...] = jnp.zeros_like(qg)
    step(weighed, h0)
    step(h1)
    step(w3)
    step(weighed, h0)
    step(h1)
    step(weighed)
    last_g.wait_recv()
    for copy in local:
        copy.wait()

    def row_of(table, member, part, k):
        return table[member, pl.ds(part * EXPERTS + first + k, 1), :]

    def slots_of(member):
        return pl.ds(pl.multiple_of(member * CAP, CAP), CAP)

    def all_slots_of(member, part):
        return pl.ds(pl.multiple_of(part * HALF + member * CAP, CAP), CAP)

    def picks(member, part):
        chosen = [places == row_of(pos, member, part, k) for k in range(HERE)]
        return chosen, jnp.concatenate([c.astype(F32).astype(BF16) for c in chosen])

    def gather_g(part):
        @pl.loop(0, 8)
        def _(member):
            chosen, pick = picks(member, part)
            here = all_slots_of(member, part)
            got = dot(pick, gb[member, part * LENGTH : (part + 1) * LENGTH]).astype(BF16)
            for k in range(HERE):
                gs[k, here] = got[k * CAP : (k + 1) * CAP]
                weight = jnp.sum(
                    jnp.where(chosen[k], row_of(gates, member, part, k), 0.0),
                    axis=1,
                    keepdims=True,
                )
                gcol[k, here] = jnp.broadcast_to(weight, (CAP, LENGTH))

    def gather_h(part):
        @pl.loop(0, 8)
        def _(member):
            _, pick = picks(member, part)
            here = all_slots_of(member, part)
            got = dot(pick, hb[member, part * LENGTH : (part + 1) * LENGTH]).astype(BF16)
            for k in range(HERE):
                xs[k, here] = got[k * CAP : (k + 1) * CAP]

    def work(part, e):
        slot = lax.rem(e, 2)
        for copy in fetch(e):
            copy.wait()

        @pl.loop(0, HALF // TILE)
        def _(r):
            near = pl.ds(pl.multiple_of(r * TILE, TILE), TILE)
            here = pl.ds(pl.multiple_of(part * HALF + r * TILE, TILE), TILE)
            x = xs[e, here]
            g_slot = gs[e, here].astype(F32)
            weight = gcol[e, here][:, :1]
            dy = (weight * (RESIDUAL * g_slot)).astype(BF16)
            gs[e, here] = dy
            a = dot(x, wg[slot])
            b = dot(x, wu[slot])
            sig = jax.nn.sigmoid(a)
            swish = a * sig
            m = (swish * b).astype(BF16)
            ms[e, here] = m
            y = dot(m, wdb[e]).astype(BF16).astype(F32)
            inner = RESIDUAL * jnp.sum(g_slot * y, axis=1, keepdims=True)
            dcol[near] = jnp.broadcast_to(inner, (TILE, LENGTH))
            gys[e, near] = (weight * y).astype(BF16)
            dm = dot(dy, wdb[e], ((1,), (1,)))
            da = (dm * b * sig * (1.0 + a * (1.0 - sig))).astype(BF16)
            db = (dm * swish).astype(BF16)
            das[e, here] = da
            dbs[e, here] = db
            dh_slot = dot(da, wg[slot], ((1,), (1,))) + dot(db, wu[slot], ((1,), (1,)))
            dhs[e, near] = dh_slot.astype(BF16)

        @pl.loop(0, 8)
        def _(member):
            chosen = places == row_of(pos, member, part, e)
            qg[member, pl.ds(part * EXPERTS + first + e, 1), :] = jnp.sum(
                jnp.where(chosen, dcol[slots_of(member)], 0.0), axis=0, keepdims=True
            )

        def refill():
            for copy in fetch(lax.rem(e + 2, HERE)):
                copy.start()

        if part == 0:
            refill()
        else:
            pl.when(e < 2)(refill)

    def combine(source, target, part):
        @pl.loop(0, 8)
        def _(member):
            _, pick = picks(member, part)
            here = slots_of(member)
            stack = jnp.concatenate([source[k, here] for k in range(HERE)])
            target[member, part * LENGTH : (part + 1) * LENGTH] = dot(
                pick, stack, ((0,), (0,))
            ).astype(BF16)

    gather_g(0)
    gather_g(1)
    step(h1)
    step(w3)
    drive(h0)
    gather_h(0)
    drive(w3)
    for copy in shared:
        copy.wait_recv()

    @pl.loop(0, HERE)
    def _(e):
        work(0, e)

    drive(h1, weighed)
    lines.drain()
    gather_h(1)
    sums = [
        group_scatter(lines, me, gb, dh, part * LENGTH, LENGTH, *scratch[8 * part : 8 * part + 8])
        for part in range(2)
    ]
    grad = group_scatter(lines, me, qg, dg, 0, 2 * EXPERTS, *scratch[16:24])
    combine(dhs, gb, 0)
    step(sums[0])
    combine(gys, hb, 0)

    @pl.loop(0, 2)
    def _(e):
        work(1, e)

    step(sums[0])

    @pl.loop(2, HERE)
    def _(e):
        work(1, e)

    combine(dhs, gb, 1)
    step(sums[1], grad)
    step(sums[0])
    combine(gys, hb, 1)
    keep = pltpu.make_async_copy(hb, qy, local_sems.at[4])
    keep.start()
    handed = Lines(hand_send, hand_recv)
    copies = []
    for e in range(HERE):
        for copy in copies:
            copy.wait()
        handed.drain()

        @pl.loop(0, D // 256)
        def _(r, e=e):
            here = pl.ds(pl.multiple_of(r * 256, 256), 256)
            x = xs[e, :, here]
            gg_part[here] = dot(x, das[e], ((0,), (0,))).astype(BF16)
            gu_part[here] = dot(x, dbs[e], ((0,), (0,))).astype(BF16)

        @pl.loop(0, FE // 256)
        def _(r, e=e):
            here = pl.ds(pl.multiple_of(r * 256, 256), 256)
            gd_part[here] = dot(ms[e, :, here], gs[e], ((0,), (0,))).astype(BF16)

        copies = []
        for i, (part, target) in enumerate(((gg_part, gg), (gu_part, gu), (gd_part, gd))):
            size = part.shape[0] // 2
            mine = pl.ds(pl.multiple_of(me.core * size, size), size)
            theirs = pl.ds(pl.multiple_of((1 - me.core) * size, size), size)
            copies.append(pltpu.make_async_copy(part.at[mine], target.at[0, e], local_sems.at[i]))
            copies[i].start()
            handed.send(part.at[theirs], target.at[1, e], me.sibling())
        step(*(sums[:1], [sums[1], grad], [sums[1], grad], [*sums, grad])[e])
    drive(sums[1], grad, sums[0])
    for copy in copies:
        copy.wait()
    handed.drain()
    for copy in handed.copies:
        copy.wait_recv()
    keep.wait()
    lines.drain()


def experts(h2, gates, g, pos, wg, wu, wd):
    rows = 2 * HALF
    shape = jax.ShapeDtypeStruct
    return pl.pallas_call(
        experts_kernel,
        name="experts",
        out_shape=(
            shape(g.shape, BF16),
            shape(h2.shape, F32),
            shape(gates.shape, F32),
            shape((2, HERE, D // 2, FE), BF16),
            shape((2, HERE, D // 2, FE), BF16),
            shape((2, HERE, FE // 2, D), BF16),
        ),
        in_specs=anywhere(3) + vmem(1) + anywhere(3),
        out_specs=anywhere(1) + vmem(2) + anywhere(3),
        scratch_shapes=[
            pltpu.VMEM(g.shape, BF16),
            pltpu.VMEM(g.shape, BF16),
            pltpu.VMEM(pos.shape, F32),
            pltpu.VMEM((HERE, FE, D), BF16),
            pltpu.VMEM((2, D, FE), BF16),
            pltpu.VMEM((2, D, FE), BF16),
            pltpu.VMEM((HERE, rows, D), BF16),
            pltpu.VMEM((HERE, rows, D), BF16),
            pltpu.VMEM((HERE, rows, FE), BF16),
            pltpu.VMEM((HERE, rows, FE), BF16),
            pltpu.VMEM((HERE, rows, FE), BF16),
            pltpu.VMEM((HERE, HALF, D), BF16),
            pltpu.VMEM((HERE, HALF, D), BF16),
            pltpu.VMEM((HERE, rows, LENGTH), F32),
            pltpu.VMEM((HALF, LENGTH), F32),
            pltpu.VMEM(pos.shape, F32),
            pltpu.VMEM((D, FE), BF16),
            pltpu.VMEM((D, FE), BF16),
            pltpu.VMEM((FE, D), BF16),
            pltpu.SemaphoreType.DMA((11,)),
        ]
        + sems(64)
        + sems(12)
        + scatter_scratch(LENGTH, D, BF16)
        + scatter_scratch(LENGTH, D, BF16)
        + scatter_scratch(gates.shape[0], gates.shape[1], F32),
        compiler_params=params(1, 60),
    )(h2, gates, g, pos, wg, wu, wd)


def on_device(
    tokens,
    segments,
    routes,
    cotangent,
    attn_gain,
    moe_gain,
    w_query,
    w_key,
    w_value,
    w_output,
    w_router,
    w_gate,
    w_up,
    w_down,
):
    micro = tokens.shape[0]
    rows = micro * LENGTH
    inputs = tokens.reshape(rows, D)
    upstream = cotangent.reshape(rows, D)
    dense, gbuf, sbuf, wgb, wub, h2, q, k, v, p, o, y1, gates, cos, sin = front(
        inputs,
        segments[:, 0],
        routes.reshape(rows, TOPK),
        w_query,
        w_key,
        w_value,
        w_output,
        w_router,
        jnp.stack([attn_gain, moe_gain]).astype(F32),
        upstream,
        w_gate[0],
        w_up[0],
    )

    qy, dh, gate_grad, gg, gu, gd = experts(
        h2, gates, gbuf, sbuf, wgb, wub, w_down[0]
    )
    grads, got, grad_tokens, result, tg, tu, td = retreat(
        inputs, cos, sin, gates, dense.reshape(D, WIDE), upstream, y1, q, k, v, p, o, dh, gate_grad,
        qy, gg, gu, gd,
    )
    gq, gk, gv, go, gsmall, grad_gate, grad_up, grad_down, grad_tokens, result = finish(
        *settle(grads, got, tg, tu, td), grad_tokens, result
    )
    return (
        result.reshape(micro, 1, LENGTH, D),
        grad_tokens.reshape(micro, 1, LENGTH, D),
        gsmall[:, 32],
        gsmall[:, 33],
        gq,
        gk,
        gv,
        go,
        gsmall[:, :32],
        grad_gate.reshape(1, D, FE),
        grad_up.reshape(1, D, FE),
        grad_down.reshape(1, FE, D),
    )


def solution(mesh):
    sequences = P(None, ("rep", "fsdp"), None, None)
    placed = (
        sequences,
        P(None, ("rep", "fsdp"), None),
        sequences,
        sequences,
        P("fsdp"),
        P("fsdp"),
        P("fsdp", None),
        P("fsdp", None),
        P("fsdp", None),
        P("fsdp", None),
        P("fsdp", None),
        P("fsdp", None, None),
        P("fsdp", None, None),
        P("fsdp", None, None),
    )
    return jax.shard_map(
        on_device,
        mesh=mesh,
        in_specs=placed,
        out_specs=(sequences, sequences) + placed[4:],
        check_vma=False,
    )
```

```python
import functools
import math

import jax
import jax.numpy as jnp
from jax import lax
from jax.experimental import pallas as pl
from jax.experimental.pallas import tpu as pltpu
from jax.sharding import PartitionSpec as P

D = 1024
HEADS = 16
KV_HEADS = 8
HEAD_DIM = 64
EXPERTS = 32
FE = 512
TOPK = 8
CAP = 48
LENGTH = 128

EPS = 1e-06
RESIDUAL = 0.22
ATT_SCALE = 0.015625
ROPE_BASE = 10000.0
NEG = -1000000000.0

MESH = pl.DeviceIdType.MESH
F32 = jnp.float32
BF16 = jnp.bfloat16
WIDE = 3200
CUT = 1664
HERE = 4


class Place:
    def __init__(self):
        rep = lax.axis_index("rep")
        flat = lax.axis_index("fsdp")
        self.core = lax.rem(rep, 2)
        self.low = lax.div(rep, 2)
        self.high = lax.div(flat, 16)
        self.x = lax.rem(lax.div(flat, 4), 4)
        self.z = lax.rem(flat, 4)

    def at(self, low=None, core=None, high=None, x=None, z=None):
        low = self.low if low is None else low
        core = self.core if core is None else core
        high = self.high if high is None else high
        x = self.x if x is None else x
        z = self.z if z is None else z
        return (low * 2 + core, high * 16 + x * 4 + z)

    def right(self):
        return self.at(x=lax.rem(self.x + 1, 4))

    def left(self):
        return self.at(x=lax.rem(self.x + 3, 4))

    def above(self):
        return self.at(z=lax.rem(self.z + 1, 4))

    def below(self):
        return self.at(z=lax.rem(self.z + 3, 4))

    def cross(self):
        return self.at(low=1 - self.low, high=1 - self.high)

    def twin(self):
        return self.at(low=1 - self.low)

    def sibling(self):
        return self.at(core=1 - self.core)


class Lines:
    def __init__(self, send_sems, recv_sems):
        self.send_sems, self.recv_sems, self.copies, self.left = send_sems, recv_sems, [], 0

    def send(self, src, dst, device):
        i = len(self.copies)
        assert i < self.send_sems.shape[0]
        copy = pltpu.make_async_remote_copy(
            src_ref=src,
            dst_ref=dst,
            send_sem=self.send_sems.at[i],
            recv_sem=self.recv_sems.at[i],
            device_id=device,
            device_id_type=MESH,
        )
        copy.start()
        self.copies.append(copy)
        return copy

    def drain(self):
        for copy in self.copies[self.left :]:
            copy.wait_send()
        self.left = len(self.copies)


def step(*chains):
    for chain in chains:
        next(chain, None)


def greet(partners):
    barrier = pltpu.get_barrier_semaphore()
    for partner in partners:
        pl.semaphore_signal(barrier, inc=1, device_id=partner, device_id_type=MESH)
    pl.semaphore_wait(barrier, len(partners))


def drive(*chains):
    live = list(chains)
    while live:
        for chain in list(live):
            try:
                next(chain)
            except StopIteration:
                live.remove(chain)


def ring_gather(lines, source, slot, half, pos, right, left, spread=None):
    ahead, behind, far = lax.rem(pos + 1, 4), lax.rem(pos + 3, 4), lax.rem(pos + 2, 4)
    spread = spread or (lambda p: None)
    a = lines.send(source, slot(pos), right)
    b = lines.send(source, slot(pos), left)
    yield
    a.wait_recv()
    c = lines.send(half(behind, 0), half(behind, 0), right)
    b.wait_recv()
    d = lines.send(half(ahead, 1), half(ahead, 1), left)
    spread(behind)
    spread(ahead)
    yield
    c.wait_recv()
    d.wait_recv()
    spread(far)


def group_gather(lines, me, source, buf, start=0, rows=None, last=True):
    rows = rows or buf.shape[1]
    ahead, behind, far = lax.rem(me.x + 1, 4), lax.rem(me.x + 3, 4), lax.rem(me.x + 2, 4)
    right, left, cross = me.right(), me.left(), me.cross()
    base, other = me.high * 4, (1 - me.high) * 4

    def slot(k):
        return buf.at[k, pl.ds(start, rows)]

    def half(k, h):
        return buf.at[k, pl.ds(start + h * rows // 2, rows // 2)]

    e = lines.send(source, slot(base + me.x), cross)
    a = lines.send(source, slot(base + me.x), right)
    b = lines.send(source, slot(base + me.x), left)
    yield
    a.wait_recv()
    c = lines.send(half(base + behind, 0), half(base + behind, 0), right)
    b.wait_recv()
    d = lines.send(half(base + ahead, 1), half(base + ahead, 1), left)
    e.wait_recv()
    f = lines.send(slot(other + me.x), slot(other + me.x), right)
    g = lines.send(slot(other + me.x), slot(other + me.x), left)
    yield
    c.wait_recv()
    d.wait_recv()
    if last:
        h = lines.send(slot(base + far), slot(base + far), cross)
        yield
        h.wait_recv()
    f.wait_recv()
    g.wait_recv()


def weight_chain(lines, me, shared, source, buf):
    half_rows = source.shape[0] // 2
    quarter = half_rows // 2
    start = me.core * half_rows
    mine = pl.ds(pl.multiple_of(start, half_rows), half_rows)

    def slot(p):
        return buf.at[p, mine]

    def half(p, k):
        return buf.at[p, pl.ds(pl.multiple_of(start + k * quarter, quarter), quarter)]

    def spread(p):
        shared.append(lines.send(slot(p), slot(p), me.sibling()))

    yield from ring_gather(
        lines, source.at[mine], slot, half, me.z, me.above(), me.below(), spread=spread
    )


def group_scatter(lines, me, q, out, start, rows, by, tl, tr, hl, hr, fl, fr, fy):
    mid = rows // 2
    step_rows = min(32, mid)
    ahead, behind, far = lax.rem(me.x + 1, 4), lax.rem(me.x + 3, 4), lax.rem(me.x + 2, 4)
    right, left, cross = me.right(), me.left(), me.cross()
    base, other = me.high * 4, (1 - me.high) * 4
    first, second = pl.ds(0, mid), pl.ds(mid, mid)

    def whole(k):
        return q.at[k, pl.ds(start, rows)]

    def part(k, h):
        return q.at[k, pl.ds(start + h * mid, mid)]

    def each(count, offset, body):
        @pl.loop(0, count // step_rows)
        def _(i):
            here = pl.multiple_of(i * step_rows, step_rows)
            there = pl.multiple_of(start + offset + i * step_rows, step_rows)
            body(pl.ds(here, step_rows), pl.ds(there, step_rows))

    e = lines.send(whole(other + far), by, cross)
    g1 = lines.send(whole(other + ahead), tl, right)
    g2 = lines.send(whole(other + behind), tr, left)
    i1 = lines.send(part(base + ahead, 1), fl.at[second], right)
    i2 = lines.send(part(base + behind, 0), fr.at[first], left)
    yield
    e.wait_recv()

    def far_sum(here, there):
        by[here] = q[base + far, there] + by[here]

    each(rows, 0, far_sum)
    j1 = lines.send(by.at[first], hl, right)
    j2 = lines.send(by.at[second], hr, left)
    yield
    g1.wait_recv()
    g2.wait_recv()

    def partner_sum(here, there):
        total = q[other + me.x, there].astype(F32) + tl[here].astype(F32) + tr[here].astype(F32)
        tl[here] = total.astype(tl.dtype)

    each(rows, 0, partner_sum)
    k = lines.send(tl, fy, cross)
    yield
    j1.wait_recv()

    def right_sum(here, there):
        hl[here] = q[base + ahead, there] + hl[here]

    each(mid, 0, right_sum)
    l1 = lines.send(hl, fl.at[first], right)
    j2.wait_recv()

    def left_sum(here, there):
        hr[here] = q[base + behind, there] + hr[here]

    each(mid, mid, left_sum)
    l2 = lines.send(hr, fr.at[second], left)
    yield
    for copy in (i1, i2, l1, l2, k):
        copy.wait_recv()

    def total(here, there):
        out[there] = (
            q[base + me.x, there].astype(F32)
            + fl[here].astype(F32)
            + fr[here].astype(F32)
            + fy[here].astype(F32)
        )

    each(rows, 0, total)


def ring_scatter(lines, arr, pos, right, left, hl, hr, fl, fr, store):
    n = arr.shape[2]
    ahead, behind, far = lax.rem(pos + 1, 4), lax.rem(pos + 3, 4), lax.rem(pos + 2, 4)
    a = lines.send(arr.at[far, 0], hl, right)
    b = lines.send(arr.at[far, 1], hr, left)
    c = lines.send(arr.at[ahead, 1], fl.at[1], right)
    d = lines.send(arr.at[behind, 0], fr.at[0], left)
    yield
    a.wait_recv()

    @pl.loop(0, n)
    def _(j):
        arr[ahead, 0, j] = arr[ahead, 0, j] + hl[j]

    e = lines.send(arr.at[ahead, 0], fl.at[0], right)
    b.wait_recv()

    @pl.loop(0, n)
    def _(j):
        arr[behind, 1, j] = arr[behind, 1, j] + hr[j]

    f = lines.send(arr.at[behind, 1], fr.at[1], left)
    yield
    for copy in (c, d, e, f):
        copy.wait_recv()
    for half in range(2):

        @pl.loop(0, n)
        def _(j, half=half):
            store(
                half,
                j,
                arr[pos, half, j].astype(F32) + fl[half, j].astype(F32) + fr[half, j].astype(F32),
            )


def dot(a, b, dims=((1,), (0,))):
    return lax.dot_general(a, b, (dims, ((), ())), preferred_element_type=F32)


def lanes():
    return lax.broadcasted_iota(jnp.int32, (1, 128), 1)


def swap_halves(u):
    return jnp.where(
        lax.rem(lanes(), 64) < 32, pltpu.roll(u, 96, axis=1), pltpu.roll(u, 32, axis=1)
    )


def doubled(tile, odd):
    wide = tile.astype(F32)
    turned = pltpu.roll(wide, 64, axis=1)
    low = lanes() < 64
    return jnp.where(low, turned if odd else wide, wide if odd else turned).astype(BF16)


def stacked(pair):
    wide = pair.astype(F32)
    low = lanes() < 64
    return jnp.concatenate([jnp.where(low, wide, 0.0), jnp.where(low, 0.0, wide)]).astype(BF16)


def side_by_side(both):
    return jnp.where(lanes() < 64, both[:128], both[128:])


def folded(even, odd):
    even = even + pltpu.roll(even, 64, axis=1)
    odd = odd + pltpu.roll(odd, 64, axis=1)
    return jnp.where(lanes() < 64, even, odd)


def side(table):
    return jnp.concatenate([table[:EXPERTS], table[EXPERTS:]], axis=1)


def phases(segment):
    across = jnp.broadcast_to(segment.astype(F32), (LENGTH, LENGTH))
    down = jnp.transpose(across)
    t = lax.broadcasted_iota(jnp.int32, (LENGTH, LENGTH), 0)
    u = lax.broadcasted_iota(jnp.int32, (LENGTH, LENGTH), 1)
    keep = jnp.where((u <= t) & (across == down), 1.0, 0.0)
    offset = jnp.sum(keep, axis=1, keepdims=True) - 1.0
    step_of = lax.rem(lanes(), 32).astype(F32)
    frequency = jnp.exp(-math.log(ROPE_BASE) * 2.0 * step_of / HEAD_DIM)
    angles = offset * frequency
    sign = jnp.where(lax.rem(lanes(), 64) < 32, -1.0, 1.0)
    return jnp.cos(angles), sign * jnp.sin(angles), keep


def slot_table(route_ids):
    wide = jnp.concatenate([route_ids.astype(F32), jnp.zeros((LENGTH, 128 - TOPK), F32)], axis=1)
    by_choice = jnp.transpose(wide)
    ids = lax.broadcasted_iota(jnp.int32, (EXPERTS, LENGTH), 0).astype(F32)
    named = jnp.zeros((EXPERTS, LENGTH), F32)
    for j in range(TOPK):
        named = jnp.where(by_choice[j : j + 1] == ids, 1.0, named)
    t = lax.broadcasted_iota(jnp.int32, (LENGTH, LENGTH), 0)
    u = lax.broadcasted_iota(jnp.int32, (LENGTH, LENGTH), 1)
    before = jnp.where(t < u, 1.0, 0.0).astype(BF16)
    return jnp.where(named > 0.0, dot(named.astype(BF16), before), -1.0)


def small_shard(router, gains):
    wide = jnp.concatenate([router.astype(F32), jnp.zeros((32, 128 - EXPERTS), F32)], axis=1)
    row = lax.broadcasted_iota(jnp.int32, (32, 32), 0)
    lane = lax.broadcasted_iota(jnp.int32, (32, 32), 1)
    for i in range(2):
        across = jnp.broadcast_to(gains[i : i + 1].astype(F32), (32, 32))
        column = jnp.sum(jnp.where(row == lane, across, 0.0), axis=1, keepdims=True)
        wide = jnp.where(lanes() == EXPERTS + i, column, wide)
    return wide.astype(BF16)


def norm_scale(values):
    return lax.rsqrt(jnp.mean(values * values, axis=1, keepdims=True) + EPS)


def gain_rows(small):
    row = lax.broadcasted_iota(jnp.int32, (8, 128), 0)
    lane = lax.broadcasted_iota(jnp.int32, (8, 128), 1)
    pick = (lane == row + EXPERTS).astype(F32).astype(BF16)
    rows = dot(pick, small, ((1,), (1,)))
    return rows[0:1], rows[1:2]


def column_sums(values, column):
    rows = values.shape[0]
    pick = (lax.broadcasted_iota(jnp.int32, (rows, 128), 1) == column).astype(F32).astype(BF16)
    upper = values.astype(BF16)
    lower = (values - upper.astype(F32)).astype(BF16)
    return dot(upper, pick, ((0,), (0,))) + dot(lower, pick, ((0,), (0,)))


def anywhere(n):
    return [pl.BlockSpec(memory_space=pl.ANY)] * n


def vmem(n):
    return [pl.BlockSpec(memory_space=pltpu.VMEM)] * n


def sems(n):
    return [pltpu.SemaphoreType.DMA((n,)), pltpu.SemaphoreType.DMA((n,))]


def params(number=None, limit=56):
    if number is None:
        return pltpu.CompilerParams(vmem_limit_bytes=limit << 20)
    return pltpu.CompilerParams(
        collective_id=number, has_side_effects=True, vmem_limit_bytes=limit << 20
    )


def front_kernel(
    tokens, segments, routes, wq_own, wk_own, wv_own, wo_own, wr_own, gains, g, wg, wu,
    dense, gbuf, sbuf, wgb, wub, h2, q, k, v, p, o, y1, gates, cos, sin,
    dn, h, keep, slots, send_sems, recv_sems, local_sems,
):
    me = Place()
    right, left, above, below = me.right(), me.left(), me.above(), me.below()
    cross, sibling = me.cross(), me.sibling()
    rows = pl.ds(pl.multiple_of(me.core * 16, 16), 16)
    own = me.high * 4 + me.x
    local = [
        pltpu.make_async_copy(g, gbuf.at[own], local_sems.at[1]),
        pltpu.make_async_copy(wg, wgb.at[me.z], local_sems.at[3]),
        pltpu.make_async_copy(wu, wub.at[me.z], local_sems.at[4]),
    ]
    for copy in local:
        copy.start()
    shard = dn.at[me.high, me.x, me.z]
    shard[:, 0:1024] = wq_own[...]
    shard[:, 1024:1536] = wk_own[...]
    shard[:, 1536:2048] = wv_own[...]
    shard[:, 2048:3072] = wo_own[...]
    shard[:, 3072:3200] = small_shard(wr_own[...], gains[...])
    greet((right, left, above, below, cross, sibling))
    lines = Lines(send_sems, recv_sems)
    shared = []

    def dense_chain(columns, x_first):
        on_x, on_z = (me.x, right, left), (me.z, above, below)
        (pos, up, down), (pos2, up2, down2) = (on_x, on_z) if x_first else (on_z, on_x)
        ahead, behind, far = lax.rem(pos + 1, 4), lax.rem(pos + 3, 4), lax.rem(pos + 2, 4)

        def piece(one, two, k=None):
            x, z = (one, two) if x_first else (two, one)
            return dn.at[slice(None) if k is None else k, x, z, rows, columns]

        def unit(one):
            def spread(two):
                shared.append(lines.send(piece(one, two), piece(one, two), sibling))

            def slot(two):
                return piece(one, two)

            def half(two, k):
                return piece(one, two, k)

            chain = ring_gather(lines, slot(pos2), slot, half, pos2, up2, down2, spread=spread)
            next(chain)
            spread(pos2)
            return chain

        mine = piece(pos, pos2)
        a = lines.send(mine, mine, up)
        b = lines.send(mine, mine, down)
        units = [unit(pos)]
        yield
        a.wait_recv()
        c = lines.send(piece(behind, pos2, 0), piece(behind, pos2, 0), up)
        units.append(unit(behind))
        b.wait_recv()
        d = lines.send(piece(ahead, pos2, 1), piece(ahead, pos2, 1), down)
        units.append(unit(ahead))
        yield
        step(units[0])
        yield
        c.wait_recv()
        d.wait_recv()
        units.append(unit(far))
        yield
        step(units[1], units[2])
        yield
        step(units[0], units[3])
        yield
        step(*units[1:])
        step(*units)

    swap = lines.send(shard.at[rows], shard.at[rows], cross)
    for part in range(2):
        here = slice(part * LENGTH, (part + 1) * LENGTH)
        cos[here], sin[here], keep[part] = phases(segments[part : part + 1, :])
        slots[part * EXPERTS : (part + 1) * EXPERTS] = slot_table(routes[here, :])
    local.append(pltpu.make_async_copy(slots, sbuf.at[own], local_sems.at[2]))
    local[-1].start()
    swap.wait_recv()
    gs = group_gather(lines, me, g, gbuf, last=False)
    ss = group_gather(lines, me, slots, sbuf)
    w1 = weight_chain(lines, me, shared, wg, wgb)
    w2 = weight_chain(lines, me, shared, wu, wub)
    dense_a, dense_b = dense_chain(pl.ds(0, CUT), False), dense_chain(pl.ds(CUT, WIDE - CUT), True)
    step(dense_a, dense_b)
    step(gs, ss, w1)
    drive(dense_a, dense_b)
    for copy in shared:
        copy.wait_recv()
    del shared[:]
    step(gs, ss, w2)
    keeping = pltpu.make_async_copy(dn, dense, local_sems.at[6])
    keeping.start()

    def weight(start, size):
        return dn[:, :, :, :, start : start + size].reshape(D, size)

    small = weight(3072, 128)
    gain_one, gain_two = gain_rows(small)
    x = tokens[...].astype(F32)
    h[...] = (x * norm_scale(x) * gain_one).astype(BF16)
    for piece in range(4):
        raw = dot(h[...], weight(piece * 256, 256))
        for t in range(2):
            u = raw[:, t * 128 : t * 128 + 128]
            q[:, piece * 256 + t * 128 : piece * 256 + t * 128 + 128] = (
                u * cos[...] + swap_halves(u) * sin[...]
            ).astype(BF16)
    for piece in range(2):
        raw = dot(h[...], weight(1024 + piece * 256, 256))
        for t in range(2):
            u = raw[:, t * 128 : t * 128 + 128]
            k[:, piece * 256 + t * 128 : piece * 256 + t * 128 + 128] = (
                u * cos[...] + swap_halves(u) * sin[...]
            ).astype(BF16)
    v[...] = dot(h[...], weight(1536, 512)).astype(BF16)
    step(w1)

    def attend(i):
        s, m = lax.div(i, 4), lax.rem(i, 4)
        here = pl.ds(pl.multiple_of(s * 128, 128), 128)
        column = pl.ds(pl.multiple_of(m * 128, 128), 128)
        seen = keep[s]
        seen = jnp.concatenate([seen, seen]) > 0.0
        k_tile, v_tile = k[here, column], v[here, column]
        for odd in range(2):
            q_column = pl.ds(pl.multiple_of(m * 256 + odd * 128, 128), 128)
            scores = dot(stacked(q[here, q_column]), doubled(k_tile, odd), ((1,), (1,))) * ATT_SCALE
            scores = jnp.where(seen, scores, NEG)
            raised = jnp.exp(scores - jnp.max(scores, axis=1, keepdims=True))
            probs = raised / jnp.sum(raised, axis=1, keepdims=True)
            p[i, odd] = probs
            both = dot(probs.astype(BF16), doubled(v_tile, odd))
            o[here, q_column] = side_by_side(both).astype(BF16)

    for part in range(2):

        @pl.loop(part * 4, part * 4 + 4)
        def _(i):
            attend(i)

        if part == 0:
            step(w2, ss)

    middle = tokens[...].astype(F32) + RESIDUAL * dot(o[...], weight(2048, 1024))
    y1[...] = middle
    h2[...] = (middle * norm_scale(middle) * gain_two).astype(BF16)
    logits = dot(small, h2[...], ((0,), (1,)))[:EXPERTS]
    named = side(slots) >= 0.0
    top = jnp.max(jnp.where(named, logits, -jnp.inf), axis=0, keepdims=True)
    raised = jnp.where(named, jnp.exp(jnp.where(named, logits - top, 0.0)), 0.0)
    raised = raised / jnp.sum(raised, axis=0, keepdims=True)
    gates[:EXPERTS] = raised[:, :LENGTH]
    gates[EXPERTS:] = raised[:, LENGTH:]
    drive(ss, w1, w2, gs)
    for copy in shared:
        copy.wait_recv()
    for copy in local + [keeping]:
        copy.wait()
    lines.drain()


def front(tokens, segments, routes, wq, wk, wv, wo, wr, gains, g, wg, wu):
    shape = jax.ShapeDtypeStruct
    rows = tokens.shape[0]
    slots = shape((2 * EXPERTS, LENGTH), F32)
    return pl.pallas_call(
        front_kernel,
        name="front",
        out_shape=(
            shape((2, 4, 4, 32, WIDE), BF16),
            shape((8,) + g.shape, BF16),
            shape((8,) + slots.shape, F32),
            shape((4,) + wg.shape, BF16),
            shape((4,) + wu.shape, BF16),
            shape((rows, D), BF16),
            shape((rows, 1024), BF16),
            shape((rows, 512), BF16),
            shape((rows, 512), BF16),
            shape((8, 2, 256, 128), F32),
            shape((rows, 1024), BF16),
            shape((rows, D), F32),
            shape(slots.shape, F32),
            shape((rows, 128), F32),
            shape((rows, 128), F32),
        ),
        in_specs=vmem(12),
        out_specs=anywhere(5) + vmem(10),
        scratch_shapes=[
            pltpu.VMEM((2, 4, 4, 32, WIDE), BF16),
            pltpu.VMEM((rows, D), BF16),
            pltpu.VMEM((2, LENGTH, LENGTH), F32),
            pltpu.VMEM(slots.shape, F32),
        ]
        + sems(140)
        + [pltpu.SemaphoreType.DMA((7,))],
        compiler_params=params(0),
    )(tokens, segments, routes, wq, wk, wv, wo, wr, gains, g, wg, wu)


def scatter_scratch(rows, columns, dtype):
    full = pltpu.VMEM((rows, columns), dtype)
    half = pltpu.VMEM((rows // 2, columns), dtype)
    return [full] * 3 + [half] * 2 + [full] * 3


def retreat_kernel(
    tokens, cos, sin, gates, dense, g, y1, q, k, v, p, o, dh, dg, qy, gg, gu, gd,
    grads, got, grad_tokens, result, tg, tu, td,
    h, do, dq, dk, dv, small_grad, mixture, *scratch,
):
    me = Place()
    send_sems, recv_sems, local_sems = scratch[:3]
    above, below = me.above(), me.below()
    local = []
    for i, (grad, acc) in enumerate(((gg, scratch[4]), (gu, scratch[10]), (gd, scratch[16]))):
        local.append(pltpu.make_async_copy(grad.at[0], acc, local_sems.at[i]))
        local[-1].start()
    for i, (grad, rc) in enumerate(((gg, scratch[3]), (gu, scratch[9]), (gd, scratch[15]))):
        local.append(pltpu.make_async_copy(grad.at[1], rc, local_sems.at[3 + i]))
        local[-1].start()
    greet((me.right(), me.left(), me.cross(), above, below, me.sibling()))
    lines = Lines(send_sems, recv_sems)

    theirs = pl.ds(pl.multiple_of((1 - me.core) * 16, 16), 16)
    handed = []

    def keep_rows(t, columns, value):
        shards = value.astype(BF16).reshape(2, 4, 32, value.shape[1])
        grads[t // 2, (t % 2) * 2 : (t % 2) * 2 + 2, :, :, columns] = shards

    def hand(columns):
        handed.append(
            lines.send(
                grads.at[:, :, :, theirs, columns], got.at[:, :, :, :, columns], me.sibling()
            )
        )

    def chain(tot, mine, theirs_in, rc, acc, hl, hr, fl, fr):
        mine.wait()
        theirs_in.wait()

        @pl.loop(0, 32)
        def _(i):
            a, b, j = lax.div(i, 8), lax.rem(lax.div(i, 4), 2), lax.rem(i, 4)
            acc[a, b, j] = acc[a, b, j] + rc[a, b, j]

        def store(b, j, value):
            tot[b, j] = value.astype(BF16)

        yield from ring_scatter(lines, acc, me.z, above, below, hl, hr, fl, fr, store)

    e1 = chain(tg, local[0], local[3], *scratch[3:9])
    e2 = chain(tu, local[1], local[4], *scratch[9:15])
    e3 = chain(td, local[2], local[5], *scratch[15:21])
    ys = group_scatter(lines, me, qy, mixture, 0, 2 * LENGTH, *scratch[21:29])
    step(e1, e2, ys)

    small = dense[:, 3072:3200]
    gain_one, gain_two = gain_rows(small)
    x = tokens[...].astype(F32)
    h[...] = (x * norm_scale(x) * gain_one).astype(BF16)
    middle = y1[...]
    scale = norm_scale(middle)
    normed = middle * scale
    routed = (normed * gain_two).astype(BF16)
    weights, grad = side(gates), side(dg)
    choice = weights * (grad - jnp.sum(weights * grad, axis=0, keepdims=True))
    by_token = jnp.transpose(
        jnp.concatenate([choice, jnp.zeros((128 - EXPERTS, choice.shape[1]), F32)])
    ).astype(BF16)
    dh2 = dh[...] + dot(by_token, small, ((1,), (1,)))
    small_grad[...] = dot(routed, by_token, ((0,), (0,))) + column_sums(dh2 * normed, EXPERTS + 1)
    dn = dh2 * gain_two
    dy = g[...].astype(F32) + scale * (dn - normed * jnp.mean(dn * normed, axis=1, keepdims=True))
    grad_tokens[...] = dy
    dz = (RESIDUAL * dy).astype(BF16)
    step(e3)
    for t in range(4):
        here = slice(t * 256, t * 256 + 256)
        keep_rows(t, pl.ds(2048, 1024), dot(o[:, here], dz, ((0,), (0,))))
    hand(pl.ds(2048, 1024))
    do[...] = dot(dz, dense[:, 2048:3072], ((1,), (1,))).astype(BF16)
    step(e1, ys)

    def attend_back(i):
        s, m = lax.div(i, 4), lax.rem(i, 4)
        here = pl.ds(pl.multiple_of(s * 128, 128), 128)
        column = pl.ds(pl.multiple_of(m * 128, 128), 128)
        cos_s, sin_s = cos[here], sin[here]
        k_tile, v_tile = k[here, column], v[here, column]
        dk_both, dv_both = [], []
        for odd in range(2):
            q_column = pl.ds(pl.multiple_of(m * 256 + odd * 128, 128), 128)
            q_two, do_two = stacked(q[here, q_column]), stacked(do[here, q_column])
            probs = p[i, odd]
            dp = dot(do_two, doubled(v_tile, odd), ((1,), (1,)))
            inner = jnp.sum(probs * dp, axis=1, keepdims=True)
            ds = (probs * (dp - inner)).astype(BF16)
            dv_both.append(dot(probs.astype(BF16), do_two, ((0,), (0,))))
            dk_both.append(dot(ds, q_two, ((0,), (0,))) * ATT_SCALE)
            u = side_by_side(dot(ds, doubled(k_tile, odd))) * ATT_SCALE
            dq[here, q_column] = (u * cos_s - swap_halves(u) * sin_s).astype(BF16)
        u = folded(*dk_both)
        dk[here, column] = (u * cos_s - swap_halves(u) * sin_s).astype(BF16)
        dv[here, column] = folded(*dv_both).astype(BF16)

    for part in range(4):

        @pl.loop(part * 2, part * 2 + 2)
        def _(i):
            attend_back(i)

        step(*((), (ys, e2), (e1,), (ys, e3))[part])

    for t in range(4):
        here = slice(t * 256, t * 256 + 256)
        keep_rows(t, pl.ds(0, 1024), dot(h[:, here], dq[...], ((0,), (0,))))
        keep_rows(t, pl.ds(1024, 512), dot(h[:, here], dk[...], ((0,), (0,))))
        keep_rows(t, pl.ds(1536, 512), dot(h[:, here], dv[...], ((0,), (0,))))
    hand(pl.ds(0, 2048))
    dh1 = (
        dot(dq[...], dense[:, 0:1024], ((1,), (1,)))
        + dot(dk[...], dense[:, 1024:1536], ((1,), (1,)))
        + dot(dv[...], dense[:, 1536:2048], ((1,), (1,)))
    )
    step(e2, ys)
    x = tokens[...].astype(F32)
    scale = norm_scale(x)
    normed = x * scale
    small_sum = small_grad[...] + column_sums(dh1 * normed, EXPERTS)
    for t in range(4):
        keep_rows(t, pl.ds(3072, 128), small_sum[t * 256 : t * 256 + 256])
    hand(pl.ds(3072, 128))
    dn = dh1 * gain_one
    grad_tokens[...] += scale * (dn - normed * jnp.mean(dn * normed, axis=1, keepdims=True))
    drive(ys, e1, e2, e3)
    result[...] = (y1[...] + RESIDUAL * mixture[...]).astype(BF16)
    for copy in handed:
        copy.wait_recv()
    lines.drain()


def halves(r, w):
    return (2, 4, 2, 4, r, w)


def retreat(tokens, cos, sin, gates, dense, g, y1, q, k, v, p, o, dh, dg, qy, gg, gu, gd):
    def scratch(r, w):
        shapes = [(4, 2, 4, r, w)] * 2 + [(4, r, w)] * 2 + [(2, 4, r, w)] * 2
        return [pltpu.VMEM(s, BF16) for s in shapes]

    shape = jax.ShapeDtypeStruct
    rows = tokens.shape[0]
    return pl.pallas_call(
        retreat_kernel,
        name="retreat",
        out_shape=(
            shape((2, 4, 4, 32, WIDE), BF16),
            shape((2, 4, 4, 16, WIDE), BF16),
            shape((rows, D), F32),
            shape((rows, D), BF16),
            shape((2, 4, 64, 512), BF16),
            shape((2, 4, 64, 512), BF16),
            shape((2, 4, 32, 1024), BF16),
        ),
        in_specs=vmem(15) + anywhere(3),
        out_specs=vmem(1) + anywhere(1) + vmem(5),
        scratch_shapes=[
            pltpu.VMEM((rows, D), BF16),
            pltpu.VMEM((rows, 1024), BF16),
            pltpu.VMEM((rows, 1024), BF16),
            pltpu.VMEM((rows, 512), BF16),
            pltpu.VMEM((rows, 512), BF16),
            pltpu.VMEM((D, 128), F32),
            pltpu.VMEM((rows, D), F32),
        ]
        + sems(40)
        + [pltpu.SemaphoreType.DMA((6,))]
        + scratch(64, 512)
        + scratch(64, 512)
        + scratch(32, 1024)
        + scatter_scratch(rows, D, BF16),
        compiler_params=params(2, 60),
    )(
        tokens, cos, sin, gates, dense, g, y1, q, k, v, p, o, dh, dg, qy,
        gg.reshape(halves(64, 512)), gu.reshape(halves(64, 512)), gd.reshape(halves(32, 1024)),
    )


def settle_kernel(grads, rc, tg, tu, td, oq, ok, ov, oo, osmall, og, ou, od, out, *scratch):
    me = Place()
    send_sems, recv_sems = scratch[:2]
    right, left, above, below = me.right(), me.left(), me.above(), me.below()
    cross, twin, sibling = me.cross(), me.twin(), me.sibling()
    greet((right, left, above, below, cross, twin, sibling))
    lines = Lines(send_sems, recv_sems)
    mine = pl.ds(pl.multiple_of(me.core * 16, 16), 16)
    theirs = pl.ds(pl.multiple_of((1 - me.core) * 16, 16), 16)

    def chain(columns, x_first, acc, second, hl, hr, fl, fr, hl2, hr2, fl2, fr2, r2, ry, r3, yb):
        @pl.loop(0, 32)
        def _(i):
            k, x, z = lax.div(i, 16), lax.rem(lax.div(i, 4), 4), lax.rem(i, 4)
            value = grads[k, x, z, mine, columns] + rc[k, x, z, :, columns]
            if x_first:
                acc[x, k, z] = value
            else:
                acc[z, k, x] = value

        yield

        def store(k, j, value):
            second[j, k, 0] = value.astype(BF16)

        def store_last(k, j, value):
            r2[k] = value.astype(BF16)

        on_x, on_z = (me.x, right, left), (me.z, above, below)
        one, two = (on_x, on_z) if x_first else (on_z, on_x)
        yield from ring_scatter(lines, acc, *one, hl, hr, fl, fr, store)
        yield from ring_scatter(lines, second, *two, hl2, hr2, fl2, fr2, store_last)
        a = lines.send(r2.at[1 - me.high], ry, cross)
        yield
        a.wait_recv()
        r3[...] = (r2[me.high].astype(F32) + ry[...].astype(F32)).astype(BF16)
        b = lines.send(r3, yb, twin)
        yield
        b.wait_recv()
        out[mine, columns] = r3[...].astype(F32) + yb[...].astype(F32)
        c = lines.send(out.at[mine, columns], out.at[mine, columns], sibling)
        yield
        c.wait_recv()

    def swapped(tot, whole, other):
        a = lines.send(tot, other, twin)
        yield
        a.wait_recv()
        for k in range(2):

            @pl.loop(0, 4)
            def _(j, k=k):
                whole[me.core, k, j] = tot[k, j].astype(F32) + other[k, j].astype(F32)

        b = lines.send(whole.at[me.core], whole.at[me.core], sibling)
        yield
        b.wait_recv()

    others = [swapped(t, w, s) for t, w, s in zip((tg, tu, td), (og, ou, od), scratch[30:33])]
    step(*others)
    one = chain(pl.ds(0, CUT), True, *scratch[2:16])
    two = chain(pl.ds(CUT, WIDE - CUT), False, *scratch[16:30])
    step(one)
    step(one)
    step(two)
    step(two)
    drive(one, two)
    drive(*others)
    start = 0
    for part in (oq, ok, ov, oo, osmall):
        part[...] = out[:, start : start + part.shape[1]]
        start += part.shape[1]
    lines.drain()


def settle(grads, got, tg, tu, td):
    def scratch(w):
        shapes = [
            (4, 2, 4, 16, w),
            (4, 2, 1, 16, w),
            (4, 16, w),
            (4, 16, w),
            (2, 4, 16, w),
            (2, 4, 16, w),
            (1, 16, w),
            (1, 16, w),
            (2, 1, 16, w),
            (2, 1, 16, w),
            (2, 16, w),
            (16, w),
            (16, w),
            (16, w),
        ]
        return [pltpu.VMEM(s, BF16) for s in shapes]

    shape = jax.ShapeDtypeStruct
    return pl.pallas_call(
        settle_kernel,
        name="settle",
        out_shape=(
            shape((32, 1024), F32),
            shape((32, 512), F32),
            shape((32, 512), F32),
            shape((32, 1024), F32),
            shape((32, 128), F32),
            shape((2, 2, 4, 64, 512), F32),
            shape((2, 2, 4, 64, 512), F32),
            shape((2, 2, 4, 32, 1024), F32),
        ),
        in_specs=vmem(5),
        out_specs=vmem(8),
        scratch_shapes=[pltpu.VMEM((32, WIDE), F32)]
        + sems(48)
        + scratch(CUT)
        + scratch(WIDE - CUT)
        + [pltpu.VMEM(t.shape, BF16) for t in (tg, tu, td)],
        compiler_params=params(3),
    )(grads, got, tg, tu, td)


def finish_kernel(*refs):
    n = len(refs) // 3
    sources, targets, stages, arrived = refs[:n], refs[n : 2 * n], refs[2 * n : 3 * n], refs[3 * n]
    fetches, writes = [], []
    for i in range(n):
        fetches.append(pltpu.make_async_copy(sources[i], stages[i], arrived.at[i]))
        writes.append(pltpu.make_async_copy(stages[i], targets[i], arrived.at[n + i]))
        fetches[i].start()
    for i in range(n):
        fetches[i].wait()
        writes[i].start()
    for write in writes:
        write.wait()


def finish(*arrays):
    n = len(arrays)
    return pl.pallas_call(
        finish_kernel,
        name="finish",
        out_shape=tuple(jax.ShapeDtypeStruct(a.shape, a.dtype) for a in arrays),
        in_specs=anywhere(n),
        out_specs=tuple(anywhere(n)),
        scratch_shapes=[pltpu.VMEM(a.shape, a.dtype) for a in arrays]
        + [pltpu.SemaphoreType.DMA((2 * n,))],
        compiler_params=params(limit=60),
    )(*arrays)


HALF = 8 * CAP
TILE = 384


def experts_kernel(
    h2, own_gates, g_all, pos, wg_all, wu_all, wd,
    qy, dh, dg, gg, gu, gd,
    hb, gb, gates, wdb, wg, wu, xs, gs, ms, das, dbs, gys, dhs, gcol, dcol, qg, gg_part, gu_part, gd_part,
    local_sems, send_sems, recv_sems, hand_send, hand_recv, *scratch,
):
    me = Place()
    own = me.high * 4 + me.x
    first = me.high * 16 + me.x * 4
    rows = 2 * HALF
    places = lax.broadcasted_iota(jnp.int32, (CAP, LENGTH), 0).astype(F32)

    def fetch(e):
        slot = lax.rem(e, 2)
        return (
            pltpu.make_async_copy(wg_all.at[e], wg.at[slot], local_sems.at[slot]),
            pltpu.make_async_copy(wu_all.at[e], wu.at[slot], local_sems.at[2 + slot]),
        )

    base, other = me.high * 4, (1 - me.high) * 4
    ahead, behind, far = lax.rem(me.x + 1, 4), lax.rem(me.x + 3, 4), lax.rem(me.x + 2, 4)
    local = [
        pltpu.make_async_copy(h2, hb.at[own], local_sems.at[4]),
        pltpu.make_async_copy(own_gates, gates.at[own], local_sems.at[5]),
        pltpu.make_async_copy(wd, wdb.at[me.z], local_sems.at[6]),
        pltpu.make_async_copy(g_all.at[pl.ds(base, 4)], gb.at[pl.ds(base, 4)], local_sems.at[7]),
    ] + [
        pltpu.make_async_copy(g_all.at[other + p], gb.at[other + p], local_sems.at[8 + i])
        for i, p in enumerate((me.x, ahead, behind))
    ]
    for copy in (*local, *fetch(0), *fetch(1)):
        copy.start()
    greet((me.right(), me.left(), me.cross(), me.above(), me.below(), me.sibling()))
    lines = Lines(send_sems, recv_sems)
    shared = []
    weighed = group_gather(lines, me, own_gates, gates)
    h0 = group_gather(lines, me, h2.at[pl.ds(0, LENGTH)], hb, 0, LENGTH)
    h1 = group_gather(lines, me, h2.at[pl.ds(LENGTH, LENGTH)], hb, LENGTH, LENGTH)
    w3 = weight_chain(lines, me, shared, wd, wdb)
    step(weighed, h0, w3)
    last_g = lines.send(g_all.at[base + far], gb.at[base + far], me.cross())
    qg[...] = jnp.zeros_like(qg)
    step(weighed, h0)
    step(h1)
    step(w3)
    step(weighed, h0)
    step(h1)
    step(weighed)
    last_g.wait_recv()
    for copy in local:
        copy.wait()

    def row_of(table, member, part, k):
        return table[member, pl.ds(part * EXPERTS + first + k, 1), :]

    def slots_of(member):
        return pl.ds(pl.multiple_of(member * CAP, CAP), CAP)

    def all_slots_of(member, part):
        return pl.ds(pl.multiple_of(part * HALF + member * CAP, CAP), CAP)

    def picks(member, part):
        chosen = [places == row_of(pos, member, part, k) for k in range(HERE)]
        return chosen, jnp.concatenate([c.astype(F32).astype(BF16) for c in chosen])

    def gather_g(part):
        @pl.loop(0, 8)
        def _(member):
            chosen, pick = picks(member, part)
            here = all_slots_of(member, part)
            got = dot(pick, gb[member, part * LENGTH : (part + 1) * LENGTH]).astype(BF16)
            for k in range(HERE):
                gs[k, here] = got[k * CAP : (k + 1) * CAP]
                weight = jnp.sum(
                    jnp.where(chosen[k], row_of(gates, member, part, k), 0.0),
                    axis=1,
                    keepdims=True,
                )
                gcol[k, here] = jnp.broadcast_to(weight, (CAP, LENGTH))

    def gather_h(part):
        @pl.loop(0, 8)
        def _(member):
            _, pick = picks(member, part)
            here = all_slots_of(member, part)
            got = dot(pick, hb[member, part * LENGTH : (part + 1) * LENGTH]).astype(BF16)
            for k in range(HERE):
                xs[k, here] = got[k * CAP : (k + 1) * CAP]

    def work(part, e):
        slot = lax.rem(e, 2)
        for copy in fetch(e):
            copy.wait()

        @pl.loop(0, HALF // TILE)
        def _(r):
            near = pl.ds(pl.multiple_of(r * TILE, TILE), TILE)
            here = pl.ds(pl.multiple_of(part * HALF + r * TILE, TILE), TILE)
            x = xs[e, here]
            g_slot = gs[e, here].astype(F32)
            weight = gcol[e, here][:, :1]
            dy = (weight * (RESIDUAL * g_slot)).astype(BF16)
            gs[e, here] = dy
            a = dot(x, wg[slot])
            b = dot(x, wu[slot])
            sig = jax.nn.sigmoid(a)
            swish = a * sig
            m = (swish * b).astype(BF16)
            ms[e, here] = m
            y = dot(m, wdb[e]).astype(BF16).astype(F32)
            inner = RESIDUAL * jnp.sum(g_slot * y, axis=1, keepdims=True)
            dcol[near] = jnp.broadcast_to(inner, (TILE, LENGTH))
            gys[e, near] = (weight * y).astype(BF16)
            dm = dot(dy, wdb[e], ((1,), (1,)))
            da = (dm * b * sig * (1.0 + a * (1.0 - sig))).astype(BF16)
            db = (dm * swish).astype(BF16)
            das[e, here] = da
            dbs[e, here] = db
            dh_slot = dot(da, wg[slot], ((1,), (1,))) + dot(db, wu[slot], ((1,), (1,)))
            dhs[e, near] = dh_slot.astype(BF16)

        @pl.loop(0, 8)
        def _(member):
            chosen = places == row_of(pos, member, part, e)
            qg[member, pl.ds(part * EXPERTS + first + e, 1), :] = jnp.sum(
                jnp.where(chosen, dcol[slots_of(member)], 0.0), axis=0, keepdims=True
            )

        def refill():
            for copy in fetch(lax.rem(e + 2, HERE)):
                copy.start()

        if part == 0:
            refill()
        else:
            pl.when(e < 2)(refill)

    def combine(source, target, part):
        @pl.loop(0, 8)
        def _(member):
            _, pick = picks(member, part)
            here = slots_of(member)
            stack = jnp.concatenate([source[k, here] for k in range(HERE)])
            target[member, part * LENGTH : (part + 1) * LENGTH] = dot(
                pick, stack, ((0,), (0,))
            ).astype(BF16)

    gather_g(0)
    gather_g(1)
    step(h1)
    step(w3)
    drive(h0)
    gather_h(0)
    drive(w3)
    for copy in shared:
        copy.wait_recv()

    @pl.loop(0, HERE)
    def _(e):
        work(0, e)

    drive(h1, weighed)
    lines.drain()
    gather_h(1)
    sums = [
        group_scatter(lines, me, gb, dh, part * LENGTH, LENGTH, *scratch[8 * part : 8 * part + 8])
        for part in range(2)
    ]
    grad = group_scatter(lines, me, qg, dg, 0, 2 * EXPERTS, *scratch[16:24])
    combine(dhs, gb, 0)
    step(sums[0])
    combine(gys, hb, 0)

    @pl.loop(0, 2)
    def _(e):
        work(1, e)

    step(sums[0])

    @pl.loop(2, HERE)
    def _(e):
        work(1, e)

    combine(dhs, gb, 1)
    step(sums[1], grad)
    step(sums[0])
    combine(gys, hb, 1)
    keep = pltpu.make_async_copy(hb, qy, local_sems.at[4])
    keep.start()
    handed = Lines(hand_send, hand_recv)
    copies = []
    for e in range(HERE):
        for copy in copies:
            copy.wait()
        handed.drain()

        @pl.loop(0, D // 256)
        def _(r, e=e):
            here = pl.ds(pl.multiple_of(r * 256, 256), 256)
            x = xs[e, :, here]
            gg_part[here] = dot(x, das[e], ((0,), (0,))).astype(BF16)
            gu_part[here] = dot(x, dbs[e], ((0,), (0,))).astype(BF16)

        @pl.loop(0, FE // 256)
        def _(r, e=e):
            here = pl.ds(pl.multiple_of(r * 256, 256), 256)
            gd_part[here] = dot(ms[e, :, here], gs[e], ((0,), (0,))).astype(BF16)

        copies = []
        for i, (part, target) in enumerate(((gg_part, gg), (gu_part, gu), (gd_part, gd))):
            size = part.shape[0] // 2
            mine = pl.ds(pl.multiple_of(me.core * size, size), size)
            theirs = pl.ds(pl.multiple_of((1 - me.core) * size, size), size)
            copies.append(pltpu.make_async_copy(part.at[mine], target.at[0, e], local_sems.at[i]))
            copies[i].start()
            handed.send(part.at[theirs], target.at[1, e], me.sibling())
        step(*(sums[:1], [sums[1], grad], [sums[1], grad], [*sums, grad])[e])
    drive(sums[1], grad, sums[0])
    for copy in copies:
        copy.wait()
    handed.drain()
    for copy in handed.copies:
        copy.wait_recv()
    keep.wait()
    lines.drain()


def experts(h2, gates, g, pos, wg, wu, wd):
    rows = 2 * HALF
    shape = jax.ShapeDtypeStruct
    return pl.pallas_call(
        experts_kernel,
        name="experts",
        out_shape=(
            shape(g.shape, BF16),
            shape(h2.shape, F32),
            shape(gates.shape, F32),
            shape((2, HERE, D // 2, FE), BF16),
            shape((2, HERE, D // 2, FE), BF16),
            shape((2, HERE, FE // 2, D), BF16),
        ),
        in_specs=anywhere(3) + vmem(1) + anywhere(3),
        out_specs=anywhere(1) + vmem(2) + anywhere(3),
        scratch_shapes=[
            pltpu.VMEM(g.shape, BF16),
            pltpu.VMEM(g.shape, BF16),
            pltpu.VMEM(pos.shape, F32),
            pltpu.VMEM((HERE, FE, D), BF16),
            pltpu.VMEM((2, D, FE), BF16),
            pltpu.VMEM((2, D, FE), BF16),
            pltpu.VMEM((HERE, rows, D), BF16),
            pltpu.VMEM((HERE, rows, D), BF16),
            pltpu.VMEM((HERE, rows, FE), BF16),
            pltpu.VMEM((HERE, rows, FE), BF16),
            pltpu.VMEM((HERE, rows, FE), BF16),
            pltpu.VMEM((HERE, HALF, D), BF16),
            pltpu.VMEM((HERE, HALF, D), BF16),
            pltpu.VMEM((HERE, rows, LENGTH), F32),
            pltpu.VMEM((HALF, LENGTH), F32),
            pltpu.VMEM(pos.shape, F32),
            pltpu.VMEM((D, FE), BF16),
            pltpu.VMEM((D, FE), BF16),
            pltpu.VMEM((FE, D), BF16),
            pltpu.SemaphoreType.DMA((11,)),
        ]
        + sems(64)
        + sems(12)
        + scatter_scratch(LENGTH, D, BF16)
        + scatter_scratch(LENGTH, D, BF16)
        + scatter_scratch(gates.shape[0], gates.shape[1], F32),
        compiler_params=params(1, 60),
    )(h2, gates, g, pos, wg, wu, wd)


def on_device(
    tokens,
    segments,
    routes,
    cotangent,
    attn_gain,
    moe_gain,
    w_query,
    w_key,
    w_value,
    w_output,
    w_router,
    w_gate,
    w_up,
    w_down,
):
    micro = tokens.shape[0]
    rows = micro * LENGTH
    inputs = tokens.reshape(rows, D)
    upstream = cotangent.reshape(rows, D)
    dense, gbuf, sbuf, wgb, wub, h2, q, k, v, p, o, y1, gates, cos, sin = front(
        inputs,
        segments[:, 0],
        routes.reshape(rows, TOPK),
        w_query,
        w_key,
        w_value,
        w_output,
        w_router,
        jnp.stack([attn_gain, moe_gain]).astype(F32),
        upstream,
        w_gate[0],
        w_up[0],
    )

    qy, dh, gate_grad, gg, gu, gd = experts(
        h2, gates, gbuf, sbuf, wgb, wub, w_down[0]
    )
    grads, got, grad_tokens, result, tg, tu, td = retreat(
        inputs, cos, sin, gates, dense.reshape(D, WIDE), upstream, y1, q, k, v, p, o, dh, gate_grad,
        qy, gg, gu, gd,
    )
    gq, gk, gv, go, gsmall, grad_gate, grad_up, grad_down, grad_tokens, result = finish(
        *settle(grads, got, tg, tu, td), grad_tokens, result
    )
    return (
        result.reshape(micro, 1, LENGTH, D),
        grad_tokens.reshape(micro, 1, LENGTH, D),
        gsmall[:, 32],
        gsmall[:, 33],
        gq,
        gk,
        gv,
        go,
        gsmall[:, :32],
        grad_gate.reshape(1, D, FE),
        grad_up.reshape(1, D, FE),
        grad_down.reshape(1, FE, D),
    )


def solution(mesh):
    sequences = P(None, ("rep", "fsdp"), None, None)
    placed = (
        sequences,
        P(None, ("rep", "fsdp"), None),
        sequences,
        sequences,
        P("fsdp"),
        P("fsdp"),
        P("fsdp", None),
        P("fsdp", None),
        P("fsdp", None),
        P("fsdp", None),
        P("fsdp", None),
        P("fsdp", None, None),
        P("fsdp", None, None),
        P("fsdp", None, None),
    )
    return jax.shard_map(
        on_device,
        mesh=mesh,
        in_specs=placed,
        out_specs=(sequences, sequences) + placed[4:],
        check_vma=False,
    )
```
